32 devices in a mesh: seq: 8 (over y, x, core), tp: 4 (over z).
Axes of the slice: x: 2, y: 2, z: 4, core: 2. Of those that a mesh axis runs over, the one named last changes fastest.
Arguments:
- layer_input: bfloat16 [8192, 2048], P(('seq', 'tp')), may hold values from -6 to 6
- output_grad: bfloat16 [8192, 2048], P(('seq', 'tp')), may hold values from -6 to 6
- segment_ids: int32 [8192], P('seq'), may hold values from 0 to 41, as said below
- positions: int32 [8192], P('seq'), may hold values from 0 to 1999, as said below
- qkv_weight: float32 [2048, 3072], P('seq', 'tp'), may hold values from -0.125 to 0.125
- qkv_moment: float32 [2048, 3072], P('seq', 'tp'), may hold values from -192 to 192
- qkv_square: float32 [2048, 3072], P('seq', 'tp'), may hold values from 65536 to 2097152
- out_weight: float32 [2048, 2048], P('tp', 'seq'), may hold values from -2 to 2
- out_moment: float32 [2048, 2048], P('tp', 'seq'), may hold values from -192 to 192
- out_square: float32 [2048, 2048], P('tp', 'seq'), may hold values from 128 to 4096
- gate_up_weight: float32 [2, 2048, 8192], P(None, 'seq', 'tp'), may hold values from -0.125 to 0.125
- gate_up_moment: float32 [2, 2048, 8192], P(None, 'seq', 'tp'), may hold values from -192 to 192
- gate_up_square: float32 [2, 2048, 8192], P(None, 'seq', 'tp'), may hold values from 128 to 4096
- down_weight: float32 [8192, 2048], P('tp', 'seq'), may hold values from -0.0625 to 0.0625
- down_moment: float32 [8192, 2048], P('tp', 'seq'), may hold values from -192 to 192
- down_square: float32 [8192, 2048], P('tp', 'seq'), may hold values from 128 to 4096
- norm_gains: float32 [2, 2048], replicated, may hold values from 0.5 to 1.5
- gains_moment: float32 [2, 2048], replicated, may hold values from -1024 to 1024
- gains_square: float32 [2, 2048], replicated, may hold values from 4096 to 65536
Outputs:
- outputs: bfloat16 [8192, 2048], P(('seq', 'tp'))
- input_grad: float32 [8192, 2048], P(('seq', 'tp'))
- qkv_grad: float32 [2048, 3072], P('seq', 'tp')
- qkv_master: float32 [2048, 3072], P('seq', 'tp')
- qkv_moment_new: float32 [2048, 3072], P('seq', 'tp')
- qkv_square_new: float32 [2048, 3072], P('seq', 'tp')
- qkv_copy: bfloat16 [2048, 3072], P('seq', 'tp')
- out_grad: float32 [2048, 2048], P('tp', 'seq')
- out_update: float32 [2048, 2048], P('tp', 'seq')
- out_moment_new: float32 [2048, 2048], P('tp', 'seq')
- out_square_new: float32 [2048, 2048], P('tp', 'seq')
- gate_up_grad: float32 [2, 2048, 8192], P(None, 'seq', 'tp')
- gate_up_master: float32 [2, 2048, 8192], P(None, 'seq', 'tp')
- gate_up_moment_new: float32 [2, 2048, 8192], P(None, 'seq', 'tp')
- gate_up_square_new: float32 [2, 2048, 8192], P(None, 'seq', 'tp')
- gate_up_copy: bfloat16 [2, 2048, 8192], P(None, 'seq', 'tp')
- down_grad: float32 [8192, 2048], P('tp', 'seq')
- down_master: float32 [8192, 2048], P('tp', 'seq')
- down_moment_new: float32 [8192, 2048], P('tp', 'seq')
- down_square_new: float32 [8192, 2048], P('tp', 'seq')
- down_copy: bfloat16 [8192, 2048], P('tp', 'seq')
- gains_grad: float32 [2, 2048], replicated
- gains_update: float32 [2, 2048], replicated
- gains_moment_new: float32 [2, 2048], replicated
- gains_square_new: float32 [2, 2048], replicated
The draws below stay inside these ranges and needn't reach their ends.
Inputs may be any that keep to these rules, and one draw needn't show every extreme that they name: `segment_ids`: documents are runs of equal numbers that never fall; each is 1 to 2000 tokens long and lies within one sequence of 4096 tokens; every sequence begins with a document of exactly 2000 tokens. In the k-th sequence the first document has number k * 21 and the last k * 21 + 20. `positions`: each token's position counted from the start of its document.
All inputs are finite; a program needn't handle non-finite values.
Results may differ from the reference program's by a relative error of at most 0.025.
Values may be sent and summed in bfloat16 or wider, within the bound.
No kernel may reach another device: no remote copies, remote signals or barrier semaphores. Data moves between devices by JAX's collectives and lax.ppermute only.
A program may use at most 384 MiB of HBM per device.

```python
import math
import jax
import jax.numpy as jnp
from jax import lax

D = 2048
H = 32
KV = 8
HD = 64
FF = 8192
QPK = 4
SEQLEN = 4096
MINDOC = 200
MAXDOC = 2000
TOKENS = 8192
DOCS = 21


def doc_layout(key):
    seq_count = TOKENS // SEQLEN
    lengths = jax.random.randint(key, (seq_count, DOCS), MINDOC, MAXDOC + 1)
    lengths = jnp.concatenate([jnp.full((seq_count, 1), MAXDOC, jnp.int32), lengths[:, 1:].astype(jnp.int32)], axis=1)
    doc_ends = jnp.cumsum(lengths, axis=1)
    doc_starts = doc_ends - lengths
    token_index = jnp.arange(SEQLEN).astype(jnp.int32)
    local_doc = jnp.sum((doc_ends[:, None, :] <= token_index[None, :, None]).astype(jnp.int32), axis=2)
    token_start = jnp.take_along_axis(doc_starts, local_doc, axis=1)
    position = token_index[None, :] - token_start
    doc_count = local_doc[:, SEQLEN - 1:SEQLEN] + 1
    renumbered = jnp.where(local_doc == 0, 0, DOCS - doc_count + local_doc).astype(jnp.int32)
    segment = renumbered + jnp.arange(seq_count).astype(jnp.int32)[:, None] * DOCS
    return (segment.reshape(TOKENS).astype(jnp.int32), position.reshape(TOKENS).astype(jnp.int32))


def draw_segment_ids(key, part):
    return doc_layout(jax.random.fold_in(key, 11))[0]


def draw_positions(key, part):
    return doc_layout(jax.random.fold_in(key, 11))[1]


def block_levels(own_key, dims, pieces, low, largest):
    level, own = 1.0, jax.random.fold_in(own_key, 6)
    for dim, blocks in pieces:
        steps = jnp.exp(jax.random.uniform(jax.random.fold_in(own, dim), (blocks,), jnp.float32, low / len(pieces), largest / len(pieces)))
        level = level * jnp.repeat(steps, dims[dim] // blocks).reshape([-1 if axis == dim else 1 for axis in range(len(dims))])
    return level


def bell_draw(rng, shape, spread, limit, cuts=(), dtype=jnp.bfloat16):
    values = jax.random.normal(rng, shape, jnp.float32) * spread
    if len(cuts) > 0:
        values = block_levels(rng, shape, cuts, -0.22, 0.18) * values
    return jnp.clip(values, min=-limit, max=limit).astype(dtype)


def setup_inputs(seed: int = 0) -> dict:
    seeds = jax.random.split(jax.random.key(seed), 20)
    layer_input = bell_draw(seeds[0], (TOKENS, D), 1.0, 6.0, ((0, 32),))
    output_grad = bell_draw(seeds[1], (TOKENS, D), 1.0, 6.0, ((0, 32),))
    segment_ids = draw_segment_ids(jax.random.fold_in(seeds[19], 71), 0)
    positions = draw_positions(jax.random.fold_in(seeds[19], 71), 0)
    qkv_weight = bell_draw(seeds[4], (D, KV * (QPK + 2) * HD), D ** -0.5, 0.125, ((0, 8), (1, 4)), jnp.float32)
    qkv_moment = bell_draw(seeds[5], (D, KV * (QPK + 2) * HD), (TOKENS // 256), 192.0, ((0, 8), (1, 4)), jnp.float32)
    qkv_square = jnp.clip(jnp.exp(math.log(2097152) - 3.465736 * jax.random.uniform(seeds[6], (D, KV * (QPK + 2) * HD), jnp.float32) ** block_levels(seeds[6], (D, KV * (QPK + 2) * HD), ((0, 8), (1, 4)), -0.2, 0.2)), 65536.0, 2097152)
    out_weight = bell_draw(seeds[7], (H * HD, D), (H * HD // 256) ** -0.5, 2.0, ((0, 4), (1, 8)), jnp.float32)
    out_moment = bell_draw(seeds[8], (H * HD, D), (TOKENS // 256), 192.0, ((0, 4), (1, 8)), jnp.float32)
    out_square = jnp.clip(jnp.exp(math.log(4096.0) - 3.465736 * jax.random.uniform(seeds[9], (H * HD, D), jnp.float32) ** block_levels(seeds[9], (H * HD, D), ((0, 4), (1, 8)), -0.2, 0.2)), 128.0, 4096.0)
    gate_up_weight = bell_draw(seeds[10], (2, D, FF), D ** -0.5, 0.125, ((1, 8), (2, 4)), jnp.float32)
    gate_up_moment = bell_draw(seeds[11], (2, D, FF), (TOKENS // 256), 192.0, ((1, 8), (2, 4)), jnp.float32)
    gate_up_square = jnp.clip(jnp.exp(math.log(4096.0) - 3.465736 * jax.random.uniform(seeds[12], (2, D, FF), jnp.float32) ** block_levels(seeds[12], (2, D, FF), ((1, 8), (2, 4)), -0.2, 0.2)), 128.0, 4096.0)
    down_weight = bell_draw(seeds[13], (FF, D), FF ** -0.5, 0.0625, ((0, 4), (1, 8)), jnp.float32)
    down_moment = bell_draw(seeds[14], (FF, D), (TOKENS // 256), 192.0, ((0, 4), (1, 8)), jnp.float32)
    down_square = jnp.clip(jnp.exp(math.log(4096.0) - 3.465736 * jax.random.uniform(seeds[15], (FF, D), jnp.float32) ** block_levels(seeds[15], (FF, D), ((0, 4), (1, 8)), -0.2, 0.2)), 128.0, 4096.0)
    norm_gains = jnp.clip(1.0 + 0.1 * jax.random.normal(seeds[16], (2, D), jnp.float32), 0.5, 1.5)
    gains_moment = bell_draw(seeds[17], (2, D), (2 * TOKENS ** 0.5), 1024.0, (), jnp.float32)
    gains_square = jnp.clip(jnp.exp(jax.random.uniform(seeds[18], (2, D), jnp.float32, math.log(4096.0), math.log(65536.0))), 4096.0, 65536.0)
    return dict(layer_input=layer_input, output_grad=output_grad, segment_ids=segment_ids, positions=positions, qkv_weight=qkv_weight, qkv_moment=qkv_moment, qkv_square=qkv_square, out_weight=out_weight, out_moment=out_moment, out_square=out_square, gate_up_weight=gate_up_weight, gate_up_moment=gate_up_moment, gate_up_square=gate_up_square, down_weight=down_weight, down_moment=down_moment, down_square=down_square, norm_gains=norm_gains, gains_moment=gains_moment, gains_square=gains_square)


NORM_EPS = 1e-05
ROPE_BASE = 500000.0
BETA = 0.5
RATE = 0.02
DECAY = 0.1
ADAM_EPS = 1e-08
NEG_FILL = -1e+30
HIGHEST = lax.Precision.HIGHEST

@jax.custom_vjp
def low(v):
    return lax.optimization_barrier(v.astype(jnp.bfloat16)).astype(jnp.float32)

@jax.custom_vjp
def low_back(v):
    return v

def low_keep(v):
    return (low(v), None)

def low_pass(kept, grad):
    return (grad,)

def back_keep(v):
    return (v, None)

def back_low(kept, grad):
    return (low(grad),)
low.defvjp(low_keep, low_pass)
low_back.defvjp(back_keep, back_low)

def matmul(left, right):
    return jnp.dot(left, right, precision=HIGHEST, preferred_element_type=jnp.float32)

def rope_tables(positions):
    half_size = HD // 2
    freq = ROPE_BASE ** (-(jnp.arange(half_size).astype(jnp.float32) * 2.0 / HD))
    angle = positions.astype(jnp.float32)[:, None] * freq[None, :]
    return (jnp.cos(angle), jnp.sin(angle))

def rotate(vector, cos_part, sin_part):
    half_size = vector.shape[-1] // 2
    front_half = vector[..., :half_size]
    back_half = vector[..., half_size:]
    return jnp.concatenate([front_half * cos_part - back_half * sin_part, back_half * cos_part + front_half * sin_part], axis=-1)

def rms_norm(vector, gain):
    inverse = lax.rsqrt(lax.optimization_barrier(jnp.mean(vector * vector, axis=-1, keepdims=True)) + NORM_EPS)
    return vector * inverse * gain

def attend_group(group_item):
    query_blk, key_blk, value_blk, segment_blk = group_item
    scores = low_back(jnp.einsum('sqd,td->qst', query_blk, key_blk, precision=HIGHEST) * HD ** (-0.5))
    token_index = jnp.arange(SEQLEN)
    allowed = (segment_blk[:, None] == segment_blk[None, :]) & (token_index[None, :] <= token_index[:, None])
    scores = jnp.where(allowed[None], scores, NEG_FILL)
    row_max = lax.optimization_barrier(jnp.max(scores, axis=-1, keepdims=True))
    expo = jnp.exp(scores - row_max)
    soft_probs = expo / lax.optimization_barrier(jnp.sum(expo, axis=-1, keepdims=True))
    return jnp.einsum('qst,td->sqd', low(soft_probs), value_blk, precision=HIGHEST)

def layer_forward(resid_in, w_qkv, w_out, w_gate_up, w_down, gains, segment_ids, positions):
    seq_count = TOKENS // SEQLEN
    normed_one = low(rms_norm(resid_in, gains[0]))
    qkv_mixed = low_back(matmul(normed_one, low(w_qkv))).reshape(TOKENS, KV, QPK + 2, HD)
    cos_table, sin_table = rope_tables(positions)
    queries = low(rotate(qkv_mixed[:, :, :QPK], cos_table[:, None, None, :], sin_table[:, None, None, :]))
    key_rows = low(rotate(qkv_mixed[:, :, QPK], cos_table[:, None, :], sin_table[:, None, :]))
    value_rows = low(qkv_mixed[:, :, QPK + 1])
    query_items = queries.reshape(seq_count, SEQLEN, KV, QPK, HD).transpose(0, 2, 1, 3, 4).reshape(seq_count * KV, SEQLEN, QPK, HD)
    key_items = key_rows.reshape(seq_count, SEQLEN, KV, HD).transpose(0, 2, 1, 3).reshape(seq_count * KV, SEQLEN, HD)
    value_items = value_rows.reshape(seq_count, SEQLEN, KV, HD).transpose(0, 2, 1, 3).reshape(seq_count * KV, SEQLEN, HD)
    segment_items = jnp.repeat(segment_ids.reshape(seq_count, SEQLEN), KV, axis=0)
    attn = lax.map(jax.checkpoint(attend_group), (query_items, key_items, value_items, segment_items))
    attn = attn.reshape(seq_count, KV, SEQLEN, QPK, HD).transpose(0, 2, 1, 3, 4).reshape(TOKENS, H * HD)
    attn_in = low(low_back(attn))
    resid_mid = resid_in + low_back(matmul(attn_in, low(w_out)))
    normed_two = low(rms_norm(resid_mid, gains[1]))
    gate_up_low = low(w_gate_up)
    gate_pre = low_back(matmul(normed_two, gate_up_low[0]))
    up_pre = low_back(matmul(normed_two, gate_up_low[1]))
    hidden = low(low_back(gate_pre * jax.nn.sigmoid(gate_pre) * up_pre))
    return resid_mid + low_back(matmul(hidden, low(w_down)))

def adam_step(weight_old, grad_new, moment_one, moment_two):
    moment_next = BETA * moment_one + (1.0 - BETA) * grad_new
    square_next = BETA * moment_two + (1.0 - BETA) * grad_new * grad_new
    change = -RATE * (moment_next / (jnp.sqrt(square_next) + ADAM_EPS) + DECAY * weight_old)
    return (weight_old + change, moment_next, square_next, change)

def reference(layer_input, output_grad, segment_ids, positions, qkv_weight, qkv_moment, qkv_square, out_weight, out_moment, out_square, gate_up_weight, gate_up_moment, gate_up_square, down_weight, down_moment, down_square, norm_gains, gains_moment, gains_square):
    resid_in = layer_input.astype(jnp.float32)

    def forward_fn(resid_arg, w_qkv, w_out, w_gate_up, w_down, gains_arg):
        return layer_forward(resid_arg, w_qkv, w_out, w_gate_up, w_down, gains_arg, segment_ids, positions)
    result, pullback = jax.vjp(forward_fn, resid_in, qkv_weight, out_weight, gate_up_weight, down_weight, norm_gains)
    input_grad, qkv_grad, out_grad, gate_up_grad, down_grad, gains_grad = pullback(output_grad.astype(jnp.float32))
    qkv_new = adam_step(qkv_weight, qkv_grad, qkv_moment, qkv_square)
    out_new = adam_step(out_weight, out_grad, out_moment, out_square)
    gate_up_new = adam_step(gate_up_weight, gate_up_grad, gate_up_moment, gate_up_square)
    down_new = adam_step(down_weight, down_grad, down_moment, down_square)
    gains_new = adam_step(norm_gains, gains_grad, gains_moment, gains_square)
    return (result.astype(jnp.bfloat16), input_grad, qkv_grad, qkv_new[0], qkv_new[1], qkv_new[2], qkv_new[0].astype(jnp.bfloat16), out_grad, out_new[3], out_new[1], out_new[2], gate_up_grad, gate_up_new[0], gate_up_new[1], gate_up_new[2], gate_up_new[0].astype(jnp.bfloat16), down_grad, down_new[0], down_new[1], down_new[2], down_new[0].astype(jnp.bfloat16), gains_grad, gains_new[3], gains_new[1], gains_new[2])
```

```python
import functools

import jax
import jax.numpy as jnp
from jax import lax
from jax.experimental import pallas as pl
from jax.experimental.pallas import tpu as pltpu
from jax.sharding import PartitionSpec as P

HD = 64
QPK = 4
REACH = 2
SEQLEN = 4096

NORM_EPS = 1e-05
ROPE_BASE = 500000.0
BETA = 0.5
RATE = 0.02
DECAY = 0.1
ADAM_EPS = 1e-08
NEG_FILL = -1e30
LOG2E = 1.4426950408889634
EXP_SCALE = HD**-0.5 * LOG2E
VMEM_LIMIT = 48 * 2**20

ROWS_BY_ROWS = (((0,), (0,)), ((), ()))
COLS_BY_COLS = (((1,), (1,)), ((), ()))


def cost(micros):
    return pl.CostEstimate(
        flops=int(micros * 1.15e9), transcendentals=0, bytes_accessed=int(micros * 3.0e6)
    )


def after(block, *others):
    return lax.optimization_barrier((block, *others))[0]


def contract_rows(left, right):
    return lax.dot_general(left, right, ROWS_BY_ROWS, preferred_element_type=jnp.float32)


def contract_cols(left, right):
    return lax.dot_general(left, right, COLS_BY_COLS, preferred_element_type=jnp.float32)


def shifted(block, axis, distance):
    size = lax.axis_size(axis)
    return lax.ppermute(
        block, axis, [(i, i + distance) for i in range(size) if 0 <= i + distance < size]
    )


class LineGather:
    def __init__(self, block, axis):
        self.axis = axis
        self.hops = lax.axis_size(axis) - 1
        self.from_low = [block]
        self.from_high = [block]

    @property
    def step(self):
        return len(self.from_low) - 1

    def hop(self):
        self.from_low.append(shifted(self.from_low[-1], self.axis, 1))
        self.from_high.append(shifted(self.from_high[-1], self.axis, -1))

    @property
    def moving(self):
        return self.from_low[-1], self.from_high[-1]

    @moving.setter
    def moving(self, pair):
        self.from_low[-1], self.from_high[-1] = pair

    @property
    def pieces(self):
        return [*self.from_low, *self.from_high[1:]]


def send_order(size):
    return [sorted(range(size), key=lambda peer: (-abs(peer - me), peer)) for me in range(size)]


def peers_of(axis):
    size = lax.axis_size(axis)
    return jnp.array(send_order(size), jnp.int32)[lax.axis_index(axis)]


class LineScatter:
    def __init__(self, made, axis):
        self.axis = axis
        self.hops = lax.axis_size(axis) - 1
        self.made = list(made)
        self.step = 0
        self.moving = None

    def addend(self, distance):
        order = send_order(self.hops + 1)
        slots = [
            order[me].index(me + distance) if 0 <= me + distance <= self.hops else None
            for me in range(self.hops + 1)
        ]
        choices = sorted(set(slots) - {None})
        table = jnp.array([choices[0] if slot is None else slot for slot in slots], jnp.int32)
        block = self.made[choices[0]]
        for choice in choices[1:]:
            chosen = table[lax.axis_index(self.axis)] == choice
            block = jnp.where(chosen, self.made[choice], block)
        return block

    def hop(self):
        self.step += 1
        size, step = self.hops + 1, self.step
        to_high = self.addend(size - step)
        to_low = self.addend(step - size)
        if step > 1:
            to_high = to_high + self.moving[0]
            to_low = to_low + self.moving[1]
        self.moving = (
            lax.ppermute(to_high, self.axis, [(i, i + 1) for i in range(step)]),
            lax.ppermute(to_low, self.axis, [(i, i - 1) for i in range(size - step, size)]),
        )

    @property
    def parts(self):
        return [self.made[-1], *self.moving]


def swap_gather(block, axis):
    copies = jnp.broadcast_to(block[None], (lax.axis_size(axis), *block.shape))
    return lax.all_to_all(copies, axis, split_axis=0, concat_axis=0, tiled=True)


def swap_scatter_parts(block, axis):
    size = lax.axis_size(axis)
    parts = block.reshape(size, block.shape[0] // size, block.shape[1])
    return lax.all_to_all(parts, axis, split_axis=0, concat_axis=0, tiled=True)


def sum_parts(parts):
    return jnp.sum(parts.astype(jnp.float32), axis=0)


def halving_hop(blocks, axis, hop):
    rank = lax.axis_index(axis)
    pairs = blocks.reshape(blocks.shape[0] // 2, 2, *blocks.shape[1:])
    mine = (rank // hop) % 2
    keep = lax.dynamic_index_in_dim(pairs, mine, axis=1, keepdims=False)
    send = lax.dynamic_index_in_dim(pairs, 1 - mine, axis=1, keepdims=False)
    came = lax.ppermute(send, axis, [(i, i ^ hop) for i in range(lax.axis_size(axis))])
    return (keep.astype(jnp.float32) + came.astype(jnp.float32)).astype(blocks.dtype)


def sum_everywhere(block, axes):
    for axis in axes:
        size = lax.axis_size(axis)
        hop = 1
        while hop < size:
            block = block + lax.ppermute(block, axis, [(i, i ^ hop) for i in range(size)])
            hop *= 2
    return block


def along_sequence(block, distance, tokens):
    shards = SEQLEN // tokens
    route = [
        (i, i + distance)
        for i in range(lax.axis_size("seq"))
        if 0 <= i + distance < lax.axis_size("seq") and i // shards == (i + distance) // shards
    ]
    return lax.ppermute(block, "seq", route)


def turn_halves(block):
    lane = lax.broadcasted_iota(jnp.int32, block.shape, 1)
    return jnp.where(lane % HD < HD // 2, pltpu.roll(block, 96, 1), pltpu.roll(block, 32, 1))


def pick_piece(pieces, below, put):
    size = (len(pieces) + 1) // 2
    for distance in range(1 - size, size):
        piece = pieces[distance if distance >= 0 else size - 1 - distance]
        pl.when(below == distance)(functools.partial(put, piece))


def place_kernel(rank_ref, *refs):
    *pieces, out_ref = refs

    def put(piece):
        out_ref[...] = piece[...]

    pick_piece(pieces, rank_ref[0] - pl.program_id(0), put)


def place_rows(pieces, rank):
    own, width = pieces[0].shape
    size = (len(pieces) + 1) // 2
    return pl.pallas_call(
        place_kernel,
        grid_spec=pltpu.PrefetchScalarGridSpec(
            num_scalar_prefetch=1,
            grid=(size,),
            in_specs=[pl.BlockSpec((own, width), lambda i, r: (0, 0))] * len(pieces),
            out_specs=pl.BlockSpec((own, width), lambda i, r: (i, 0)),
        ),
        out_shape=jax.ShapeDtypeStruct((own * size, width), pieces[0].dtype),
        compiler_params=pltpu.CompilerParams(vmem_limit_bytes=VMEM_LIMIT),
        cost_estimate=cost(4),
        name="place_rows",
    )(jnp.reshape(rank, (1,)).astype(jnp.int32), *pieces)


def qkv_kernel(rank_ref, w_ref, gain_ref, cos_ref, sin_ref, *refs):
    x_ref, normed_ref, q_ref, kv_ref = refs[-4:]

    def put(piece):
        x_ref[...] = piece[...]

    pick_piece(refs[:-4], rank_ref[0] - pl.program_id(0), put)
    x = x_ref[...].astype(jnp.float32)
    inverse = lax.rsqrt(jnp.mean(x * x, axis=1, keepdims=True) + NORM_EPS)
    normed = (x * inverse * gain_ref[...]).astype(jnp.bfloat16)
    normed_ref[...] = normed
    mixed = jnp.dot(normed, w_ref[...], preferred_element_type=jnp.float32)
    cos, sin = cos_ref[...], sin_ref[...]
    key_lane = lax.broadcasted_iota(jnp.int32, cos.shape, 1) < HD
    for group in range(mixed.shape[1] // ((QPK + 2) * HD)):
        base = group * (QPK + 2) * HD
        for pair in range(QPK // 2):
            part = mixed[:, base + pair * 128 : base + (pair + 1) * 128]
            part = part * cos + turn_halves(part) * sin
            q_ref[:, group * QPK * HD + pair * 128 : group * QPK * HD + (pair + 1) * 128] = (
                part.astype(jnp.bfloat16)
            )
        part = mixed[:, base + QPK * HD : base + (QPK + 2) * HD]
        part = jnp.where(key_lane, part * cos + turn_halves(part) * sin, part)
        kv_ref[:, group * 128 : (group + 1) * 128] = part.astype(jnp.bfloat16)


def project_qkv(pieces, rank, weight, gain, cos, sin):
    own, width = pieces[0].shape
    size = (len(pieces) + 1) // 2
    tokens = own * size
    groups = weight.shape[1] // ((QPK + 2) * HD)

    def rows(wide):
        return pl.BlockSpec((own, wide), lambda i, r: (i, 0))

    def whole(shape):
        return pl.BlockSpec(shape, lambda i, r: (0, 0))

    widths = (width, width, groups * QPK * HD, groups * 2 * HD)
    return pl.pallas_call(
        qkv_kernel,
        grid_spec=pltpu.PrefetchScalarGridSpec(
            num_scalar_prefetch=1,
            grid=(size,),
            in_specs=[whole(weight.shape), whole((1, width)), rows(128), rows(128)]
            + [whole((own, width))] * len(pieces),
            out_specs=[rows(wide) for wide in widths],
        ),
        out_shape=[jax.ShapeDtypeStruct((tokens, wide), jnp.bfloat16) for wide in widths],
        compiler_params=pltpu.CompilerParams(vmem_limit_bytes=VMEM_LIMIT),
        cost_estimate=cost(9),
        name="project_qkv",
    )(jnp.reshape(rank, (1,)).astype(jnp.int32), weight, gain[None], cos, sin, *pieces)


def stack_heads(block, low_lanes):
    rows = block.shape[0]
    lane = lax.broadcasted_iota(jnp.int32, (rows, 128), 1)
    keep = (lane < HD) if low_lanes else (lane >= HD)
    stacked = []
    for pair in range(QPK // 2):
        both = block[:, pair * 128 : (pair + 1) * 128].astype(jnp.float32)
        turned = pltpu.roll(both, HD, 1)
        for part in (both, turned) if low_lanes else (turned, both):
            stacked.append(jnp.where(keep, part, 0.0))
    return jnp.concatenate(stacked, axis=0).astype(jnp.bfloat16)


def unstack_heads(stacked, low_lanes):
    rows = stacked.shape[0] // QPK
    lane = lax.broadcasted_iota(jnp.int32, (rows, 128), 1)
    blocks = []
    for pair in range(QPK // 2):
        first = stacked[2 * pair * rows : (2 * pair + 1) * rows]
        second = stacked[(2 * pair + 1) * rows : (2 * pair + 2) * rows]
        if low_lanes:
            second = pltpu.roll(second, HD, 1)
        else:
            first = pltpu.roll(first, HD, 1)
        blocks.append(jnp.where(lane < HD, first, second))
    return blocks


def key_blocks(pos_ref, tile, tq, tk, step, low=0, high=None):
    tokens = pos_ref.shape[0]
    query = tile * tq
    start = REACH * tokens + query
    first = jnp.maximum(start - pos_ref[query], low)
    last_start = start + tq - 1 - pos_ref[query + tq - 1]
    end = (start + tq - 1) // tk + 1
    if high is not None:
        end = jnp.minimum(end, high // tk)

    def body(block, carry):
        key = block * tk
        clear = (key >= last_start) & (key + tk - 1 <= start)

        @pl.when(clear)
        def _():
            step(key, False)

        @pl.when(jnp.logical_not(clear))
        def _():
            step(key, True)

        return carry

    lax.fori_loop(first // tk, end, body, 0)


def allowed_block(key, tile, tokens, tk, tq, back_row):
    key_at = key + lax.broadcasted_iota(jnp.int32, (tk, tq), 0)
    query_at = REACH * tokens + tile * tq + lax.broadcasted_iota(jnp.int32, (tk, tq), 1)
    back = query_at - key_at
    allowed = (back >= 0) & (back <= back_row)
    return jnp.concatenate([allowed] * QPK, axis=1)


def attend_step(key, masked, tile, tk, base, back_ref, kv, vx, qs, acc, top, tokens):
    tq = qs.shape[0] // QPK
    scores = lax.dot_general(
        kv[pl.ds(key - base, tk), :], qs[...], COLS_BY_COLS, preferred_element_type=jnp.float32
    )
    if masked:
        allowed = allowed_block(key, tile, tokens, tk, tq, back_ref[0:1, :])
        scores = jnp.where(allowed, scores, NEG_FILL)
    old = top[0:1, :]
    new = jnp.maximum(old, jnp.max(scores, axis=0, keepdims=True))
    top[0:1, :] = new
    probs = jnp.exp2((scores - new) * EXP_SCALE).astype(jnp.bfloat16)
    fade = jnp.exp2((old - new) * EXP_SCALE)
    acc[...] = acc[...] * fade + lax.dot_general(
        vx[pl.ds(key - base, tk), :], probs, ROWS_BY_ROWS, preferred_element_type=jnp.float32
    )


def load_sources(refs, kv, vx):
    tokens = refs[0].shape[0]
    lane = lax.broadcasted_iota(jnp.int32, (tokens, 2 * HD), 1)
    for i, ref in enumerate(refs):
        kv[pl.ds(i * tokens, tokens), :] = ref[...]
        vx[pl.ds(i * tokens, tokens), :] = jnp.where(lane < HD, jnp.ones_like(ref), ref[...])


def attend_here_kernel(tk, pos_ref, q_ref, back_ref, here, acc_ref, top_ref, vx, qs):
    tokens = here.shape[0]
    tq = q_ref.shape[0]
    tile = pl.program_id(0)
    acc, top = acc_ref.at[0], top_ref.at[0]

    @pl.when(tile == 0)
    def _():
        lane = lax.broadcasted_iota(jnp.int32, (tokens, 2 * HD), 1)
        vx[...] = jnp.where(lane < HD, jnp.ones_like(here), here[...])

    qs[...] = stack_heads(q_ref[...], True)
    acc[...] = jnp.zeros_like(acc)
    top[...] = jnp.full_like(top, NEG_FILL)
    base = REACH * tokens

    def step(key, masked):
        attend_step(key, masked, tile, tk, base, back_ref, here, vx, qs, acc, top, tokens)

    key_blocks(pos_ref, tile, tq, tk, step, low=base)


def attend_far_kernel(
    tk, pos_ref, q_ref, back_ref, far_two, far_one, acc_ref, top_ref,
    out_ref, lse_ref, kv, vx, qs, acc, top
):
    tokens = far_one.shape[0]
    tq = q_ref.shape[0]
    tile = pl.program_id(0)

    @pl.when(tile == 0)
    def _():
        load_sources((far_two, far_one), kv, vx)

    qs[...] = stack_heads(q_ref[...], True)
    acc[...] = acc_ref[0]
    top[...] = top_ref[0]

    def step(key, masked):
        attend_step(key, masked, tile, tk, 0, back_ref, kv, vx, qs, acc, top, tokens)

    key_blocks(pos_ref, tile, tq, tk, step, high=REACH * tokens)
    total = acc[...]
    weight = total[0:1]
    blocks = unstack_heads(jnp.transpose(total / weight), False)
    out_ref[...] = jnp.concatenate(blocks, axis=1).astype(jnp.bfloat16)
    lse = top[0:1, :] * EXP_SCALE + jnp.log2(weight)
    lse_ref[...] = jnp.broadcast_to(lse, (8, lse.shape[1]))[None]


def attend_here(queries, here, positions, back_rows, group, tq, tk):
    tokens = queries.shape[0]
    state = (
        jax.ShapeDtypeStruct((tokens // tq, 2 * HD, QPK * tq), jnp.float32),
        jax.ShapeDtypeStruct((tokens // tq, 8, QPK * tq), jnp.float32),
    )
    return pl.pallas_call(
        functools.partial(attend_here_kernel, tk),
        grid_spec=pltpu.PrefetchScalarGridSpec(
            num_scalar_prefetch=1,
            grid=(tokens // tq,),
            in_specs=[
                pl.BlockSpec((tq, QPK * HD), lambda i, p: (i, group)),
                pl.BlockSpec((8, tq), lambda i, p: (0, i)),
                pl.BlockSpec((tokens, 2 * HD), lambda i, p: (0, group)),
            ],
            out_specs=[pl.BlockSpec((1, *shape.shape[1:]), lambda i, p: (i, 0, 0)) for shape in state],
            scratch_shapes=[
                pltpu.VMEM((tokens, 2 * HD), jnp.bfloat16),
                pltpu.VMEM((QPK * tq, 2 * HD), jnp.bfloat16),
            ],
        ),
        out_shape=state,
        compiler_params=pltpu.CompilerParams(vmem_limit_bytes=VMEM_LIMIT),
        cost_estimate=cost(10),
        name="attend_here",
    )(positions, queries, back_rows, here)


def attend_far(queries, far, state, positions, back_rows, group, tq, tk):
    tokens = queries.shape[0]
    kv_spec = pl.BlockSpec((tokens, 2 * HD), lambda i, p: (0, group))
    return pl.pallas_call(
        functools.partial(attend_far_kernel, tk),
        grid_spec=pltpu.PrefetchScalarGridSpec(
            num_scalar_prefetch=1,
            grid=(tokens // tq,),
            in_specs=[
                pl.BlockSpec((tq, QPK * HD), lambda i, p: (i, group)),
                pl.BlockSpec((8, tq), lambda i, p: (0, i)),
                kv_spec,
                kv_spec,
            ]
            + [pl.BlockSpec((1, *part.shape[1:]), lambda i, p: (i, 0, 0)) for part in state],
            out_specs=[
                pl.BlockSpec((tq, QPK * HD), lambda i, p: (i, 0)),
                pl.BlockSpec((1, 8, QPK * tq), lambda i, p: (i, 0, 0)),
            ],
            scratch_shapes=[
                pltpu.VMEM((REACH * tokens, 2 * HD), jnp.bfloat16),
                pltpu.VMEM((REACH * tokens, 2 * HD), jnp.bfloat16),
                pltpu.VMEM((QPK * tq, 2 * HD), jnp.bfloat16),
                pltpu.VMEM((2 * HD, QPK * tq), jnp.float32),
                pltpu.VMEM((8, QPK * tq), jnp.float32),
            ],
        ),
        out_shape=[
            jax.ShapeDtypeStruct((tokens, QPK * HD), jnp.bfloat16),
            jax.ShapeDtypeStruct((tokens // tq, 8, QPK * tq), jnp.float32),
        ],
        compiler_params=pltpu.CompilerParams(vmem_limit_bytes=VMEM_LIMIT),
        cost_estimate=cost(14),
        name="attend_far",
    )(positions, queries, back_rows, *far, *state)


def attend_back_kernel(
    tk, pos_ref, q_ref, do_ref, o_ref, back_ref, lse_ref, cos_ref, sin_ref, far_two, far_one, here,
    dq_ref, d_far_two, d_far_one, d_here, kv, dkv, qs, dos, dq
):
    tokens = here.shape[0]
    tq = q_ref.shape[0]
    tile = pl.program_id(0)

    @pl.when(tile == 0)
    def _():
        for i, ref in enumerate((far_two, far_one, here)):
            kv[pl.ds(i * tokens, tokens), :] = ref[...]
        dkv[...] = jnp.zeros_like(dkv)

    qs[...] = stack_heads(q_ref[...], True)
    dos[...] = stack_heads(do_ref[...], False)
    dq[...] = jnp.zeros_like(dq)
    product = dos[...].astype(jnp.float32) * stack_heads(o_ref[...], False).astype(jnp.float32)
    delta = jnp.sum(jnp.transpose(product), axis=0, keepdims=True)
    lse = lse_ref[0, 0:1, :]

    def step(key, masked):
        keys = kv[pl.ds(key, tk), :]
        scores = lax.dot_general(keys, qs[...], COLS_BY_COLS, preferred_element_type=jnp.float32)
        probs = jnp.exp2(scores * EXP_SCALE - lse)
        if masked:
            allowed = allowed_block(key, tile, tokens, tk, tq, back_ref[0:1, :])
            probs = jnp.where(allowed, probs, 0.0)
        d_probs = lax.dot_general(keys, dos[...], COLS_BY_COLS, preferred_element_type=jnp.float32)
        d_scores = (probs * (d_probs - delta)).astype(jnp.bfloat16)
        d_keys = jnp.dot(d_scores, qs[...], preferred_element_type=jnp.float32)
        d_values = jnp.dot(probs.astype(jnp.bfloat16), dos[...], preferred_element_type=jnp.float32)
        dkv[pl.ds(key, tk), :] += d_keys * HD**-0.5 + d_values
        dq[...] += lax.dot_general(
            d_scores, keys, ROWS_BY_ROWS, preferred_element_type=jnp.float32
        )

    key_blocks(pos_ref, tile, tq, tk, step)
    cos, sin = cos_ref[...], sin_ref[...]
    blocks = unstack_heads(dq[...] * HD**-0.5, True)
    blocks = [block * cos - turn_halves(block) * sin for block in blocks]
    dq_ref[...] = jnp.concatenate(blocks, axis=1).astype(jnp.bfloat16)

    @pl.when(tile == pl.num_programs(0) - 1)
    def _():
        d_far_two[...] = dkv[pl.ds(0, tokens), :].astype(jnp.bfloat16)
        d_far_one[...] = dkv[pl.ds(tokens, tokens), :].astype(jnp.bfloat16)
        d_here[...] = dkv[pl.ds(2 * tokens, tokens), :]


def attend_back(
    queries, d_attn, attn, lse, sources, positions, back_rows, cos, sin, group, tq, tk
):
    tokens = queries.shape[0]
    kv_spec = pl.BlockSpec((tokens, 2 * HD), lambda i, p: (0, group))
    own_kv = pl.BlockSpec((tokens, 2 * HD), lambda i, p: (0, 0))
    q_spec = pl.BlockSpec((tq, QPK * HD), lambda i, p: (i, group))
    own_q = pl.BlockSpec((tq, QPK * HD), lambda i, p: (i, 0))
    angle_spec = pl.BlockSpec((tq, 128), lambda i, p: (i, 0))
    return pl.pallas_call(
        functools.partial(attend_back_kernel, tk),
        grid_spec=pltpu.PrefetchScalarGridSpec(
            num_scalar_prefetch=1,
            grid=(tokens // tq,),
            in_specs=[
                q_spec,
                q_spec,
                own_q,
                pl.BlockSpec((8, tq), lambda i, p: (0, i)),
                pl.BlockSpec((1, 8, QPK * tq), lambda i, p: (i, 0, 0)),
                angle_spec,
                angle_spec,
                kv_spec,
                kv_spec,
                kv_spec,
            ],
            out_specs=[own_q, own_kv, own_kv, own_kv],
            scratch_shapes=[
                pltpu.VMEM(((REACH + 1) * tokens, 2 * HD), jnp.bfloat16),
                pltpu.VMEM(((REACH + 1) * tokens, 2 * HD), jnp.float32),
                pltpu.VMEM((QPK * tq, 2 * HD), jnp.bfloat16),
                pltpu.VMEM((QPK * tq, 2 * HD), jnp.bfloat16),
                pltpu.VMEM((QPK * tq, 2 * HD), jnp.float32),
            ],
        ),
        out_shape=[
            jax.ShapeDtypeStruct((tokens, QPK * HD), jnp.bfloat16),
            jax.ShapeDtypeStruct((tokens, 2 * HD), jnp.bfloat16),
            jax.ShapeDtypeStruct((tokens, 2 * HD), jnp.bfloat16),
            jax.ShapeDtypeStruct((tokens, 2 * HD), jnp.float32),
        ],
        compiler_params=pltpu.CompilerParams(vmem_limit_bytes=VMEM_LIMIT),
        cost_estimate=cost(28),
        name="attend_back",
    )(positions, queries, d_attn, attn, back_rows, lse, cos, sin, *sources)


def mix_kernel(groups, cos_ref, sin_ref, *refs):
    out_ref = refs[-1]
    cos, sin = cos_ref[...], sin_ref[...]
    key_lane = lax.broadcasted_iota(jnp.int32, cos.shape, 1) < HD
    for group in range(groups):
        dq_ref, here, from_one, from_two = refs[4 * group : 4 * group + 4]
        base = group * (QPK + 2) * HD
        out_ref[:, base : base + QPK * HD] = dq_ref[...]
        total = here[...] + from_one[...].astype(jnp.float32) + from_two[...].astype(jnp.float32)
        turned = total * cos - turn_halves(total) * sin
        out_ref[:, base + QPK * HD : base + (QPK + 2) * HD] = jnp.where(
            key_lane, turned, total
        ).astype(jnp.bfloat16)


def mix_grads(parts, cos, sin, tile):
    tokens = cos.shape[0]
    groups = len(parts)

    def rows(wide):
        return pl.BlockSpec((tile, wide), lambda i: (i, 0))

    flat = [array for part in parts for array in part]
    return pl.pallas_call(
        functools.partial(mix_kernel, groups),
        grid=(tokens // tile,),
        in_specs=[rows(128), rows(128)] + [rows(array.shape[1]) for array in flat],
        out_specs=rows(groups * (QPK + 2) * HD),
        out_shape=jax.ShapeDtypeStruct((tokens, groups * (QPK + 2) * HD), jnp.bfloat16),
        compiler_params=pltpu.CompilerParams(vmem_limit_bytes=VMEM_LIMIT),
        cost_estimate=cost(3),
        name="mix_grads",
    )(cos, sin, *flat)


def out_kernel(rank_ref, x_ref, w_ref, gain_ref, *refs):
    *pieces, mid_ref, normed_ref, own_ref, heads = refs
    size = (len(pieces) + 1) // 2
    columns = pieces[0].shape[1]
    for slot in range(size):

        def put(piece, slot=slot):
            heads[:, slot * columns : (slot + 1) * columns] = piece[...]

        pick_piece(pieces, rank_ref[0] - slot, put)
    mid = x_ref[...].astype(jnp.float32) + jnp.dot(
        heads[...], w_ref[...], preferred_element_type=jnp.float32
    )
    mid_ref[...] = mid
    inverse = lax.rsqrt(jnp.mean(mid * mid, axis=1, keepdims=True) + NORM_EPS)
    normed_ref[...] = (mid * inverse * gain_ref[...]).astype(jnp.bfloat16)

    @pl.when(pl.program_id(0) == rank_ref[0])
    def _():
        own_ref[...] = heads[...]


def project_out(x_rows, pieces, rank, weight, gain, own):
    tokens, width = x_rows.shape
    columns = weight.shape[0]

    def rows(wide):
        return pl.BlockSpec((own, wide), lambda i, r: (i, 0))

    def whole(shape):
        return pl.BlockSpec(shape, lambda i, r: (0, 0))

    return pl.pallas_call(
        out_kernel,
        grid_spec=pltpu.PrefetchScalarGridSpec(
            num_scalar_prefetch=1,
            grid=(tokens // own,),
            in_specs=[rows(width), whole(weight.shape), whole((1, width))]
            + [rows(piece.shape[1]) for piece in pieces],
            out_specs=[rows(width), rows(width), whole((own, columns))],
            scratch_shapes=[pltpu.VMEM((own, columns), jnp.bfloat16)],
        ),
        out_shape=[
            jax.ShapeDtypeStruct((tokens, width), jnp.float32),
            jax.ShapeDtypeStruct((tokens, width), jnp.bfloat16),
            jax.ShapeDtypeStruct((own, columns), jnp.bfloat16),
        ],
        compiler_params=pltpu.CompilerParams(vmem_limit_bytes=VMEM_LIMIT),
        cost_estimate=cost(15),
        name="project_out",
    )(jnp.reshape(rank, (1,)).astype(jnp.int32), x_rows, weight, gain[None], *pieces)


def gate_kernel(n_ref, w_ref, dh_ref, hidden_ref, dgu_ref):
    wide = dh_ref.shape[1]
    both = jnp.dot(n_ref[...], w_ref[...], preferred_element_type=jnp.float32)
    gate, up = both[:, :wide], both[:, wide:]
    sigmoid = jax.nn.sigmoid(gate)
    silu = gate * sigmoid
    d_hidden = dh_ref[...].astype(jnp.float32)
    hidden_ref[...] = (silu * up).astype(jnp.bfloat16)
    d_gate = d_hidden * up * (sigmoid + silu * (1.0 - sigmoid))
    dgu_ref[...] = jnp.concatenate([d_gate, d_hidden * silu], axis=1).astype(jnp.bfloat16)


def gate_and_back(normed, weight, d_hidden, tile, wide):
    tokens, width = normed.shape
    units = d_hidden.shape[1]
    cell = pl.BlockSpec((tile, wide), lambda j, i: (i, j))
    pair_cell = pl.BlockSpec((tile, 2 * wide), lambda j, i: (i, j))
    return pl.pallas_call(
        gate_kernel,
        grid=(units // wide, tokens // tile),
        in_specs=[
            pl.BlockSpec((tile, width), lambda j, i: (i, 0)),
            pl.BlockSpec((width, 2 * wide), lambda j, i: (0, j)),
            cell,
        ],
        out_specs=[cell, pair_cell],
        out_shape=[
            jax.ShapeDtypeStruct((tokens, units), jnp.bfloat16),
            jax.ShapeDtypeStruct((tokens, 2 * units), jnp.bfloat16),
        ],
        compiler_params=pltpu.CompilerParams(vmem_limit_bytes=VMEM_LIMIT),
        cost_estimate=cost(27),
        name="gate_and_back",
    )(normed, weight, d_hidden)


def blocks_kernel(chunks_ref, *refs):
    count = (len(refs) - 1) // 2
    left = jnp.concatenate([ref[...] for ref in refs[:count]], axis=0)
    product = lax.dot_general(
        left, refs[count][...], COLS_BY_COLS, preferred_element_type=jnp.float32
    ).astype(jnp.bfloat16)
    rows = refs[0].shape[0]
    for i, out_ref in enumerate(refs[count + 1 :]):
        out_ref[...] = product[i * rows : (i + 1) * rows]


def blocks_times(left, right, chunks, rows, wide, micros):
    depth = left.shape[1]
    count = chunks.shape[0]

    def block_spec(i):
        return pl.BlockSpec((rows, depth), lambda j, c: (c[i], 0))

    return pl.pallas_call(
        blocks_kernel,
        grid_spec=pltpu.PrefetchScalarGridSpec(
            num_scalar_prefetch=1,
            grid=(right.shape[0] // wide,),
            in_specs=[block_spec(i) for i in range(count)]
            + [pl.BlockSpec((wide, depth), lambda j, c: (j, 0))],
            out_specs=[pl.BlockSpec((rows, wide), lambda j, c: (0, j))] * count,
        ),
        out_shape=[jax.ShapeDtypeStruct((rows, right.shape[0]), jnp.bfloat16)] * count,
        compiler_params=pltpu.CompilerParams(vmem_limit_bytes=VMEM_LIMIT),
        cost_estimate=cost(micros),
        name="blocks_times",
    )(chunks, *[left] * count, right)


def gain_kernel(part_ref, w_ref, out_ref):
    product = part_ref[...].astype(jnp.float32) * w_ref[...].astype(jnp.float32)
    ones = jnp.ones((8, product.shape[1]), jnp.float32)
    out_ref[...] = lax.dot_general(
        ones, product, COLS_BY_COLS, precision=lax.Precision.HIGHEST,
        preferred_element_type=jnp.float32,
    )


def row_products(part, weight, tile):
    rows, columns = part.shape
    cell = pl.BlockSpec((tile, columns), lambda i: (i, 0))
    sums = pl.pallas_call(
        gain_kernel,
        grid=(rows // tile,),
        in_specs=[cell, cell],
        out_specs=pl.BlockSpec((8, tile), lambda i: (0, i)),
        out_shape=jax.ShapeDtypeStruct((8, rows), jnp.float32),
        compiler_params=pltpu.CompilerParams(vmem_limit_bytes=VMEM_LIMIT),
        cost_estimate=cost(4),
        name="row_products",
    )(part, weight)
    return sums[0]


def norm_back_rows(vector, grad_in, gain):
    inverse = lax.rsqrt(jnp.mean(vector * vector, axis=1, keepdims=True) + NORM_EPS)
    scaled = grad_in * gain
    mean = jnp.mean(vector * scaled, axis=1, keepdims=True)
    grad = inverse * scaled - vector * (inverse * inverse * inverse * mean)
    return grad, jnp.sum(grad_in * vector * inverse, axis=0, keepdims=True)


def sum_refs(refs):
    total = refs[0][...].astype(jnp.float32)
    for ref in refs[1:]:
        total = total + ref[...].astype(jnp.float32)
    return total


def mid_kernel(rank_ref, mid_ref, dy_ref, gain_ref, *refs):
    *parts, d_mid_ref, branch_ref, mid_out, gain_grad_ref = refs
    mid = mid_ref[...]
    grad, gain_grad = norm_back_rows(mid, sum_refs(parts), gain_ref[...])
    d_mid = dy_ref[...].astype(jnp.float32) + grad
    d_mid_ref[...] = d_mid
    branch_ref[...] = d_mid.astype(jnp.bfloat16)
    mid_out[...] = mid
    gain_grad = jnp.broadcast_to(gain_grad, gain_grad_ref.shape)

    @pl.when(pl.program_id(0) == 0)
    def _():
        gain_grad_ref[...] = gain_grad

    @pl.when(pl.program_id(0) > 0)
    def _():
        gain_grad_ref[...] += gain_grad


def back_to_mid(parts, mid_rows, rank, output_grad, gain):
    own, width = output_grad.shape
    tile = min(64, own)
    tiles = own // tile

    def rows(index):
        return pl.BlockSpec((tile, width), index)

    own_rows = rows(lambda i, r: (i, 0))
    outs = pl.pallas_call(
        mid_kernel,
        grid_spec=pltpu.PrefetchScalarGridSpec(
            num_scalar_prefetch=1,
            grid=(tiles,),
            in_specs=[
                rows(lambda i, r: (r[0] * tiles + i, 0)),
                own_rows,
                pl.BlockSpec((1, width), lambda i, r: (0, 0)),
            ]
            + [own_rows] * len(parts),
            out_specs=[own_rows, own_rows, own_rows, pl.BlockSpec((8, width), lambda i, r: (0, 0))],
        ),
        out_shape=[
            jax.ShapeDtypeStruct((own, width), jnp.float32),
            jax.ShapeDtypeStruct((own, width), jnp.bfloat16),
            jax.ShapeDtypeStruct((own, width), jnp.float32),
            jax.ShapeDtypeStruct((8, width), jnp.float32),
        ],
        compiler_params=pltpu.CompilerParams(vmem_limit_bytes=VMEM_LIMIT),
        cost_estimate=cost(4),
        name="back_to_mid",
    )(jnp.reshape(rank, (1,)).astype(jnp.int32), mid_rows, output_grad, gain[None], *parts)
    return outs[0], outs[1], outs[2], outs[3][0]


def input_kernel(x_ref, d_mid_ref, gain_ref, *refs):
    *parts, out_ref = refs
    x = x_ref[...].astype(jnp.float32)
    grad, _ = norm_back_rows(x, sum_refs(parts), gain_ref[...])
    out_ref[...] = d_mid_ref[...] + grad


def back_to_input(parts, layer_input, d_mid, gain):
    own, width = layer_input.shape
    tile = min(64, own)
    rows = pl.BlockSpec((tile, width), lambda i: (i, 0))
    return pl.pallas_call(
        input_kernel,
        grid=(own // tile,),
        in_specs=[rows, rows, pl.BlockSpec((1, width), lambda i: (0, 0))] + [rows] * len(parts),
        out_specs=rows,
        out_shape=jax.ShapeDtypeStruct((own, width), jnp.float32),
        compiler_params=pltpu.CompilerParams(vmem_limit_bytes=VMEM_LIMIT),
        cost_estimate=cost(4),
        name="back_to_input",
    )(layer_input, d_mid, gain[None], *parts)


def round_kernel(w_ref, out_ref):
    out_ref[...] = w_ref[0].astype(jnp.bfloat16)


def round_interleaved(weight, wide):
    _, rows, units = weight.shape
    return pl.pallas_call(
        round_kernel,
        grid=(units // wide, 2),
        in_specs=[pl.BlockSpec((1, rows, wide), lambda j, k: (k, 0, j))],
        out_specs=pl.BlockSpec((rows, wide), lambda j, k: (0, 2 * j + k)),
        out_shape=jax.ShapeDtypeStruct((rows, 2 * units), jnp.bfloat16),
        cost_estimate=cost(6),
        name="round_interleaved",
    )(weight)


def adam_kernel(g_ref, w_ref, m_ref, s_ref, grad_ref, w_out, m_out, s_out, copy_out):
    grad = g_ref[...].astype(jnp.float32)
    new, moment, square, _ = adam_step(w_ref[0], grad, m_ref[0], s_ref[0])
    grad_ref[0] = grad
    w_out[0] = new
    m_out[0] = moment
    s_out[0] = square
    copy_out[0] = new.astype(jnp.bfloat16)


def adam_interleaved(grad, weight, moment, square, wide):
    _, rows, units = weight.shape
    cell = pl.BlockSpec((1, rows, wide), lambda j, k: (k, 0, j))
    shape = jax.ShapeDtypeStruct(weight.shape, jnp.float32)
    return pl.pallas_call(
        adam_kernel,
        grid=(units // wide, 2),
        in_specs=[pl.BlockSpec((rows, wide), lambda j, k: (0, 2 * j + k)), cell, cell, cell],
        out_specs=[cell] * 5,
        out_shape=[shape] * 4 + [jax.ShapeDtypeStruct(weight.shape, jnp.bfloat16)],
        compiler_params=pltpu.CompilerParams(vmem_limit_bytes=VMEM_LIMIT),
        cost_estimate=cost(13),
        name="adam_interleaved",
    )(grad, weight, moment, square)


def angle_tables(positions):
    half_size = HD // 2
    freq = ROPE_BASE ** (-(jnp.arange(half_size).astype(jnp.float32) * 2.0 / HD))
    angle = positions.astype(jnp.float32)[:, None] * freq[None, :]
    cos, sin = jnp.cos(angle), jnp.sin(angle)
    return jnp.concatenate([cos] * 4, axis=1), jnp.concatenate([-sin, sin] * 2, axis=1)


def adam_step(weight_old, grad_new, moment_one, moment_two):
    moment_next = BETA * moment_one + (1.0 - BETA) * grad_new
    square_next = BETA * moment_two + (1.0 - BETA) * grad_new * grad_new
    change = -RATE * (moment_next / (jnp.sqrt(square_next) + ADAM_EPS) + DECAY * weight_old)
    return (weight_old + change, moment_next, square_next, change)


def local(
    layer_input,
    output_grad,
    segment_ids,
    positions,
    qkv_weight,
    qkv_moment,
    qkv_square,
    out_weight,
    out_moment,
    out_square,
    gate_up_weight,
    gate_up_moment,
    gate_up_square,
    down_weight,
    down_moment,
    down_square,
    norm_gains,
    gains_moment,
    gains_square,
):
    low = low_type = jnp.bfloat16
    full = jnp.float32
    own, width = layer_input.shape
    tokens = positions.shape[0]
    rank = lax.axis_index("tp")
    units = down_weight.shape[0]
    groups = qkv_weight.shape[1] // ((QPK + 2) * HD)
    head_columns = groups * QPK * HD
    tile = min(256, own)
    gain_one = norm_gains[0]
    gain_two = norm_gains[1]

    wide = min(512, units)

    close = lax.optimization_barrier

    low_qkv = qkv_weight.astype(low)
    low_down = down_weight.astype(low)
    w_qkv = lax.all_gather(low_qkv, "seq", axis=0, tiled=True)
    w_down = lax.all_gather(low_down, "seq", axis=1, tiled=True)
    low_gate_up = round_interleaved(gate_up_weight, wide)
    low_out = out_weight.astype(low)
    cos, sin = angle_tables(positions)
    back_rows = jnp.broadcast_to(positions[None, :], (8, tokens))
    side = (low_gate_up, low_out, cos, sin, back_rows)
    x_line = LineGather(layer_input, "tp")
    for _ in range(x_line.hops):
        x_line.hop()
        x_line.moving, side = close((x_line.moving, side))
    pieces, side, w_qkv, output_grad = close((x_line.pieces, side, w_qkv, output_grad))
    low_gate_up, low_out, cos, sin, back_rows = side

    dy_line = LineGather(output_grad, "tp")
    dy_line.hop()
    made = project_qkv(pieces, rank, w_qkv, gain_one, cos, sin)
    made, dy_line.moving, w_down, low_out = close((made, dy_line.moving, w_down, low_out))
    x_rows, normed_one, queries, kv = made
    out_strip = lax.all_gather(low_out, "tp", axis=0, tiled=True)
    far = [along_sequence(kv, distance, tokens) for distance in (2, 1)]
    if dy_line.hops > 1:
        dy_line.hop()
    states = [
        attend_here(queries, kv, positions, back_rows, group, 256, 512) for group in range(groups)
    ]
    far, states, out_strip, queries, low_gate_up, dy_line.moving = close(
        (far, states, out_strip, queries, low_gate_up, dy_line.moving)
    )
    w_out = lax.all_gather(out_strip, "seq", axis=1, tiled=True)
    w_gate_up = lax.all_gather(low_gate_up, "seq", axis=0, tiled=True)
    for _ in range(2, dy_line.hops):
        dy_line.hop()
    attn, lse = [], []
    for group in range(groups):
        out, log_total = attend_far(
            queries, far, states[group], positions, back_rows, group, 256, 512
        )
        attn.append(out)
        lse.append(log_total)
    attn, lse, dy_pieces, w_down, x_rows = close((attn, lse, dy_line.pieces, w_down, x_rows))

    heads_line = LineGather(jnp.concatenate(attn, axis=1), "tp")
    for index in range(heads_line.hops):
        heads_line.hop()
        if index == 0:
            grad_rows = place_rows(dy_pieces, rank)
            d_hidden = contract_cols(grad_rows, w_down).astype(low)
            side = (grad_rows, d_hidden, x_rows)
            heads_line.moving, side, w_out = close((heads_line.moving, side, w_out))
        else:
            heads_line.moving, side = close((heads_line.moving, side))
    grad_rows, d_hidden, x_rows = side

    mid_rows, normed_two, own_heads = project_out(
        x_rows, heads_line.pieces, rank, w_out, gain_two, own
    )
    mid_rows, normed_two, own_heads, w_gate_up, d_hidden = close(
        (mid_rows, normed_two, own_heads, w_gate_up, d_hidden)
    )
    hidden, d_gate_up = close(gate_and_back(normed_two, w_gate_up, d_hidden, 512, wide))
    peers = peers_of("tp")
    half = peers.shape[0] // 2
    first = blocks_times(d_gate_up, w_gate_up, peers[:half], own, 256, 15)
    first, side = close((first, (hidden, d_gate_up, normed_two, grad_rows)))
    back_line = LineScatter(first, "tp")
    for index in range(back_line.hops):
        back_line.hop()
        hidden, d_gate_up, normed_two, grad_rows = side
        if index == 0:
            second = blocks_times(d_gate_up, w_gate_up, peers[half:], own, 256, 15)
            down_grad = contract_rows(hidden, grad_rows).astype(low)
            back_line.moving, side, second, down_grad = close(
                (back_line.moving, side, second, down_grad)
            )
            back_line.made += second
            down_grad = lax.psum_scatter(down_grad, "seq", scatter_dimension=1, tiled=True)
        elif index == 1:
            gate_up_grad = contract_rows(normed_two, d_gate_up).astype(low)
            back_line.moving, side, gate_up_grad = close((back_line.moving, side, gate_up_grad))
            gate_up_grad = lax.psum_scatter(gate_up_grad, "seq", scatter_dimension=0, tiled=True)
        elif index == 2:
            partial_out = jnp.dot(hidden, w_down, preferred_element_type=full).astype(low)
            back_line.moving, side, partial_out = close((back_line.moving, side, partial_out))
        else:
            back_line.moving, side = close((back_line.moving, side))
    d_mid, d_branch, mid, gain_two_grad = back_to_mid(
        back_line.parts, mid_rows, rank, output_grad, gain_two
    )

    d_attn = contract_cols(d_branch, w_out).astype(low)
    d_attn, d_branch, d_mid, mid, gain_two_grad, own_heads, partial_out = close(
        (d_attn, d_branch, d_mid, mid, gain_two_grad, own_heads, partial_out)
    )
    d_attn = lax.all_to_all(d_attn, "tp", split_axis=1, concat_axis=0, tiled=True)
    out_grad = contract_rows(own_heads, d_branch).astype(low)
    d_attn, out_grad, partial_out, down_grad = close((d_attn, out_grad, partial_out, down_grad))
    out_grad = lax.psum_scatter(out_grad, "seq", scatter_dimension=1, tiled=True)
    made = [
        lax.dynamic_slice_in_dim(partial_out, peers[i] * own, own, axis=0)
        for i in range(peers.shape[0])
    ]
    out_line = LineScatter(made, "tp")
    grads = []
    travelled = []
    for group in range(groups):
        out_line.hop()
        made = attend_back(
            queries, d_attn, attn[group], lse[group], [*far, kv], positions, back_rows,
            cos, sin, group, 256, 512,
        )
        made, d_attn, travelled, out_line.moving = close(
            (made, d_attn, travelled, out_line.moving)
        )
        grads.append(made)
        travelled.append(
            [along_sequence(made[2], -1, tokens), along_sequence(made[1], -2, tokens)]
        )
    down_new = adam_step(down_weight, down_grad.astype(full), down_moment, down_square)
    while out_line.step < out_line.hops:
        out_line.hop()
        down_new, grads, travelled, down_grad, out_line.moving = close(
            (down_new, grads, travelled, down_grad, out_line.moving)
        )
    d_mixed = mix_grads(
        [(made[0], made[3], *moved) for made, moved in zip(grads, travelled, strict=True)],
        cos, sin, tile,
    )
    made = blocks_times(d_mixed, w_qkv, peers, own, 512, 7)
    made, d_mixed, gate_up_grad = close((made, d_mixed, gate_up_grad))
    in_line = LineScatter(made, "tp")
    bits = [1 << bit for bit in range(lax.axis_size("seq").bit_length() - 1)]
    for index in range(in_line.hops):
        in_line.hop()
        if index == 0:
            qkv_grad = contract_rows(normed_one, d_mixed).astype(low)
            gain_one_grad = row_products(qkv_grad, w_qkv, min(512, width)) / gain_one
            qkv_grad = qkv_grad.reshape(lax.axis_size("seq"), -1, qkv_grad.shape[1])
            in_line.moving, qkv_grad, gain_one_grad = close(
                (in_line.moving, qkv_grad, gain_one_grad)
            )
        elif index == 1:
            gate_up_new = adam_interleaved(
                gate_up_grad, gate_up_weight, gate_up_moment, gate_up_square, wide
            )
            for hop in bits[:2]:
                qkv_grad = halving_hop(qkv_grad, "seq", hop)
            gains_grad = sum_everywhere(jnp.stack([gain_one_grad, gain_two_grad]), ("seq",))
            in_line.moving, gate_up_new, gains_grad, qkv_grad = close(
                (in_line.moving, gate_up_new, gains_grad, qkv_grad)
            )
            for hop in bits[2:]:
                qkv_grad = halving_hop(qkv_grad, "seq", hop)
            qkv_grad = qkv_grad[0]
            gains_grad = sum_everywhere(gains_grad, ("tp",))
            outputs = (mid + sum(part.astype(full) for part in out_line.parts)).astype(low)
        elif index == in_line.hops - 1:
            in_line.moving, gains_grad, qkv_grad, outputs, out_grad = close(
                (in_line.moving, gains_grad, qkv_grad, outputs, out_grad)
            )
        else:
            in_line.moving = close(in_line.moving)
    out_parts = swap_scatter_parts(out_grad, "tp")
    input_grad = back_to_input(in_line.parts, layer_input, d_mid, gain_one)
    out_grad = sum_parts(out_parts)
    out_new = adam_step(out_weight, out_grad, out_moment, out_square)

    qkv_grad = qkv_grad.astype(full)
    out_grad = out_grad.astype(full)
    down_grad = down_grad.astype(full)
    qkv_new = adam_step(qkv_weight, qkv_grad, qkv_moment, qkv_square)
    gains_new = adam_step(norm_gains, gains_grad, gains_moment, gains_square)
    return (
        outputs,
        input_grad,
        qkv_grad,
        qkv_new[0],
        qkv_new[1],
        qkv_new[2],
        qkv_new[0].astype(low),
        out_grad,
        out_new[3],
        out_new[1],
        out_new[2],
        *gate_up_new,
        down_grad,
        down_new[0],
        down_new[1],
        down_new[2],
        down_new[0].astype(low),
        gains_grad,
        gains_new[3],
        gains_new[1],
        gains_new[2],
    )


def solution(mesh):
    tokens = P(("seq", "tp"), None)
    rows = P("seq", "tp")
    columns = P("tp", "seq")
    pair = P(None, "seq", "tp")
    return jax.shard_map(
        local,
        mesh=mesh,
        in_specs=(
            (tokens,) * 2 + (P("seq"),) * 2 + (rows,) * 3 + (columns,) * 3 + (pair,) * 3
            + (columns,) * 3 + (P(),) * 3
        ),
        out_specs=(
            (tokens,) * 2 + (rows,) * 5 + (columns,) * 4 + (pair,) * 5 + (columns,) * 5 + (P(),) * 4
        ),
        check_vma=False,
    )
```

```python
import functools

import jax
import jax.numpy as jnp
from jax import lax
from jax.experimental import pallas as pl
from jax.experimental.pallas import tpu as pltpu
from jax.sharding import PartitionSpec as P

HD = 64
QPK = 4
REACH = 2
SEQLEN = 4096

NORM_EPS = 1e-05
ROPE_BASE = 500000.0
BETA = 0.5
RATE = 0.02
DECAY = 0.1
ADAM_EPS = 1e-08
NEG_FILL = -1e30
LOG2E = 1.4426950408889634
EXP_SCALE = HD**-0.5 * LOG2E
VMEM_LIMIT = 48 * 2**20

ROWS_BY_ROWS = (((0,), (0,)), ((), ()))
COLS_BY_COLS = (((1,), (1,)), ((), ()))


def cost(micros):
    return pl.CostEstimate(
        flops=int(micros * 1.15e9), transcendentals=0, bytes_accessed=int(micros * 3.0e6)
    )


def after(block, *others):
    return lax.optimization_barrier((block, *others))[0]


def contract_rows(left, right):
    return lax.dot_general(left, right, ROWS_BY_ROWS, preferred_element_type=jnp.float32)


def contract_cols(left, right):
    return lax.dot_general(left, right, COLS_BY_COLS, preferred_element_type=jnp.float32)


class LineGather:
    def __init__(self, block, axis):
        self.axis = axis
        self.hops = lax.axis_size(axis) - 1
        self.from_low = [block]
        self.from_high = [block]

    @property
    def step(self):
        return len(self.from_low) - 1

    def hop(self):
        size, passed = self.hops + 1, self.step
        up = [(i, i + 1) for i in range(passed, size - 1)]
        down = [(i, i - 1) for i in range(1, size - passed)]
        self.from_low.append(lax.ppermute(self.from_low[-1], self.axis, up))
        self.from_high.append(lax.ppermute(self.from_high[-1], self.axis, down))

    @property
    def moving(self):
        return self.from_low[-1], self.from_high[-1]

    @moving.setter
    def moving(self, pair):
        self.from_low[-1], self.from_high[-1] = pair

    @property
    def pieces(self):
        return [*self.from_low, *self.from_high[1:]]


def send_order(size):
    return [sorted(range(size), key=lambda peer: (-abs(peer - me), peer)) for me in range(size)]


def peers_of(axis):
    size = lax.axis_size(axis)
    return jnp.array(send_order(size), jnp.int32)[lax.axis_index(axis)]


class LineScatter:
    def __init__(self, made, axis):
        self.axis = axis
        self.hops = lax.axis_size(axis) - 1
        self.made = list(made)
        self.step = 0
        self.moving = None

    def addend(self, distance):
        order = send_order(self.hops + 1)
        slots = [
            order[me].index(me + distance) if 0 <= me + distance <= self.hops else None
            for me in range(self.hops + 1)
        ]
        choices = sorted(set(slots) - {None})
        table = jnp.array([choices[0] if slot is None else slot for slot in slots], jnp.int32)
        block = self.made[choices[0]]
        for choice in choices[1:]:
            chosen = table[lax.axis_index(self.axis)] == choice
            block = jnp.where(chosen, self.made[choice], block)
        return block

    def hop(self):
        self.step += 1
        size, step = self.hops + 1, self.step
        to_high = self.addend(size - step)
        to_low = self.addend(step - size)
        if step > 1:
            to_high = to_high + self.moving[0]
            to_low = to_low + self.moving[1]
        self.moving = (
            lax.ppermute(to_high, self.axis, [(i, i + 1) for i in range(step)]),
            lax.ppermute(to_low, self.axis, [(i, i - 1) for i in range(size - step, size)]),
        )

    @property
    def parts(self):
        return [self.made[-1], *self.moving]


def swap_gather(block, axis):
    copies = jnp.broadcast_to(block[None], (lax.axis_size(axis), *block.shape))
    return lax.all_to_all(copies, axis, split_axis=0, concat_axis=0, tiled=True)


def swap_scatter_parts(block, axis):
    size = lax.axis_size(axis)
    parts = block.reshape(size, block.shape[0] // size, block.shape[1])
    return lax.all_to_all(parts, axis, split_axis=0, concat_axis=0, tiled=True)


def sum_parts(parts):
    return jnp.sum(parts.astype(jnp.float32), axis=0)


def sum_by_swaps(block, axis):
    size = lax.axis_size(axis)
    hop = 1
    while hop < size:
        block = block + lax.ppermute(block, axis, [(i, i ^ hop) for i in range(size)])
        hop *= 2
    return block


def sum_at_once(block, axis):
    size = lax.axis_size(axis)
    came = [block]
    for distance in range(1, size):
        route = [(i, (i + distance) % size) for i in range(size)]
        came.append(lax.ppermute(block, axis, route))
    came = jnp.stack(came)
    rank = lax.axis_index(axis)
    total = lax.dynamic_index_in_dim(came, rank, keepdims=False)
    for peer in range(1, size):
        total = total + lax.dynamic_index_in_dim(came, (rank - peer) % size, keepdims=False)
    return total


def along_sequence(block, distance, tokens):
    shards = SEQLEN // tokens
    route = [
        (i, i + distance)
        for i in range(lax.axis_size("seq"))
        if 0 <= i + distance < lax.axis_size("seq") and i // shards == (i + distance) // shards
    ]
    return lax.ppermute(block, "seq", route)


def turn_halves(block):
    lane = lax.broadcasted_iota(jnp.int32, block.shape, 1)
    return jnp.where(lane % HD < HD // 2, pltpu.roll(block, 96, 1), pltpu.roll(block, 32, 1))


def pick_piece(pieces, below, put):
    size = (len(pieces) + 1) // 2
    for distance in range(1 - size, size):
        piece = pieces[distance if distance >= 0 else size - 1 - distance]
        pl.when(below == distance)(functools.partial(put, piece))


def place_kernel(rank_ref, *refs):
    *pieces, out_ref = refs

    def put(piece):
        out_ref[...] = piece[...]

    pick_piece(pieces, rank_ref[0] - pl.program_id(0), put)


def place_rows(pieces, rank):
    own, width = pieces[0].shape
    size = (len(pieces) + 1) // 2
    return pl.pallas_call(
        place_kernel,
        grid_spec=pltpu.PrefetchScalarGridSpec(
            num_scalar_prefetch=1,
            grid=(size,),
            in_specs=[pl.BlockSpec((own, width), lambda i, r: (0, 0))] * len(pieces),
            out_specs=pl.BlockSpec((own, width), lambda i, r: (i, 0)),
        ),
        out_shape=jax.ShapeDtypeStruct((own * size, width), pieces[0].dtype),
        compiler_params=pltpu.CompilerParams(vmem_limit_bytes=VMEM_LIMIT),
        cost_estimate=cost(4),
        name="place_rows",
    )(jnp.reshape(rank, (1,)).astype(jnp.int32), *pieces)


def qkv_kernel(rank_ref, w_ref, gain_ref, cos_ref, sin_ref, *refs):
    x_ref, normed_ref, q_ref, kv_ref = refs[-4:]

    def put(piece):
        x_ref[...] = piece[...]

    pick_piece(refs[:-4], rank_ref[0] - pl.program_id(0), put)
    x = x_ref[...].astype(jnp.float32)
    inverse = lax.rsqrt(jnp.mean(x * x, axis=1, keepdims=True) + NORM_EPS)
    normed = (x * inverse * gain_ref[...]).astype(jnp.bfloat16)
    normed_ref[...] = normed
    mixed = jnp.dot(normed, w_ref[...], preferred_element_type=jnp.float32)
    cos, sin = cos_ref[...], sin_ref[...]
    key_lane = lax.broadcasted_iota(jnp.int32, cos.shape, 1) < HD
    for group in range(mixed.shape[1] // ((QPK + 2) * HD)):
        base = group * (QPK + 2) * HD
        for pair in range(QPK // 2):
            part = mixed[:, base + pair * 128 : base + (pair + 1) * 128]
            part = part * cos + turn_halves(part) * sin
            q_ref[:, group * QPK * HD + pair * 128 : group * QPK * HD + (pair + 1) * 128] = (
                part.astype(jnp.bfloat16)
            )
        part = mixed[:, base + QPK * HD : base + (QPK + 2) * HD]
        part = jnp.where(key_lane, part * cos + turn_halves(part) * sin, part)
        kv_ref[:, group * 128 : (group + 1) * 128] = part.astype(jnp.bfloat16)


def project_qkv(pieces, rank, weight, gain, cos, sin):
    own, width = pieces[0].shape
    size = (len(pieces) + 1) // 2
    tokens = own * size
    groups = weight.shape[1] // ((QPK + 2) * HD)

    def rows(wide):
        return pl.BlockSpec((own, wide), lambda i, r: (i, 0))

    def whole(shape):
        return pl.BlockSpec(shape, lambda i, r: (0, 0))

    widths = (width, width, groups * QPK * HD, groups * 2 * HD)
    return pl.pallas_call(
        qkv_kernel,
        grid_spec=pltpu.PrefetchScalarGridSpec(
            num_scalar_prefetch=1,
            grid=(size,),
            in_specs=[whole(weight.shape), whole((1, width)), rows(128), rows(128)]
            + [whole((own, width))] * len(pieces),
            out_specs=[rows(wide) for wide in widths],
        ),
        out_shape=[jax.ShapeDtypeStruct((tokens, wide), jnp.bfloat16) for wide in widths],
        compiler_params=pltpu.CompilerParams(vmem_limit_bytes=VMEM_LIMIT),
        cost_estimate=cost(9),
        name="project_qkv",
    )(jnp.reshape(rank, (1,)).astype(jnp.int32), weight, gain[None], cos, sin, *pieces)


def stack_heads(block, low_lanes):
    rows = block.shape[0]
    lane = lax.broadcasted_iota(jnp.int32, (rows, 128), 1)
    keep = (lane < HD) if low_lanes else (lane >= HD)
    stacked = []
    for pair in range(QPK // 2):
        both = block[:, pair * 128 : (pair + 1) * 128].astype(jnp.float32)
        turned = pltpu.roll(both, HD, 1)
        for part in (both, turned) if low_lanes else (turned, both):
            stacked.append(jnp.where(keep, part, 0.0))
    return jnp.concatenate(stacked, axis=0).astype(jnp.bfloat16)


def unstack_heads(stacked, low_lanes):
    rows = stacked.shape[0] // QPK
    lane = lax.broadcasted_iota(jnp.int32, (rows, 128), 1)
    blocks = []
    for pair in range(QPK // 2):
        first = stacked[2 * pair * rows : (2 * pair + 1) * rows]
        second = stacked[(2 * pair + 1) * rows : (2 * pair + 2) * rows]
        if low_lanes:
            second = pltpu.roll(second, HD, 1)
        else:
            first = pltpu.roll(first, HD, 1)
        blocks.append(jnp.where(lane < HD, first, second))
    return blocks


def key_blocks(pos_ref, tile, tq, tk, step, low=0, high=None):
    tokens = pos_ref.shape[0]
    query = tile * tq
    start = REACH * tokens + query
    first = jnp.maximum(start - pos_ref[query], low)
    last_start = start + tq - 1 - pos_ref[query + tq - 1]
    end = (start + tq - 1) // tk + 1
    if high is not None:
        end = jnp.minimum(end, high // tk)

    def body(block, carry):
        key = block * tk
        clear = (key >= last_start) & (key + tk - 1 <= start)

        @pl.when(clear)
        def _():
            step(key, False)

        @pl.when(jnp.logical_not(clear))
        def _():
            step(key, True)

        return carry

    lax.fori_loop(first // tk, end, body, 0)


def allowed_block(key, tile, tokens, tk, tq, back_row):
    key_at = key + lax.broadcasted_iota(jnp.int32, (tk, tq), 0)
    query_at = REACH * tokens + tile * tq + lax.broadcasted_iota(jnp.int32, (tk, tq), 1)
    back = query_at - key_at
    allowed = (back >= 0) & (back <= back_row)
    return jnp.concatenate([allowed] * QPK, axis=1)


def attend_step(key, masked, tile, tk, base, back_ref, kv, vx, qs, acc, top, tokens):
    tq = qs.shape[0] // QPK
    scores = lax.dot_general(
        kv[pl.ds(key - base, tk), :], qs[...], COLS_BY_COLS, preferred_element_type=jnp.float32
    )
    if masked:
        allowed = allowed_block(key, tile, tokens, tk, tq, back_ref[0:1, :])
        scores = jnp.where(allowed, scores, NEG_FILL)
    old = top[0:1, :]
    new = jnp.maximum(old, jnp.max(scores, axis=0, keepdims=True))
    top[0:1, :] = new
    probs = jnp.exp2((scores - new) * EXP_SCALE).astype(jnp.bfloat16)
    fade = jnp.exp2((old - new) * EXP_SCALE)
    acc[...] = acc[...] * fade + lax.dot_general(
        vx[pl.ds(key - base, tk), :], probs, ROWS_BY_ROWS, preferred_element_type=jnp.float32
    )


def load_sources(refs, kv, vx):
    tokens = refs[0].shape[0]
    lane = lax.broadcasted_iota(jnp.int32, (tokens, 2 * HD), 1)
    for i, ref in enumerate(refs):
        kv[pl.ds(i * tokens, tokens), :] = ref[...]
        vx[pl.ds(i * tokens, tokens), :] = jnp.where(lane < HD, jnp.ones_like(ref), ref[...])


def attend_here_kernel(tk, pos_ref, q_ref, back_ref, here, acc_ref, top_ref, vx, qs):
    tokens = here.shape[0]
    tq = q_ref.shape[0]
    tile = pl.program_id(0)
    acc, top = acc_ref.at[0], top_ref.at[0]

    @pl.when(tile == 0)
    def _():
        lane = lax.broadcasted_iota(jnp.int32, (tokens, 2 * HD), 1)
        vx[...] = jnp.where(lane < HD, jnp.ones_like(here), here[...])

    qs[...] = stack_heads(q_ref[...], True)
    acc[...] = jnp.zeros_like(acc)
    top[...] = jnp.full_like(top, NEG_FILL)
    base = REACH * tokens

    def step(key, masked):
        attend_step(key, masked, tile, tk, base, back_ref, here, vx, qs, acc, top, tokens)

    key_blocks(pos_ref, tile, tq, tk, step, low=base)


def attend_far_kernel(
    tk, pos_ref, q_ref, back_ref, far_two, far_one, acc_ref, top_ref,
    out_ref, lse_ref, kv, vx, qs, acc, top
):
    tokens = far_one.shape[0]
    tq = q_ref.shape[0]
    tile = pl.program_id(0)

    @pl.when(tile == 0)
    def _():
        load_sources((far_two, far_one), kv, vx)

    qs[...] = stack_heads(q_ref[...], True)
    acc[...] = acc_ref[0]
    top[...] = top_ref[0]

    def step(key, masked):
        attend_step(key, masked, tile, tk, 0, back_ref, kv, vx, qs, acc, top, tokens)

    key_blocks(pos_ref, tile, tq, tk, step, high=REACH * tokens)
    total = acc[...]
    weight = total[0:1]
    blocks = unstack_heads(jnp.transpose(total / weight), False)
    out_ref[...] = jnp.concatenate(blocks, axis=1).astype(jnp.bfloat16)
    lse = top[0:1, :] * EXP_SCALE + jnp.log2(weight)
    lse_ref[...] = jnp.broadcast_to(lse, (8, lse.shape[1]))[None]


def attend_here(queries, here, positions, back_rows, group, tq, tk):
    tokens = queries.shape[0]
    state = (
        jax.ShapeDtypeStruct((tokens // tq, 2 * HD, QPK * tq), jnp.float32),
        jax.ShapeDtypeStruct((tokens // tq, 8, QPK * tq), jnp.float32),
    )
    return pl.pallas_call(
        functools.partial(attend_here_kernel, tk),
        grid_spec=pltpu.PrefetchScalarGridSpec(
            num_scalar_prefetch=1,
            grid=(tokens // tq,),
            in_specs=[
                pl.BlockSpec((tq, QPK * HD), lambda i, p: (i, group)),
                pl.BlockSpec((8, tq), lambda i, p: (0, i)),
                pl.BlockSpec((tokens, 2 * HD), lambda i, p: (0, group)),
            ],
            out_specs=[pl.BlockSpec((1, *shape.shape[1:]), lambda i, p: (i, 0, 0)) for shape in state],
            scratch_shapes=[
                pltpu.VMEM((tokens, 2 * HD), jnp.bfloat16),
                pltpu.VMEM((QPK * tq, 2 * HD), jnp.bfloat16),
            ],
        ),
        out_shape=state,
        compiler_params=pltpu.CompilerParams(vmem_limit_bytes=VMEM_LIMIT),
        cost_estimate=cost(10),
        name="attend_here",
    )(positions, queries, back_rows, here)


def attend_far(queries, far, state, positions, back_rows, group, tq, tk):
    tokens = queries.shape[0]
    kv_spec = pl.BlockSpec((tokens, 2 * HD), lambda i, p: (0, group))
    return pl.pallas_call(
        functools.partial(attend_far_kernel, tk),
        grid_spec=pltpu.PrefetchScalarGridSpec(
            num_scalar_prefetch=1,
            grid=(tokens // tq,),
            in_specs=[
                pl.BlockSpec((tq, QPK * HD), lambda i, p: (i, group)),
                pl.BlockSpec((8, tq), lambda i, p: (0, i)),
                kv_spec,
                kv_spec,
            ]
            + [pl.BlockSpec((1, *part.shape[1:]), lambda i, p: (i, 0, 0)) for part in state],
            out_specs=[
                pl.BlockSpec((tq, QPK * HD), lambda i, p: (i, 0)),
                pl.BlockSpec((1, 8, QPK * tq), lambda i, p: (i, 0, 0)),
            ],
            scratch_shapes=[
                pltpu.VMEM((REACH * tokens, 2 * HD), jnp.bfloat16),
                pltpu.VMEM((REACH * tokens, 2 * HD), jnp.bfloat16),
                pltpu.VMEM((QPK * tq, 2 * HD), jnp.bfloat16),
                pltpu.VMEM((2 * HD, QPK * tq), jnp.float32),
                pltpu.VMEM((8, QPK * tq), jnp.float32),
            ],
        ),
        out_shape=[
            jax.ShapeDtypeStruct((tokens, QPK * HD), jnp.bfloat16),
            jax.ShapeDtypeStruct((tokens // tq, 8, QPK * tq), jnp.float32),
        ],
        compiler_params=pltpu.CompilerParams(vmem_limit_bytes=VMEM_LIMIT),
        cost_estimate=cost(14),
        name="attend_far",
    )(positions, queries, back_rows, *far, *state)


def attend_back_kernel(
    tk, pos_ref, q_ref, do_ref, o_ref, back_ref, lse_ref, cos_ref, sin_ref, far_two, far_one, here,
    dq_ref, d_far_two, d_far_one, d_here, kv, dkv, qs, dos, dq
):
    tokens = here.shape[0]
    tq = q_ref.shape[0]
    tile = pl.program_id(0)

    @pl.when(tile == 0)
    def _():
        for i, ref in enumerate((far_two, far_one, here)):
            kv[pl.ds(i * tokens, tokens), :] = ref[...]
        dkv[...] = jnp.zeros_like(dkv)

    qs[...] = stack_heads(q_ref[...], True)
    dos[...] = stack_heads(do_ref[...], False)
    dq[...] = jnp.zeros_like(dq)
    product = dos[...].astype(jnp.float32) * stack_heads(o_ref[...], False).astype(jnp.float32)
    delta = jnp.sum(jnp.transpose(product), axis=0, keepdims=True)
    lse = lse_ref[0, 0:1, :]

    def step(key, masked):
        keys = kv[pl.ds(key, tk), :]
        scores = lax.dot_general(keys, qs[...], COLS_BY_COLS, preferred_element_type=jnp.float32)
        probs = jnp.exp2(scores * EXP_SCALE - lse)
        if masked:
            allowed = allowed_block(key, tile, tokens, tk, tq, back_ref[0:1, :])
            probs = jnp.where(allowed, probs, 0.0)
        d_probs = lax.dot_general(keys, dos[...], COLS_BY_COLS, preferred_element_type=jnp.float32)
        d_scores = (probs * (d_probs - delta)).astype(jnp.bfloat16)
        d_keys = jnp.dot(d_scores, qs[...], preferred_element_type=jnp.float32)
        d_values = jnp.dot(probs.astype(jnp.bfloat16), dos[...], preferred_element_type=jnp.float32)
        dkv[pl.ds(key, tk), :] += d_keys * HD**-0.5 + d_values
        dq[...] += lax.dot_general(
            d_scores, keys, ROWS_BY_ROWS, preferred_element_type=jnp.float32
        )

    key_blocks(pos_ref, tile, tq, tk, step)
    cos, sin = cos_ref[...], sin_ref[...]
    blocks = unstack_heads(dq[...] * HD**-0.5, True)
    blocks = [block * cos - turn_halves(block) * sin for block in blocks]
    dq_ref[...] = jnp.concatenate(blocks, axis=1).astype(jnp.bfloat16)

    @pl.when(tile == pl.num_programs(0) - 1)
    def _():
        d_far_two[...] = dkv[pl.ds(0, tokens), :].astype(jnp.bfloat16)
        d_far_one[...] = dkv[pl.ds(tokens, tokens), :].astype(jnp.bfloat16)
        d_here[...] = dkv[pl.ds(2 * tokens, tokens), :]


def attend_back(
    queries, d_attn, attn, lse, sources, positions, back_rows, cos, sin, group, tq, tk
):
    tokens = queries.shape[0]
    kv_spec = pl.BlockSpec((tokens, 2 * HD), lambda i, p: (0, group))
    own_kv = pl.BlockSpec((tokens, 2 * HD), lambda i, p: (0, 0))
    q_spec = pl.BlockSpec((tq, QPK * HD), lambda i, p: (i, group))
    own_q = pl.BlockSpec((tq, QPK * HD), lambda i, p: (i, 0))
    angle_spec = pl.BlockSpec((tq, 128), lambda i, p: (i, 0))
    return pl.pallas_call(
        functools.partial(attend_back_kernel, tk),
        grid_spec=pltpu.PrefetchScalarGridSpec(
            num_scalar_prefetch=1,
            grid=(tokens // tq,),
            in_specs=[
                q_spec,
                q_spec,
                own_q,
                pl.BlockSpec((8, tq), lambda i, p: (0, i)),
                pl.BlockSpec((1, 8, QPK * tq), lambda i, p: (i, 0, 0)),
                angle_spec,
                angle_spec,
                kv_spec,
                kv_spec,
                kv_spec,
            ],
            out_specs=[own_q, own_kv, own_kv, own_kv],
            scratch_shapes=[
                pltpu.VMEM(((REACH + 1) * tokens, 2 * HD), jnp.bfloat16),
                pltpu.VMEM(((REACH + 1) * tokens, 2 * HD), jnp.float32),
                pltpu.VMEM((QPK * tq, 2 * HD), jnp.bfloat16),
                pltpu.VMEM((QPK * tq, 2 * HD), jnp.bfloat16),
                pltpu.VMEM((QPK * tq, 2 * HD), jnp.float32),
            ],
        ),
        out_shape=[
            jax.ShapeDtypeStruct((tokens, QPK * HD), jnp.bfloat16),
            jax.ShapeDtypeStruct((tokens, 2 * HD), jnp.bfloat16),
            jax.ShapeDtypeStruct((tokens, 2 * HD), jnp.bfloat16),
            jax.ShapeDtypeStruct((tokens, 2 * HD), jnp.float32),
        ],
        compiler_params=pltpu.CompilerParams(vmem_limit_bytes=VMEM_LIMIT),
        cost_estimate=cost(28),
        name="attend_back",
    )(positions, queries, d_attn, attn, back_rows, lse, cos, sin, *sources)


def mix_kernel(groups, cos_ref, sin_ref, *refs):
    out_ref = refs[-1]
    cos, sin = cos_ref[...], sin_ref[...]
    key_lane = lax.broadcasted_iota(jnp.int32, cos.shape, 1) < HD
    for group in range(groups):
        dq_ref, here, from_one, from_two = refs[4 * group : 4 * group + 4]
        base = group * (QPK + 2) * HD
        out_ref[:, base : base + QPK * HD] = dq_ref[...]
        total = here[...] + from_one[...].astype(jnp.float32) + from_two[...].astype(jnp.float32)
        turned = total * cos - turn_halves(total) * sin
        out_ref[:, base + QPK * HD : base + (QPK + 2) * HD] = jnp.where(
            key_lane, turned, total
        ).astype(jnp.bfloat16)


def mix_grads(parts, cos, sin, tile):
    tokens = cos.shape[0]
    groups = len(parts)

    def rows(wide):
        return pl.BlockSpec((tile, wide), lambda i: (i, 0))

    flat = [array for part in parts for array in part]
    return pl.pallas_call(
        functools.partial(mix_kernel, groups),
        grid=(tokens // tile,),
        in_specs=[rows(128), rows(128)] + [rows(array.shape[1]) for array in flat],
        out_specs=rows(groups * (QPK + 2) * HD),
        out_shape=jax.ShapeDtypeStruct((tokens, groups * (QPK + 2) * HD), jnp.bfloat16),
        compiler_params=pltpu.CompilerParams(vmem_limit_bytes=VMEM_LIMIT),
        cost_estimate=cost(3),
        name="mix_grads",
    )(cos, sin, *flat)


def out_step_kernel(distances, last, rank_ref, *refs):
    refs = list(refs)
    base_ref = refs.pop(0)
    gain_ref = refs.pop(0) if last else None
    total = base_ref[...].astype(jnp.float32)
    for distance, count in distances:
        piece = refs.pop(0)[...]
        if count == 2:
            piece = jnp.where(rank_ref[0] >= distance, piece, refs.pop(0)[...])
        total = total + jnp.dot(piece, refs.pop(0)[...], preferred_element_type=jnp.float32)
    refs[0][...] = total
    if last:
        inverse = lax.rsqrt(jnp.mean(total * total, axis=1, keepdims=True) + NORM_EPS)
        refs[1][...] = (total * inverse * gain_ref[...]).astype(jnp.bfloat16)


def out_step(base, pieces, rank, weight, gain=None, tile=256):
    tokens, width = base.shape
    depth = pieces[0][1][0].shape[1]
    last = gain is not None
    slots = weight.shape[0] // depth

    def rows(wide):
        return pl.BlockSpec((tile, wide), lambda i, r: (i, 0))

    def slot_rows(distance, count):
        def index(i, r):
            slot = r[0] - distance
            if count == 2:
                slot = jnp.where(r[0] >= distance, slot, r[0] + distance)
            return jnp.clip(slot, 0, slots - 1), 0

        return pl.BlockSpec((depth, width), index)

    operands, specs = [base], [rows(width)]
    if last:
        operands.append(gain[None])
        specs.append(pl.BlockSpec((1, width), lambda i, r: (0, 0)))
    for distance, blocks in pieces:
        operands += [*blocks, weight]
        specs += [rows(depth)] * len(blocks) + [slot_rows(distance, len(blocks))]
    outs = [jax.ShapeDtypeStruct((tokens, width), jnp.float32)]
    if last:
        outs.append(jax.ShapeDtypeStruct((tokens, width), jnp.bfloat16))
    distances = tuple((distance, len(blocks)) for distance, blocks in pieces)
    made = pl.pallas_call(
        functools.partial(out_step_kernel, distances, last),
        grid_spec=pltpu.PrefetchScalarGridSpec(
            num_scalar_prefetch=1,
            grid=(tokens // tile,),
            in_specs=specs,
            out_specs=[rows(width)] * len(outs),
        ),
        out_shape=outs,
        compiler_params=pltpu.CompilerParams(vmem_limit_bytes=VMEM_LIMIT),
        cost_estimate=cost(7),
        name="out_step",
    )(jnp.reshape(rank, (1,)).astype(jnp.int32), *operands)
    return made if last else made[0]


def own_kernel(rank_ref, *refs):
    *pieces, out_ref = refs

    def put(piece):
        out_ref[...] = piece[...]

    pick_piece(pieces, rank_ref[0] - pl.program_id(0), put)


def own_rows_of_heads(pieces, rank, own):
    size = (len(pieces) + 1) // 2
    columns = pieces[0].shape[1]
    return pl.pallas_call(
        own_kernel,
        grid_spec=pltpu.PrefetchScalarGridSpec(
            num_scalar_prefetch=1,
            grid=(size,),
            in_specs=[pl.BlockSpec((own, columns), lambda i, r: (r[0], 0))] * len(pieces),
            out_specs=pl.BlockSpec((own, columns), lambda i, r: (0, i)),
        ),
        out_shape=jax.ShapeDtypeStruct((own, columns * size), pieces[0].dtype),
        compiler_params=pltpu.CompilerParams(vmem_limit_bytes=VMEM_LIMIT),
        cost_estimate=cost(2),
        name="own_rows_of_heads",
    )(jnp.reshape(rank, (1,)).astype(jnp.int32), *pieces)


def gate_kernel(n_ref, w_ref, dh_ref, hidden_ref, dgu_ref):
    wide = dh_ref.shape[1]
    both = jnp.dot(n_ref[...], w_ref[...], preferred_element_type=jnp.float32)
    gate, up = both[:, :wide], both[:, wide:]
    sigmoid = jax.nn.sigmoid(gate)
    silu = gate * sigmoid
    d_hidden = dh_ref[...].astype(jnp.float32)
    hidden_ref[...] = (silu * up).astype(jnp.bfloat16)
    d_gate = d_hidden * up * (sigmoid + silu * (1.0 - sigmoid))
    dgu_ref[...] = jnp.concatenate([d_gate, d_hidden * silu], axis=1).astype(jnp.bfloat16)


def gate_and_back(normed, weight, d_hidden, tile, wide):
    tokens, width = normed.shape
    units = d_hidden.shape[1]
    cell = pl.BlockSpec((tile, wide), lambda j, i: (i, j))
    pair_cell = pl.BlockSpec((tile, 2 * wide), lambda j, i: (i, j))
    return pl.pallas_call(
        gate_kernel,
        grid=(units // wide, tokens // tile),
        in_specs=[
            pl.BlockSpec((tile, width), lambda j, i: (i, 0)),
            pl.BlockSpec((width, 2 * wide), lambda j, i: (0, j)),
            cell,
        ],
        out_specs=[cell, pair_cell],
        out_shape=[
            jax.ShapeDtypeStruct((tokens, units), jnp.bfloat16),
            jax.ShapeDtypeStruct((tokens, 2 * units), jnp.bfloat16),
        ],
        compiler_params=pltpu.CompilerParams(vmem_limit_bytes=VMEM_LIMIT),
        cost_estimate=cost(27),
        name="gate_and_back",
    )(normed, weight, d_hidden)


def blocks_kernel(chunks_ref, *refs):
    count = (len(refs) - 1) // 2
    left = jnp.concatenate([ref[...] for ref in refs[:count]], axis=0)
    product = lax.dot_general(
        left, refs[count][...], COLS_BY_COLS, preferred_element_type=jnp.float32
    ).astype(jnp.bfloat16)
    rows = refs[0].shape[0]
    for i, out_ref in enumerate(refs[count + 1 :]):
        out_ref[...] = product[i * rows : (i + 1) * rows]


def blocks_times(left, right, chunks, rows, wide, micros):
    depth = left.shape[1]
    count = chunks.shape[0]

    def block_spec(i):
        return pl.BlockSpec((rows, depth), lambda j, c: (c[i], 0))

    return pl.pallas_call(
        blocks_kernel,
        grid_spec=pltpu.PrefetchScalarGridSpec(
            num_scalar_prefetch=1,
            grid=(right.shape[0] // wide,),
            in_specs=[block_spec(i) for i in range(count)]
            + [pl.BlockSpec((wide, depth), lambda j, c: (j, 0))],
            out_specs=[pl.BlockSpec((rows, wide), lambda j, c: (0, j))] * count,
        ),
        out_shape=[jax.ShapeDtypeStruct((rows, right.shape[0]), jnp.bfloat16)] * count,
        compiler_params=pltpu.CompilerParams(vmem_limit_bytes=VMEM_LIMIT),
        cost_estimate=cost(micros),
        name="blocks_times",
    )(chunks, *[left] * count, right)


def gain_kernel(part_ref, w_ref, out_ref):
    product = part_ref[...].astype(jnp.float32) * w_ref[...].astype(jnp.float32)
    ones = jnp.ones((8, product.shape[1]), jnp.float32)
    out_ref[...] = lax.dot_general(
        ones, product, COLS_BY_COLS, precision=lax.Precision.HIGHEST,
        preferred_element_type=jnp.float32,
    )


def row_products(part, weight, tile):
    rows, columns = part.shape
    cell = pl.BlockSpec((tile, columns), lambda i: (i, 0))
    sums = pl.pallas_call(
        gain_kernel,
        grid=(rows // tile,),
        in_specs=[cell, cell],
        out_specs=pl.BlockSpec((8, tile), lambda i: (0, i)),
        out_shape=jax.ShapeDtypeStruct((8, rows), jnp.float32),
        compiler_params=pltpu.CompilerParams(vmem_limit_bytes=VMEM_LIMIT),
        cost_estimate=cost(4),
        name="row_products",
    )(part, weight)
    return sums[0]


def norm_back_rows(vector, grad_in, gain):
    inverse = lax.rsqrt(jnp.mean(vector * vector, axis=1, keepdims=True) + NORM_EPS)
    scaled = grad_in * gain
    mean = jnp.mean(vector * scaled, axis=1, keepdims=True)
    grad = inverse * scaled - vector * (inverse * inverse * inverse * mean)
    return grad, jnp.sum(grad_in * vector * inverse, axis=0, keepdims=True)


def sum_refs(refs):
    total = refs[0][...].astype(jnp.float32)
    for ref in refs[1:]:
        total = total + ref[...].astype(jnp.float32)
    return total


def mid_kernel(rank_ref, mid_ref, dy_ref, gain_ref, *refs):
    *parts, d_mid_ref, branch_ref, mid_out, gain_grad_ref = refs
    mid = mid_ref[...]
    grad, gain_grad = norm_back_rows(mid, sum_refs(parts), gain_ref[...])
    d_mid = dy_ref[...].astype(jnp.float32) + grad
    d_mid_ref[...] = d_mid
    branch_ref[...] = d_mid.astype(jnp.bfloat16)
    mid_out[...] = mid
    gain_grad = jnp.broadcast_to(gain_grad, gain_grad_ref.shape)

    @pl.when(pl.program_id(0) == 0)
    def _():
        gain_grad_ref[...] = gain_grad

    @pl.when(pl.program_id(0) > 0)
    def _():
        gain_grad_ref[...] += gain_grad


def back_to_mid(parts, mid_rows, rank, output_grad, gain):
    own, width = output_grad.shape
    tile = min(64, own)
    tiles = own // tile

    def rows(index):
        return pl.BlockSpec((tile, width), index)

    own_rows = rows(lambda i, r: (i, 0))
    outs = pl.pallas_call(
        mid_kernel,
        grid_spec=pltpu.PrefetchScalarGridSpec(
            num_scalar_prefetch=1,
            grid=(tiles,),
            in_specs=[
                rows(lambda i, r: (r[0] * tiles + i, 0)),
                own_rows,
                pl.BlockSpec((1, width), lambda i, r: (0, 0)),
            ]
            + [own_rows] * len(parts),
            out_specs=[own_rows, own_rows, own_rows, pl.BlockSpec((8, width), lambda i, r: (0, 0))],
        ),
        out_shape=[
            jax.ShapeDtypeStruct((own, width), jnp.float32),
            jax.ShapeDtypeStruct((own, width), jnp.bfloat16),
            jax.ShapeDtypeStruct((own, width), jnp.float32),
            jax.ShapeDtypeStruct((8, width), jnp.float32),
        ],
        compiler_params=pltpu.CompilerParams(vmem_limit_bytes=VMEM_LIMIT),
        cost_estimate=cost(4),
        name="back_to_mid",
    )(jnp.reshape(rank, (1,)).astype(jnp.int32), mid_rows, output_grad, gain[None], *parts)
    return outs[0], outs[1], outs[2], outs[3][0]


def input_kernel(x_ref, d_mid_ref, gain_ref, *refs):
    *parts, out_ref = refs
    x = x_ref[...].astype(jnp.float32)
    grad, _ = norm_back_rows(x, sum_refs(parts), gain_ref[...])
    out_ref[...] = d_mid_ref[...] + grad


def back_to_input(parts, layer_input, d_mid, gain):
    own, width = layer_input.shape
    tile = min(64, own)
    rows = pl.BlockSpec((tile, width), lambda i: (i, 0))
    return pl.pallas_call(
        input_kernel,
        grid=(own // tile,),
        in_specs=[rows, rows, pl.BlockSpec((1, width), lambda i: (0, 0))] + [rows] * len(parts),
        out_specs=rows,
        out_shape=jax.ShapeDtypeStruct((own, width), jnp.float32),
        compiler_params=pltpu.CompilerParams(vmem_limit_bytes=VMEM_LIMIT),
        cost_estimate=cost(4),
        name="back_to_input",
    )(layer_input, d_mid, gain[None], *parts)


def round_kernel(w_ref, out_ref):
    out_ref[...] = w_ref[0].astype(jnp.bfloat16)


def round_interleaved(weight, wide):
    _, rows, units = weight.shape
    return pl.pallas_call(
        round_kernel,
        grid=(units // wide, 2),
        in_specs=[pl.BlockSpec((1, rows, wide), lambda j, k: (k, 0, j))],
        out_specs=pl.BlockSpec((rows, wide), lambda j, k: (0, 2 * j + k)),
        out_shape=jax.ShapeDtypeStruct((rows, 2 * units), jnp.bfloat16),
        cost_estimate=cost(6),
        name="round_interleaved",
    )(weight)


def adam_kernel(g_ref, w_ref, m_ref, s_ref, grad_ref, w_out, m_out, s_out, copy_out):
    grad = g_ref[...].astype(jnp.float32)
    new, moment, square, _ = adam_step(w_ref[0], grad, m_ref[0], s_ref[0])
    grad_ref[0] = grad
    w_out[0] = new
    m_out[0] = moment
    s_out[0] = square
    copy_out[0] = new.astype(jnp.bfloat16)


def adam_interleaved(grad, weight, moment, square, wide):
    _, rows, units = weight.shape
    cell = pl.BlockSpec((1, rows, wide), lambda j, k: (k, 0, j))
    shape = jax.ShapeDtypeStruct(weight.shape, jnp.float32)
    return pl.pallas_call(
        adam_kernel,
        grid=(units // wide, 2),
        in_specs=[pl.BlockSpec((rows, wide), lambda j, k: (0, 2 * j + k)), cell, cell, cell],
        out_specs=[cell] * 5,
        out_shape=[shape] * 4 + [jax.ShapeDtypeStruct(weight.shape, jnp.bfloat16)],
        compiler_params=pltpu.CompilerParams(vmem_limit_bytes=VMEM_LIMIT),
        cost_estimate=cost(13),
        name="adam_interleaved",
    )(grad, weight, moment, square)


def angle_tables(positions):
    half_size = HD // 2
    freq = ROPE_BASE ** (-(jnp.arange(half_size).astype(jnp.float32) * 2.0 / HD))
    angle = positions.astype(jnp.float32)[:, None] * freq[None, :]
    cos, sin = jnp.cos(angle), jnp.sin(angle)
    return jnp.concatenate([cos] * 4, axis=1), jnp.concatenate([-sin, sin] * 2, axis=1)


def adam_step(weight_old, grad_new, moment_one, moment_two):
    moment_next = BETA * moment_one + (1.0 - BETA) * grad_new
    square_next = BETA * moment_two + (1.0 - BETA) * grad_new * grad_new
    change = -RATE * (moment_next / (jnp.sqrt(square_next) + ADAM_EPS) + DECAY * weight_old)
    return (weight_old + change, moment_next, square_next, change)


def local(
    layer_input,
    output_grad,
    segment_ids,
    positions,
    qkv_weight,
    qkv_moment,
    qkv_square,
    out_weight,
    out_moment,
    out_square,
    gate_up_weight,
    gate_up_moment,
    gate_up_square,
    down_weight,
    down_moment,
    down_square,
    norm_gains,
    gains_moment,
    gains_square,
):
    low = low_type = jnp.bfloat16
    full = jnp.float32
    own, width = layer_input.shape
    tokens = positions.shape[0]
    rank = lax.axis_index("tp")
    units = down_weight.shape[0]
    groups = qkv_weight.shape[1] // ((QPK + 2) * HD)
    head_columns = groups * QPK * HD
    tile = min(256, own)
    gain_one = norm_gains[0]
    gain_two = norm_gains[1]

    wide = min(512, units)

    close = lax.optimization_barrier

    low_qkv = qkv_weight.astype(low)
    low_down = down_weight.astype(low)
    w_qkv = lax.all_gather(low_qkv, "seq", axis=0, tiled=True)
    low_gate_up = round_interleaved(gate_up_weight, wide)
    w_gate_up = lax.all_gather(low_gate_up, "seq", axis=0, tiled=True)
    low_out = out_weight.astype(low)
    cos, sin = angle_tables(positions)
    back_rows = jnp.broadcast_to(positions[None, :], (8, tokens))
    side = (low_down, low_out, cos, sin, back_rows)
    x_line = LineGather(layer_input, "tp")
    for _ in range(x_line.hops):
        x_line.hop()
        x_line.moving, side = close((x_line.moving, side))
    pieces, side, w_qkv, output_grad = close((x_line.pieces, side, w_qkv, output_grad))
    low_down, low_out, cos, sin, back_rows = side

    dy_line = LineGather(output_grad, "tp")
    dy_line.hop()
    made = project_qkv(pieces, rank, w_qkv, gain_one, cos, sin)
    made, dy_line.moving, low_out, low_down = close((made, dy_line.moving, low_out, low_down))
    x_rows, normed_one, queries, kv = made
    w_down = lax.all_gather(low_down, "seq", axis=1, tiled=True)
    far = [along_sequence(kv, distance, tokens) for distance in (2, 1)]
    if dy_line.hops > 1:
        dy_line.hop()
    states = [
        attend_here(queries, kv, positions, back_rows, group, 256, 512) for group in range(groups)
    ]
    far, states, queries, low_out, w_gate_up, dy_line.moving = close(
        (far, states, queries, low_out, w_gate_up, dy_line.moving)
    )
    out_strip = swap_gather(low_out, "tp")
    for _ in range(2, dy_line.hops):
        dy_line.hop()
    attn, lse = [], []
    for group in range(groups):
        out, log_total = attend_far(
            queries, far, states[group], positions, back_rows, group, 256, 512
        )
        attn.append(out)
        lse.append(log_total)
    attn, lse, dy_pieces, w_down, x_rows, out_strip = close(
        (attn, lse, dy_line.pieces, w_down, x_rows, out_strip)
    )
    w_out = lax.all_gather(out_strip.reshape(-1, low_out.shape[1]), "seq", axis=1, tiled=True)

    heads_line = LineGather(jnp.concatenate(attn, axis=1), "tp")
    arrived = [(0, [heads_line.from_low[0]])]
    total = x_rows
    for index in range(heads_line.hops):
        heads_line.hop()
        if index == 0:
            grad_rows = place_rows(dy_pieces, rank)
            d_hidden = contract_cols(grad_rows, w_down).astype(low)
            heads_line.moving, grad_rows, d_hidden, total = close(
                (heads_line.moving, grad_rows, d_hidden, total)
            )
        elif index < heads_line.hops - 1:
            heads_line.moving, w_out = close((heads_line.moving, w_out))
        else:
            total = out_step(total, arrived, rank, w_out)
            heads_line.moving, total = close((heads_line.moving, total))
            arrived = []
        below, above = heads_line.moving
        step = heads_line.step
        if 2 * step > heads_line.hops:
            arrived.append((step, [below, above]))
        else:
            arrived += [(step, [below]), (-step, [above])]

    mid_rows, normed_two = out_step(total, arrived, rank, w_out, gain_two)
    mid_rows, normed_two, w_gate_up, d_hidden = close((mid_rows, normed_two, w_gate_up, d_hidden))
    hidden, d_gate_up = close(gate_and_back(normed_two, w_gate_up, d_hidden, 512, wide))
    down_grad = contract_rows(hidden, grad_rows).astype(low)
    down_grad, hidden, d_gate_up, normed_two, grad_rows = close(
        (down_grad, hidden, d_gate_up, normed_two, grad_rows)
    )
    down_grad = lax.psum_scatter(down_grad, "seq", scatter_dimension=1, tiled=True)
    peers = peers_of("tp")
    first = blocks_times(d_gate_up, w_gate_up, peers[:1], own, 512, 9)
    first, side = close((first, (hidden, d_gate_up, normed_two, grad_rows)))
    back_line = LineScatter(first, "tp")
    for index in range(back_line.hops):
        back_line.hop()
        hidden, d_gate_up, normed_two, grad_rows = side
        if index == 0:
            second = blocks_times(d_gate_up, w_gate_up, peers[1:], own, 256, 22)
            back_line.moving, side, second = close((back_line.moving, side, second))
            back_line.made += second
        elif index == 1:
            gate_up_grad = contract_rows(normed_two, d_gate_up).astype(low)
            back_line.moving, side, gate_up_grad = close((back_line.moving, side, gate_up_grad))
            gate_up_grad = lax.psum_scatter(gate_up_grad, "seq", scatter_dimension=0, tiled=True)
        elif index == 2:
            partial_out = jnp.dot(hidden, w_down, preferred_element_type=full).astype(low)
            back_line.moving, side, partial_out = close((back_line.moving, side, partial_out))
        else:
            back_line.moving, side = close((back_line.moving, side))
    d_mid, d_branch, mid, gain_two_grad = back_to_mid(
        back_line.parts, mid_rows, rank, output_grad, gain_two
    )

    d_attn = contract_cols(d_branch, w_out).astype(low)
    d_attn, d_branch, d_mid, mid, gain_two_grad, partial_out = close(
        (d_attn, d_branch, d_mid, mid, gain_two_grad, partial_out)
    )
    d_attn = lax.all_to_all(d_attn, "tp", split_axis=1, concat_axis=0, tiled=True)
    own_heads = own_rows_of_heads(heads_line.pieces, rank, own)
    out_grad = contract_rows(own_heads, d_branch).astype(low)
    d_attn, out_grad, partial_out, down_grad = close((d_attn, out_grad, partial_out, down_grad))
    out_grad = lax.psum_scatter(out_grad, "seq", scatter_dimension=1, tiled=True)
    result = swap_scatter_parts(partial_out, "tp")
    grads = []
    travelled = []
    for group in range(groups):
        made = attend_back(
            queries, d_attn, attn[group], lse[group], [*far, kv], positions, back_rows,
            cos, sin, group, 256, 512,
        )
        made, d_attn, travelled = close((made, d_attn, travelled))
        grads.append(made)
        travelled.append(
            [along_sequence(made[2], -1, tokens), along_sequence(made[1], -2, tokens)]
        )
    down_new = adam_step(down_weight, down_grad.astype(full), down_moment, down_square)
    down_new, grads, travelled, down_grad, result = close(
        (down_new, grads, travelled, down_grad, result)
    )
    d_mixed = mix_grads(
        [(made[0], made[3], *moved) for made, moved in zip(grads, travelled, strict=True)],
        cos, sin, tile,
    )
    made = blocks_times(d_mixed, w_qkv, peers, own, 512, 7)
    made, d_mixed, gate_up_grad = close((made, d_mixed, gate_up_grad))
    in_line = LineScatter(made, "tp")
    for index in range(in_line.hops):
        in_line.hop()
        if index == 0:
            qkv_grad = contract_rows(normed_one, d_mixed).astype(low)
            gain_one_grad = row_products(qkv_grad, w_qkv, min(512, width)) / gain_one
            gains_grad = jnp.stack([gain_one_grad, gain_two_grad])
            in_line.moving, qkv_grad, gains_grad = close((in_line.moving, qkv_grad, gains_grad))
            qkv_grad = lax.psum_scatter(qkv_grad, "seq", scatter_dimension=0, tiled=True)
        elif index == 1:
            gate_up_new = adam_interleaved(
                gate_up_grad, gate_up_weight, gate_up_moment, gate_up_square, wide
            )
            gains_grad = sum_by_swaps(gains_grad, "seq")
            in_line.moving, gate_up_new, gains_grad, out_grad = close(
                (in_line.moving, gate_up_new, gains_grad, out_grad)
            )
            out_parts = swap_scatter_parts(out_grad, "tp")
        elif index == 2:
            gains_grad = sum_at_once(gains_grad, "tp")
            outputs = (mid + sum_parts(result)).astype(low)
            in_line.moving, gains_grad, out_parts, outputs = close(
                (in_line.moving, gains_grad, out_parts, outputs)
            )
        else:
            in_line.moving = close(in_line.moving)
    input_grad = back_to_input(in_line.parts, layer_input, d_mid, gain_one)
    out_grad = sum_parts(out_parts)
    out_new = adam_step(out_weight, out_grad, out_moment, out_square)

    qkv_grad = qkv_grad.astype(full)
    out_grad = out_grad.astype(full)
    down_grad = down_grad.astype(full)
    qkv_new = adam_step(qkv_weight, qkv_grad, qkv_moment, qkv_square)
    gains_new = adam_step(norm_gains, gains_grad, gains_moment, gains_square)
    return (
        outputs,
        input_grad,
        qkv_grad,
        qkv_new[0],
        qkv_new[1],
        qkv_new[2],
        qkv_new[0].astype(low),
        out_grad,
        out_new[3],
        out_new[1],
        out_new[2],
        *gate_up_new,
        down_grad,
        down_new[0],
        down_new[1],
        down_new[2],
        down_new[0].astype(low),
        gains_grad,
        gains_new[3],
        gains_new[1],
        gains_new[2],
    )


def solution(mesh):
    tokens = P(("seq", "tp"), None)
    rows = P("seq", "tp")
    columns = P("tp", "seq")
    pair = P(None, "seq", "tp")
    return jax.shard_map(
        local,
        mesh=mesh,
        in_specs=(
            (tokens,) * 2 + (P("seq"),) * 2 + (rows,) * 3 + (columns,) * 3 + (pair,) * 3
            + (columns,) * 3 + (P(),) * 3
        ),
        out_specs=(
            (tokens,) * 2 + (rows,) * 5 + (columns,) * 4 + (pair,) * 5 + (columns,) * 5 + (P(),) * 4
        ),
        check_vma=False,
    )
```

```python
import functools

import jax
import jax.numpy as jnp
from jax import lax
from jax.experimental import pallas as pl
from jax.experimental.pallas import tpu as pltpu
from jax.sharding import PartitionSpec as P

HD = 64
QPK = 4
REACH = 2
SEQLEN = 4096

NORM_EPS = 1e-05
ROPE_BASE = 500000.0
BETA = 0.5
RATE = 0.02
DECAY = 0.1
ADAM_EPS = 1e-08
NEG_FILL = -1e30
LOG2E = 1.4426950408889634
EXP_SCALE = HD**-0.5 * LOG2E
VMEM_LIMIT = 48 * 2**20

ROWS_BY_ROWS = (((0,), (0,)), ((), ()))
COLS_BY_COLS = (((1,), (1,)), ((), ()))


def cost(micros):
    return pl.CostEstimate(
        flops=int(micros * 1.15e9), transcendentals=0, bytes_accessed=int(micros * 3.0e6)
    )


def after(block, *others):
    return lax.optimization_barrier((block, *others))[0]


def contract_rows(left, right):
    return lax.dot_general(left, right, ROWS_BY_ROWS, preferred_element_type=jnp.float32)


def contract_cols(left, right):
    return lax.dot_general(left, right, COLS_BY_COLS, preferred_element_type=jnp.float32)


class LineGather:
    def __init__(self, block, axis):
        self.axis = axis
        self.hops = lax.axis_size(axis) - 1
        self.from_low = [block]
        self.from_high = [block]

    @property
    def step(self):
        return len(self.from_low) - 1

    def hop(self):
        size, passed = self.hops + 1, self.step
        up = [(i, i + 1) for i in range(passed, size - 1)]
        down = [(i, i - 1) for i in range(1, size - passed)]
        self.from_low.append(lax.ppermute(self.from_low[-1], self.axis, up))
        self.from_high.append(lax.ppermute(self.from_high[-1], self.axis, down))

    @property
    def moving(self):
        return self.from_low[-1], self.from_high[-1]

    @moving.setter
    def moving(self, pair):
        self.from_low[-1], self.from_high[-1] = pair

    @property
    def pieces(self):
        return [*self.from_low, *self.from_high[1:]]


def send_order(size):
    return [sorted(range(size), key=lambda peer: (-abs(peer - me), peer)) for me in range(size)]


def peers_of(axis):
    size = lax.axis_size(axis)
    return jnp.array(send_order(size), jnp.int32)[lax.axis_index(axis)]


class LineScatter:
    def __init__(self, made, axis):
        self.axis = axis
        self.hops = lax.axis_size(axis) - 1
        self.made = list(made)
        self.step = 0
        self.moving = None

    def addend(self, distance):
        order = send_order(self.hops + 1)
        slots = [
            order[me].index(me + distance) if 0 <= me + distance <= self.hops else None
            for me in range(self.hops + 1)
        ]
        choices = sorted(set(slots) - {None})
        table = jnp.array([choices[0] if slot is None else slot for slot in slots], jnp.int32)
        block = self.made[choices[0]]
        for choice in choices[1:]:
            chosen = table[lax.axis_index(self.axis)] == choice
            block = jnp.where(chosen, self.made[choice], block)
        return block

    def hop(self):
        self.step += 1
        size, step = self.hops + 1, self.step
        to_high = self.addend(size - step)
        to_low = self.addend(step - size)
        if step > 1:
            to_high = to_high + self.moving[0]
            to_low = to_low + self.moving[1]
        self.moving = (
            lax.ppermute(to_high, self.axis, [(i, i + 1) for i in range(step)]),
            lax.ppermute(to_low, self.axis, [(i, i - 1) for i in range(size - step, size)]),
        )

    @property
    def parts(self):
        return [self.made[-1], *self.moving]


def swap_gather(block, axis):
    copies = jnp.broadcast_to(block[None], (lax.axis_size(axis), *block.shape))
    return lax.all_to_all(copies, axis, split_axis=0, concat_axis=0, tiled=True)


def swap_scatter_parts(block, axis):
    size = lax.axis_size(axis)
    parts = block.reshape(size, block.shape[0] // size, block.shape[1])
    return lax.all_to_all(parts, axis, split_axis=0, concat_axis=0, tiled=True)


def sum_parts(parts):
    return jnp.sum(parts.astype(jnp.float32), axis=0)


def sum_by_swaps(block, axis):
    size = lax.axis_size(axis)
    hop = 1
    while hop < size:
        block = block + lax.ppermute(block, axis, [(i, i ^ hop) for i in range(size)])
        hop *= 2
    return block


def sum_at_once(block, axis):
    size = lax.axis_size(axis)
    came = [block]
    for distance in range(1, size):
        route = [(i, (i + distance) % size) for i in range(size)]
        came.append(lax.ppermute(block, axis, route))
    came = jnp.stack(came)
    rank = lax.axis_index(axis)
    total = lax.dynamic_index_in_dim(came, rank, keepdims=False)
    for peer in range(1, size):
        total = total + lax.dynamic_index_in_dim(came, (rank - peer) % size, keepdims=False)
    return total


def along_sequence(block, distance, tokens):
    shards = SEQLEN // tokens
    route = [
        (i, i + distance)
        for i in range(lax.axis_size("seq"))
        if 0 <= i + distance < lax.axis_size("seq") and i // shards == (i + distance) // shards
    ]
    return lax.ppermute(block, "seq", route)


def turn_halves(block):
    lane = lax.broadcasted_iota(jnp.int32, block.shape, 1)
    return jnp.where(lane % HD < HD // 2, pltpu.roll(block, 96, 1), pltpu.roll(block, 32, 1))


def pick_piece(pieces, below, put):
    size = (len(pieces) + 1) // 2
    for distance in range(1 - size, size):
        piece = pieces[distance if distance >= 0 else size - 1 - distance]
        pl.when(below == distance)(functools.partial(put, piece))


def place_kernel(rank_ref, *refs):
    *pieces, out_ref = refs

    def put(piece):
        out_ref[...] = piece[...]

    pick_piece(pieces, rank_ref[0] - pl.program_id(0), put)


def place_rows(pieces, rank):
    own, width = pieces[0].shape
    size = (len(pieces) + 1) // 2
    return pl.pallas_call(
        place_kernel,
        grid_spec=pltpu.PrefetchScalarGridSpec(
            num_scalar_prefetch=1,
            grid=(size,),
            in_specs=[pl.BlockSpec((own, width), lambda i, r: (0, 0))] * len(pieces),
            out_specs=pl.BlockSpec((own, width), lambda i, r: (i, 0)),
        ),
        out_shape=jax.ShapeDtypeStruct((own * size, width), pieces[0].dtype),
        compiler_params=pltpu.CompilerParams(vmem_limit_bytes=VMEM_LIMIT),
        cost_estimate=cost(4),
        name="place_rows",
    )(jnp.reshape(rank, (1,)).astype(jnp.int32), *pieces)


def qkv_kernel(rank_ref, w_ref, gain_ref, cos_ref, sin_ref, *refs):
    x_ref, normed_ref, q_ref, kv_ref = refs[-4:]

    def put(piece):
        x_ref[...] = piece[...]

    pick_piece(refs[:-4], rank_ref[0] - pl.program_id(0), put)
    x = x_ref[...].astype(jnp.float32)
    inverse = lax.rsqrt(jnp.mean(x * x, axis=1, keepdims=True) + NORM_EPS)
    normed = (x * inverse * gain_ref[...]).astype(jnp.bfloat16)
    normed_ref[...] = normed
    mixed = jnp.dot(normed, w_ref[...], preferred_element_type=jnp.float32)
    cos, sin = cos_ref[...], sin_ref[...]
    key_lane = lax.broadcasted_iota(jnp.int32, cos.shape, 1) < HD
    for group in range(mixed.shape[1] // ((QPK + 2) * HD)):
        base = group * (QPK + 2) * HD
        for pair in range(QPK // 2):
            part = mixed[:, base + pair * 128 : base + (pair + 1) * 128]
            part = part * cos + turn_halves(part) * sin
            q_ref[:, group * QPK * HD + pair * 128 : group * QPK * HD + (pair + 1) * 128] = (
                part.astype(jnp.bfloat16)
            )
        part = mixed[:, base + QPK * HD : base + (QPK + 2) * HD]
        part = jnp.where(key_lane, part * cos + turn_halves(part) * sin, part)
        kv_ref[:, group * 128 : (group + 1) * 128] = part.astype(jnp.bfloat16)


def project_qkv(pieces, rank, weight, gain, cos, sin):
    own, width = pieces[0].shape
    size = (len(pieces) + 1) // 2
    tokens = own * size
    groups = weight.shape[1] // ((QPK + 2) * HD)

    def rows(wide):
        return pl.BlockSpec((own, wide), lambda i, r: (i, 0))

    def whole(shape):
        return pl.BlockSpec(shape, lambda i, r: (0, 0))

    widths = (width, width, groups * QPK * HD, groups * 2 * HD)
    return pl.pallas_call(
        qkv_kernel,
        grid_spec=pltpu.PrefetchScalarGridSpec(
            num_scalar_prefetch=1,
            grid=(size,),
            in_specs=[whole(weight.shape), whole((1, width)), rows(128), rows(128)]
            + [whole((own, width))] * len(pieces),
            out_specs=[rows(wide) for wide in widths],
        ),
        out_shape=[jax.ShapeDtypeStruct((tokens, wide), jnp.bfloat16) for wide in widths],
        compiler_params=pltpu.CompilerParams(vmem_limit_bytes=VMEM_LIMIT),
        cost_estimate=cost(9),
        name="project_qkv",
    )(jnp.reshape(rank, (1,)).astype(jnp.int32), weight, gain[None], cos, sin, *pieces)


def stack_heads(block, low_lanes):
    rows = block.shape[0]
    lane = lax.broadcasted_iota(jnp.int32, (rows, 128), 1)
    keep = (lane < HD) if low_lanes else (lane >= HD)
    stacked = []
    for pair in range(QPK // 2):
        both = block[:, pair * 128 : (pair + 1) * 128].astype(jnp.float32)
        turned = pltpu.roll(both, HD, 1)
        for part in (both, turned) if low_lanes else (turned, both):
            stacked.append(jnp.where(keep, part, 0.0))
    return jnp.concatenate(stacked, axis=0).astype(jnp.bfloat16)


def unstack_heads(stacked, low_lanes):
    rows = stacked.shape[0] // QPK
    lane = lax.broadcasted_iota(jnp.int32, (rows, 128), 1)
    blocks = []
    for pair in range(QPK // 2):
        first = stacked[2 * pair * rows : (2 * pair + 1) * rows]
        second = stacked[(2 * pair + 1) * rows : (2 * pair + 2) * rows]
        if low_lanes:
            second = pltpu.roll(second, HD, 1)
        else:
            first = pltpu.roll(first, HD, 1)
        blocks.append(jnp.where(lane < HD, first, second))
    return blocks


def key_blocks(pos_ref, tile, tq, tk, step, low=0, high=None):
    tokens = pos_ref.shape[0]
    query = tile * tq
    start = REACH * tokens + query
    first = jnp.maximum(start - pos_ref[query], low)
    last_start = start + tq - 1 - pos_ref[query + tq - 1]
    end = (start + tq - 1) // tk + 1
    if high is not None:
        end = jnp.minimum(end, high // tk)

    def body(block, carry):
        key = block * tk
        clear = (key >= last_start) & (key + tk - 1 <= start)

        @pl.when(clear)
        def _():
            step(key, False)

        @pl.when(jnp.logical_not(clear))
        def _():
            step(key, True)

        return carry

    lax.fori_loop(first // tk, end, body, 0)


def allowed_block(key, tile, tokens, tk, tq, back_row):
    key_at = key + lax.broadcasted_iota(jnp.int32, (tk, tq), 0)
    query_at = REACH * tokens + tile * tq + lax.broadcasted_iota(jnp.int32, (tk, tq), 1)
    back = query_at - key_at
    allowed = (back >= 0) & (back <= back_row)
    return jnp.concatenate([allowed] * QPK, axis=1)


def attend_step(key, masked, tile, tk, base, back_ref, kv, vx, qs, acc, top, tokens):
    tq = qs.shape[0] // QPK
    scores = lax.dot_general(
        kv[pl.ds(key - base, tk), :], qs[...], COLS_BY_COLS, preferred_element_type=jnp.float32
    )
    if masked:
        allowed = allowed_block(key, tile, tokens, tk, tq, back_ref[0:1, :])
        scores = jnp.where(allowed, scores, NEG_FILL)
    old = top[0:1, :]
    new = jnp.maximum(old, jnp.max(scores, axis=0, keepdims=True))
    top[0:1, :] = new
    probs = jnp.exp2((scores - new) * EXP_SCALE).astype(jnp.bfloat16)
    fade = jnp.exp2((old - new) * EXP_SCALE)
    acc[...] = acc[...] * fade + lax.dot_general(
        vx[pl.ds(key - base, tk), :], probs, ROWS_BY_ROWS, preferred_element_type=jnp.float32
    )


def load_sources(refs, kv, vx):
    tokens = refs[0].shape[0]
    lane = lax.broadcasted_iota(jnp.int32, (tokens, 2 * HD), 1)
    for i, ref in enumerate(refs):
        kv[pl.ds(i * tokens, tokens), :] = ref[...]
        vx[pl.ds(i * tokens, tokens), :] = jnp.where(lane < HD, jnp.ones_like(ref), ref[...])


def attend_here_kernel(tk, pos_ref, q_ref, back_ref, here, acc_ref, top_ref, vx, qs):
    tokens = here.shape[0]
    tq = q_ref.shape[0]
    tile = pl.program_id(0)
    acc, top = acc_ref.at[0], top_ref.at[0]

    @pl.when(tile == 0)
    def _():
        lane = lax.broadcasted_iota(jnp.int32, (tokens, 2 * HD), 1)
        vx[...] = jnp.where(lane < HD, jnp.ones_like(here), here[...])

    qs[...] = stack_heads(q_ref[...], True)
    acc[...] = jnp.zeros_like(acc)
    top[...] = jnp.full_like(top, NEG_FILL)
    base = REACH * tokens

    def step(key, masked):
        attend_step(key, masked, tile, tk, base, back_ref, here, vx, qs, acc, top, tokens)

    key_blocks(pos_ref, tile, tq, tk, step, low=base)


def attend_far_kernel(
    tk, pos_ref, q_ref, back_ref, far_two, far_one, acc_ref, top_ref,
    out_ref, lse_ref, kv, vx, qs, acc, top
):
    tokens = far_one.shape[0]
    tq = q_ref.shape[0]
    tile = pl.program_id(0)

    @pl.when(tile == 0)
    def _():
        load_sources((far_two, far_one), kv, vx)

    qs[...] = stack_heads(q_ref[...], True)
    acc[...] = acc_ref[0]
    top[...] = top_ref[0]

    def step(key, masked):
        attend_step(key, masked, tile, tk, 0, back_ref, kv, vx, qs, acc, top, tokens)

    key_blocks(pos_ref, tile, tq, tk, step, high=REACH * tokens)
    total = acc[...]
    weight = total[0:1]
    blocks = unstack_heads(jnp.transpose(total / weight), False)
    out_ref[...] = jnp.concatenate(blocks, axis=1).astype(jnp.bfloat16)
    lse = top[0:1, :] * EXP_SCALE + jnp.log2(weight)
    lse_ref[...] = jnp.broadcast_to(lse, (8, lse.shape[1]))[None]


def attend_here(queries, here, positions, back_rows, group, tq, tk):
    tokens = queries.shape[0]
    state = (
        jax.ShapeDtypeStruct((tokens // tq, 2 * HD, QPK * tq), jnp.float32),
        jax.ShapeDtypeStruct((tokens // tq, 8, QPK * tq), jnp.float32),
    )
    return pl.pallas_call(
        functools.partial(attend_here_kernel, tk),
        grid_spec=pltpu.PrefetchScalarGridSpec(
            num_scalar_prefetch=1,
            grid=(tokens // tq,),
            in_specs=[
                pl.BlockSpec((tq, QPK * HD), lambda i, p: (i, group)),
                pl.BlockSpec((8, tq), lambda i, p: (0, i)),
                pl.BlockSpec((tokens, 2 * HD), lambda i, p: (0, group)),
            ],
            out_specs=[pl.BlockSpec((1, *shape.shape[1:]), lambda i, p: (i, 0, 0)) for shape in state],
            scratch_shapes=[
                pltpu.VMEM((tokens, 2 * HD), jnp.bfloat16),
                pltpu.VMEM((QPK * tq, 2 * HD), jnp.bfloat16),
            ],
        ),
        out_shape=state,
        compiler_params=pltpu.CompilerParams(vmem_limit_bytes=VMEM_LIMIT),
        cost_estimate=cost(10),
        name="attend_here",
    )(positions, queries, back_rows, here)


def attend_far(queries, far, state, positions, back_rows, group, tq, tk):
    tokens = queries.shape[0]
    kv_spec = pl.BlockSpec((tokens, 2 * HD), lambda i, p: (0, group))
    return pl.pallas_call(
        functools.partial(attend_far_kernel, tk),
        grid_spec=pltpu.PrefetchScalarGridSpec(
            num_scalar_prefetch=1,
            grid=(tokens // tq,),
            in_specs=[
                pl.BlockSpec((tq, QPK * HD), lambda i, p: (i, group)),
                pl.BlockSpec((8, tq), lambda i, p: (0, i)),
                kv_spec,
                kv_spec,
            ]
            + [pl.BlockSpec((1, *part.shape[1:]), lambda i, p: (i, 0, 0)) for part in state],
            out_specs=[
                pl.BlockSpec((tq, QPK * HD), lambda i, p: (i, 0)),
                pl.BlockSpec((1, 8, QPK * tq), lambda i, p: (i, 0, 0)),
            ],
            scratch_shapes=[
                pltpu.VMEM((REACH * tokens, 2 * HD), jnp.bfloat16),
                pltpu.VMEM((REACH * tokens, 2 * HD), jnp.bfloat16),
                pltpu.VMEM((QPK * tq, 2 * HD), jnp.bfloat16),
                pltpu.VMEM((2 * HD, QPK * tq), jnp.float32),
                pltpu.VMEM((8, QPK * tq), jnp.float32),
            ],
        ),
        out_shape=[
            jax.ShapeDtypeStruct((tokens, QPK * HD), jnp.bfloat16),
            jax.ShapeDtypeStruct((tokens // tq, 8, QPK * tq), jnp.float32),
        ],
        compiler_params=pltpu.CompilerParams(vmem_limit_bytes=VMEM_LIMIT),
        cost_estimate=cost(14),
        name="attend_far",
    )(positions, queries, back_rows, *far, *state)


def attend_back_kernel(
    tk, pos_ref, q_ref, do_ref, o_ref, back_ref, lse_ref, cos_ref, sin_ref, far_two, far_one, here,
    dq_ref, d_far_two, d_far_one, d_here, kv, dkv, qs, dos, dq
):
    tokens = here.shape[0]
    tq = q_ref.shape[0]
    tile = pl.program_id(0)

    @pl.when(tile == 0)
    def _():
        for i, ref in enumerate((far_two, far_one, here)):
            kv[pl.ds(i * tokens, tokens), :] = ref[...]
        dkv[...] = jnp.zeros_like(dkv)

    qs[...] = stack_heads(q_ref[...], True)
    dos[...] = stack_heads(do_ref[...], False)
    dq[...] = jnp.zeros_like(dq)
    product = dos[...].astype(jnp.float32) * stack_heads(o_ref[...], False).astype(jnp.float32)
    delta = jnp.sum(jnp.transpose(product), axis=0, keepdims=True)
    lse = lse_ref[0, 0:1, :]

    def step(key, masked):
        keys = kv[pl.ds(key, tk), :]
        scores = lax.dot_general(keys, qs[...], COLS_BY_COLS, preferred_element_type=jnp.float32)
        probs = jnp.exp2(scores * EXP_SCALE - lse)
        if masked:
            allowed = allowed_block(key, tile, tokens, tk, tq, back_ref[0:1, :])
            probs = jnp.where(allowed, probs, 0.0)
        d_probs = lax.dot_general(keys, dos[...], COLS_BY_COLS, preferred_element_type=jnp.float32)
        d_scores = (probs * (d_probs - delta)).astype(jnp.bfloat16)
        d_keys = jnp.dot(d_scores, qs[...], preferred_element_type=jnp.float32)
        d_values = jnp.dot(probs.astype(jnp.bfloat16), dos[...], preferred_element_type=jnp.float32)
        dkv[pl.ds(key, tk), :] += d_keys * HD**-0.5 + d_values
        dq[...] += lax.dot_general(
            d_scores, keys, ROWS_BY_ROWS, preferred_element_type=jnp.float32
        )

    key_blocks(pos_ref, tile, tq, tk, step)
    cos, sin = cos_ref[...], sin_ref[...]
    blocks = unstack_heads(dq[...] * HD**-0.5, True)
    blocks = [block * cos - turn_halves(block) * sin for block in blocks]
    dq_ref[...] = jnp.concatenate(blocks, axis=1).astype(jnp.bfloat16)

    @pl.when(tile == pl.num_programs(0) - 1)
    def _():
        d_far_two[...] = dkv[pl.ds(0, tokens), :].astype(jnp.bfloat16)
        d_far_one[...] = dkv[pl.ds(tokens, tokens), :].astype(jnp.bfloat16)
        d_here[...] = dkv[pl.ds(2 * tokens, tokens), :]


def attend_back(
    queries, d_attn, attn, lse, sources, positions, back_rows, cos, sin, group, tq, tk
):
    tokens = queries.shape[0]
    kv_spec = pl.BlockSpec((tokens, 2 * HD), lambda i, p: (0, group))
    own_kv = pl.BlockSpec((tokens, 2 * HD), lambda i, p: (0, 0))
    q_spec = pl.BlockSpec((tq, QPK * HD), lambda i, p: (i, group))
    own_q = pl.BlockSpec((tq, QPK * HD), lambda i, p: (i, 0))
    angle_spec = pl.BlockSpec((tq, 128), lambda i, p: (i, 0))
    return pl.pallas_call(
        functools.partial(attend_back_kernel, tk),
        grid_spec=pltpu.PrefetchScalarGridSpec(
            num_scalar_prefetch=1,
            grid=(tokens // tq,),
            in_specs=[
                q_spec,
                q_spec,
                own_q,
                pl.BlockSpec((8, tq), lambda i, p: (0, i)),
                pl.BlockSpec((1, 8, QPK * tq), lambda i, p: (i, 0, 0)),
                angle_spec,
                angle_spec,
                kv_spec,
                kv_spec,
                kv_spec,
            ],
            out_specs=[own_q, own_kv, own_kv, own_kv],
            scratch_shapes=[
                pltpu.VMEM(((REACH + 1) * tokens, 2 * HD), jnp.bfloat16),
                pltpu.VMEM(((REACH + 1) * tokens, 2 * HD), jnp.float32),
                pltpu.VMEM((QPK * tq, 2 * HD), jnp.bfloat16),
                pltpu.VMEM((QPK * tq, 2 * HD), jnp.bfloat16),
                pltpu.VMEM((QPK * tq, 2 * HD), jnp.float32),
            ],
        ),
        out_shape=[
            jax.ShapeDtypeStruct((tokens, QPK * HD), jnp.bfloat16),
            jax.ShapeDtypeStruct((tokens, 2 * HD), jnp.bfloat16),
            jax.ShapeDtypeStruct((tokens, 2 * HD), jnp.bfloat16),
            jax.ShapeDtypeStruct((tokens, 2 * HD), jnp.float32),
        ],
        compiler_params=pltpu.CompilerParams(vmem_limit_bytes=VMEM_LIMIT),
        cost_estimate=cost(28),
        name="attend_back",
    )(positions, queries, d_attn, attn, back_rows, lse, cos, sin, *sources)


def mix_kernel(groups, cos_ref, sin_ref, *refs):
    out_ref = refs[-1]
    cos, sin = cos_ref[...], sin_ref[...]
    key_lane = lax.broadcasted_iota(jnp.int32, cos.shape, 1) < HD
    for group in range(groups):
        dq_ref, here, from_one, from_two = refs[4 * group : 4 * group + 4]
        base = group * (QPK + 2) * HD
        out_ref[:, base : base + QPK * HD] = dq_ref[...]
        total = here[...] + from_one[...].astype(jnp.float32) + from_two[...].astype(jnp.float32)
        turned = total * cos - turn_halves(total) * sin
        out_ref[:, base + QPK * HD : base + (QPK + 2) * HD] = jnp.where(
            key_lane, turned, total
        ).astype(jnp.bfloat16)


def mix_grads(parts, cos, sin, tile):
    tokens = cos.shape[0]
    groups = len(parts)

    def rows(wide):
        return pl.BlockSpec((tile, wide), lambda i: (i, 0))

    flat = [array for part in parts for array in part]
    return pl.pallas_call(
        functools.partial(mix_kernel, groups),
        grid=(tokens // tile,),
        in_specs=[rows(128), rows(128)] + [rows(array.shape[1]) for array in flat],
        out_specs=rows(groups * (QPK + 2) * HD),
        out_shape=jax.ShapeDtypeStruct((tokens, groups * (QPK + 2) * HD), jnp.bfloat16),
        compiler_params=pltpu.CompilerParams(vmem_limit_bytes=VMEM_LIMIT),
        cost_estimate=cost(3),
        name="mix_grads",
    )(cos, sin, *flat)


def out_step_kernel(distances, last, rank_ref, *refs):
    refs = list(refs)
    base_ref = refs.pop(0)
    gain_ref = refs.pop(0) if last else None
    total = base_ref[...].astype(jnp.float32)
    for distance, count in distances:
        piece = refs.pop(0)[...]
        if count == 2:
            piece = jnp.where(rank_ref[0] >= distance, piece, refs.pop(0)[...])
        total = total + jnp.dot(piece, refs.pop(0)[...], preferred_element_type=jnp.float32)
    if not last:
        refs[0][...] = total
    else:

        @pl.when(pl.program_id(0) == rank_ref[0])
        def _():
            refs[0][...] = total

        inverse = lax.rsqrt(jnp.mean(total * total, axis=1, keepdims=True) + NORM_EPS)
        refs[1][...] = (total * inverse * gain_ref[...]).astype(jnp.bfloat16)


def out_step(base, pieces, rank, weight, tile, gain=None):
    tokens, width = base.shape
    depth = pieces[0][1][0].shape[1]
    last = gain is not None
    slots = weight.shape[0] // depth

    def rows(wide):
        return pl.BlockSpec((tile, wide), lambda i, r: (i, 0))

    def slot_rows(distance, count):
        def index(i, r):
            slot = r[0] - distance
            if count == 2:
                slot = jnp.where(r[0] >= distance, slot, r[0] + distance)
            return jnp.clip(slot, 0, slots - 1), 0

        return pl.BlockSpec((depth, width), index)

    operands, specs = [base], [rows(width)]
    if last:
        operands.append(gain[None])
        specs.append(pl.BlockSpec((1, width), lambda i, r: (0, 0)))
    for distance, blocks in pieces:
        operands += [*blocks, weight]
        specs += [rows(depth)] * len(blocks) + [slot_rows(distance, len(blocks))]
    outs = [jax.ShapeDtypeStruct((tile if last else tokens, width), jnp.float32)]
    out_specs = [pl.BlockSpec((tile, width), lambda i, r: (0, 0)) if last else rows(width)]
    if last:
        outs.append(jax.ShapeDtypeStruct((tokens, width), jnp.bfloat16))
        out_specs.append(rows(width))
    distances = tuple((distance, len(blocks)) for distance, blocks in pieces)
    made = pl.pallas_call(
        functools.partial(out_step_kernel, distances, last),
        grid_spec=pltpu.PrefetchScalarGridSpec(
            num_scalar_prefetch=1,
            grid=(tokens // tile,),
            in_specs=specs,
            out_specs=out_specs,
        ),
        out_shape=outs,
        compiler_params=pltpu.CompilerParams(vmem_limit_bytes=VMEM_LIMIT),
        cost_estimate=cost(7),
        name="out_step",
    )(jnp.reshape(rank, (1,)).astype(jnp.int32), *operands)
    return made if last else made[0]


def own_kernel(rank_ref, *refs):
    *pieces, out_ref = refs

    def put(piece):
        out_ref[...] = piece[...]

    pick_piece(pieces, rank_ref[0] - pl.program_id(0), put)


def own_rows_of_heads(pieces, rank, own):
    size = (len(pieces) + 1) // 2
    columns = pieces[0].shape[1]
    return pl.pallas_call(
        own_kernel,
        grid_spec=pltpu.PrefetchScalarGridSpec(
            num_scalar_prefetch=1,
            grid=(size,),
            in_specs=[pl.BlockSpec((own, columns), lambda i, r: (r[0], 0))] * len(pieces),
            out_specs=pl.BlockSpec((own, columns), lambda i, r: (0, i)),
        ),
        out_shape=jax.ShapeDtypeStruct((own, columns * size), pieces[0].dtype),
        compiler_params=pltpu.CompilerParams(vmem_limit_bytes=VMEM_LIMIT),
        cost_estimate=cost(2),
        name="own_rows_of_heads",
    )(jnp.reshape(rank, (1,)).astype(jnp.int32), *pieces)


def gate_kernel(n_ref, w_ref, dh_ref, hidden_ref, dgu_ref):
    wide = dh_ref.shape[1]
    both = jnp.dot(n_ref[...], w_ref[...], preferred_element_type=jnp.float32)
    gate, up = both[:, :wide], both[:, wide:]
    sigmoid = jax.nn.sigmoid(gate)
    silu = gate * sigmoid
    d_hidden = dh_ref[...].astype(jnp.float32)
    hidden_ref[...] = (silu * up).astype(jnp.bfloat16)
    d_gate = d_hidden * up * (sigmoid + silu * (1.0 - sigmoid))
    dgu_ref[...] = jnp.concatenate([d_gate, d_hidden * silu], axis=1).astype(jnp.bfloat16)


def gate_and_back(normed, weight, d_hidden, tile, wide):
    tokens, width = normed.shape
    units = d_hidden.shape[1]
    cell = pl.BlockSpec((tile, wide), lambda j, i: (i, j))
    pair_cell = pl.BlockSpec((tile, 2 * wide), lambda j, i: (i, j))
    return pl.pallas_call(
        gate_kernel,
        grid=(units // wide, tokens // tile),
        in_specs=[
            pl.BlockSpec((tile, width), lambda j, i: (i, 0)),
            pl.BlockSpec((width, 2 * wide), lambda j, i: (0, j)),
            cell,
        ],
        out_specs=[cell, pair_cell],
        out_shape=[
            jax.ShapeDtypeStruct((tokens, units), jnp.bfloat16),
            jax.ShapeDtypeStruct((tokens, 2 * units), jnp.bfloat16),
        ],
        compiler_params=pltpu.CompilerParams(vmem_limit_bytes=VMEM_LIMIT),
        cost_estimate=cost(27),
        name="gate_and_back",
    )(normed, weight, d_hidden)


def blocks_kernel(chunks_ref, *refs):
    count = (len(refs) - 1) // 2
    left = jnp.concatenate([ref[...] for ref in refs[:count]], axis=0)
    product = lax.dot_general(
        left, refs[count][...], COLS_BY_COLS, preferred_element_type=jnp.float32
    ).astype(jnp.bfloat16)
    rows = refs[0].shape[0]
    for i, out_ref in enumerate(refs[count + 1 :]):
        out_ref[...] = product[i * rows : (i + 1) * rows]


def blocks_times(left, right, chunks, rows, wide, micros):
    depth = left.shape[1]
    count = chunks.shape[0]

    def block_spec(i):
        return pl.BlockSpec((rows, depth), lambda j, c: (c[i], 0))

    return pl.pallas_call(
        blocks_kernel,
        grid_spec=pltpu.PrefetchScalarGridSpec(
            num_scalar_prefetch=1,
            grid=(right.shape[0] // wide,),
            in_specs=[block_spec(i) for i in range(count)]
            + [pl.BlockSpec((wide, depth), lambda j, c: (j, 0))],
            out_specs=[pl.BlockSpec((rows, wide), lambda j, c: (0, j))] * count,
        ),
        out_shape=[jax.ShapeDtypeStruct((rows, right.shape[0]), jnp.bfloat16)] * count,
        compiler_params=pltpu.CompilerParams(vmem_limit_bytes=VMEM_LIMIT),
        cost_estimate=cost(micros),
        name="blocks_times",
    )(chunks, *[left] * count, right)


def gain_kernel(part_ref, w_ref, out_ref):
    product = part_ref[...].astype(jnp.float32) * w_ref[...].astype(jnp.float32)
    ones = jnp.ones((8, product.shape[1]), jnp.float32)
    out_ref[...] = lax.dot_general(
        ones, product, COLS_BY_COLS, precision=lax.Precision.HIGHEST,
        preferred_element_type=jnp.float32,
    )


def row_products(part, weight, tile):
    rows, columns = part.shape
    cell = pl.BlockSpec((tile, columns), lambda i: (i, 0))
    sums = pl.pallas_call(
        gain_kernel,
        grid=(rows // tile,),
        in_specs=[cell, cell],
        out_specs=pl.BlockSpec((8, tile), lambda i: (0, i)),
        out_shape=jax.ShapeDtypeStruct((8, rows), jnp.float32),
        compiler_params=pltpu.CompilerParams(vmem_limit_bytes=VMEM_LIMIT),
        cost_estimate=cost(4),
        name="row_products",
    )(part, weight)
    return sums[0]


def norm_back_rows(vector, grad_in, gain):
    inverse = lax.rsqrt(jnp.mean(vector * vector, axis=1, keepdims=True) + NORM_EPS)
    scaled = grad_in * gain
    mean = jnp.mean(vector * scaled, axis=1, keepdims=True)
    grad = inverse * scaled - vector * (inverse * inverse * inverse * mean)
    return grad, jnp.sum(grad_in * vector * inverse, axis=0, keepdims=True)


def sum_refs(refs):
    total = refs[0][...].astype(jnp.float32)
    for ref in refs[1:]:
        total = total + ref[...].astype(jnp.float32)
    return total


def mid_kernel(mid_ref, dy_ref, gain_ref, *refs):
    *parts, d_mid_ref, branch_ref, gain_grad_ref = refs
    grad, gain_grad = norm_back_rows(mid_ref[...], sum_refs(parts), gain_ref[...])
    d_mid = dy_ref[...].astype(jnp.float32) + grad
    d_mid_ref[...] = d_mid
    branch_ref[...] = d_mid.astype(jnp.bfloat16)
    gain_grad = jnp.broadcast_to(gain_grad, gain_grad_ref.shape)

    @pl.when(pl.program_id(0) == 0)
    def _():
        gain_grad_ref[...] = gain_grad

    @pl.when(pl.program_id(0) > 0)
    def _():
        gain_grad_ref[...] += gain_grad


def back_to_mid(parts, mid, output_grad, gain):
    own, width = output_grad.shape
    tile = min(64, own)
    rows = pl.BlockSpec((tile, width), lambda i: (i, 0))
    outs = pl.pallas_call(
        mid_kernel,
        grid=(own // tile,),
        in_specs=[rows, rows, pl.BlockSpec((1, width), lambda i: (0, 0))] + [rows] * len(parts),
        out_specs=[rows, rows, pl.BlockSpec((8, width), lambda i: (0, 0))],
        out_shape=[
            jax.ShapeDtypeStruct((own, width), jnp.float32),
            jax.ShapeDtypeStruct((own, width), jnp.bfloat16),
            jax.ShapeDtypeStruct((8, width), jnp.float32),
        ],
        compiler_params=pltpu.CompilerParams(vmem_limit_bytes=VMEM_LIMIT),
        cost_estimate=cost(4),
        name="back_to_mid",
    )(mid, output_grad, gain[None], *parts)
    return outs[0], outs[1], outs[2][0]


def input_kernel(x_ref, d_mid_ref, gain_ref, *refs):
    *parts, out_ref = refs
    x = x_ref[...].astype(jnp.float32)
    grad, _ = norm_back_rows(x, sum_refs(parts), gain_ref[...])
    out_ref[...] = d_mid_ref[...] + grad


def back_to_input(parts, layer_input, d_mid, gain):
    own, width = layer_input.shape
    tile = min(64, own)
    rows = pl.BlockSpec((tile, width), lambda i: (i, 0))
    return pl.pallas_call(
        input_kernel,
        grid=(own // tile,),
        in_specs=[rows, rows, pl.BlockSpec((1, width), lambda i: (0, 0))] + [rows] * len(parts),
        out_specs=rows,
        out_shape=jax.ShapeDtypeStruct((own, width), jnp.float32),
        compiler_params=pltpu.CompilerParams(vmem_limit_bytes=VMEM_LIMIT),
        cost_estimate=cost(4),
        name="back_to_input",
    )(layer_input, d_mid, gain[None], *parts)


def round_kernel(w_ref, out_ref):
    out_ref[...] = w_ref[0].astype(jnp.bfloat16)


def round_interleaved(weight, wide):
    _, rows, units = weight.shape
    return pl.pallas_call(
        round_kernel,
        grid=(units // wide, 2),
        in_specs=[pl.BlockSpec((1, rows, wide), lambda j, k: (k, 0, j))],
        out_specs=pl.BlockSpec((rows, wide), lambda j, k: (0, 2 * j + k)),
        out_shape=jax.ShapeDtypeStruct((rows, 2 * units), jnp.bfloat16),
        cost_estimate=cost(6),
        name="round_interleaved",
    )(weight)


def adam_kernel(g_ref, w_ref, m_ref, s_ref, grad_ref, w_out, m_out, s_out, copy_out):
    grad = g_ref[...].astype(jnp.float32)
    new, moment, square, _ = adam_step(w_ref[0], grad, m_ref[0], s_ref[0])
    grad_ref[0] = grad
    w_out[0] = new
    m_out[0] = moment
    s_out[0] = square
    copy_out[0] = new.astype(jnp.bfloat16)


def adam_interleaved(grad, weight, moment, square, wide):
    _, rows, units = weight.shape
    cell = pl.BlockSpec((1, rows, wide), lambda j, k: (k, 0, j))
    shape = jax.ShapeDtypeStruct(weight.shape, jnp.float32)
    return pl.pallas_call(
        adam_kernel,
        grid=(units // wide, 2),
        in_specs=[pl.BlockSpec((rows, wide), lambda j, k: (0, 2 * j + k)), cell, cell, cell],
        out_specs=[cell] * 5,
        out_shape=[shape] * 4 + [jax.ShapeDtypeStruct(weight.shape, jnp.bfloat16)],
        compiler_params=pltpu.CompilerParams(vmem_limit_bytes=VMEM_LIMIT),
        cost_estimate=cost(13),
        name="adam_interleaved",
    )(grad, weight, moment, square)


def angle_tables(positions):
    half_size = HD // 2
    freq = ROPE_BASE ** (-(jnp.arange(half_size).astype(jnp.float32) * 2.0 / HD))
    angle = positions.astype(jnp.float32)[:, None] * freq[None, :]
    cos, sin = jnp.cos(angle), jnp.sin(angle)
    return jnp.concatenate([cos] * 4, axis=1), jnp.concatenate([-sin, sin] * 2, axis=1)


def adam_step(weight_old, grad_new, moment_one, moment_two):
    moment_next = BETA * moment_one + (1.0 - BETA) * grad_new
    square_next = BETA * moment_two + (1.0 - BETA) * grad_new * grad_new
    change = -RATE * (moment_next / (jnp.sqrt(square_next) + ADAM_EPS) + DECAY * weight_old)
    return (weight_old + change, moment_next, square_next, change)


def local(
    layer_input,
    output_grad,
    segment_ids,
    positions,
    qkv_weight,
    qkv_moment,
    qkv_square,
    out_weight,
    out_moment,
    out_square,
    gate_up_weight,
    gate_up_moment,
    gate_up_square,
    down_weight,
    down_moment,
    down_square,
    norm_gains,
    gains_moment,
    gains_square,
):
    low = low_type = jnp.bfloat16
    full = jnp.float32
    own, width = layer_input.shape
    tokens = positions.shape[0]
    rank = lax.axis_index("tp")
    units = down_weight.shape[0]
    groups = qkv_weight.shape[1] // ((QPK + 2) * HD)
    head_columns = groups * QPK * HD
    tile = min(256, own)
    gain_one = norm_gains[0]
    gain_two = norm_gains[1]

    wide = min(512, units)

    close = lax.optimization_barrier

    w_qkv = lax.all_gather(qkv_weight.astype(low), "seq", axis=0, tiled=True)
    side = (gate_up_weight, down_weight, out_weight, positions)
    x_line = LineGather(layer_input, "tp")
    for index in range(x_line.hops):
        x_line.hop()
        if index == 1:
            held_gate_up, held_down, held_out, held_positions = side
            w_gate_up = lax.all_gather(
                round_interleaved(held_gate_up, wide), "seq", axis=0, tiled=True
            )
            cos, sin = angle_tables(held_positions)
            back_rows = jnp.broadcast_to(held_positions[None, :], (8, tokens))
            side = (held_down.astype(low), held_out.astype(low), cos, sin, back_rows)
        x_line.moving, side = close((x_line.moving, side))
    pieces, side, w_qkv, output_grad = close((x_line.pieces, side, w_qkv, output_grad))
    low_down, low_out, cos, sin, back_rows = side

    dy_line = LineGather(output_grad, "tp")
    dy_line.hop()
    made = project_qkv(pieces, rank, w_qkv, gain_one, cos, sin)
    made, dy_line.moving, low_out, low_down = close((made, dy_line.moving, low_out, low_down))
    x_rows, normed_one, queries, kv = made
    w_down = lax.all_gather(low_down, "seq", axis=1, tiled=True)
    out_strip = swap_gather(low_out, "tp")
    far = [along_sequence(kv, distance, tokens) for distance in (2, 1)]
    if dy_line.hops > 1:
        dy_line.hop()
    states = [
        attend_here(queries, kv, positions, back_rows, group, 256, 512) for group in range(groups)
    ]
    far, states, queries, w_gate_up, dy_line.moving = close(
        (far, states, queries, w_gate_up, dy_line.moving)
    )
    for _ in range(2, dy_line.hops):
        dy_line.hop()
    attn, lse = [], []
    for group in range(groups):
        out, log_total = attend_far(
            queries, far, states[group], positions, back_rows, group, 256, 512
        )
        attn.append(out)
        lse.append(log_total)
    attn, lse, dy_pieces, w_down, x_rows, out_strip = close(
        (attn, lse, dy_line.pieces, w_down, x_rows, out_strip)
    )
    w_out = lax.all_gather(out_strip.reshape(-1, low_out.shape[1]), "seq", axis=1, tiled=True)

    heads_line = LineGather(jnp.concatenate(attn, axis=1), "tp")
    arrived = [(0, [heads_line.from_low[0]])]
    total = x_rows
    for index in range(heads_line.hops):
        heads_line.hop()
        if index == 0:
            grad_rows = place_rows(dy_pieces, rank)
            d_hidden = contract_cols(grad_rows, w_down).astype(low)
            heads_line.moving, grad_rows, d_hidden, total = close(
                (heads_line.moving, grad_rows, d_hidden, total)
            )
        elif index < heads_line.hops - 1:
            heads_line.moving, w_out = close((heads_line.moving, w_out))
        else:
            total = out_step(total, arrived, rank, w_out, own)
            heads_line.moving, total = close((heads_line.moving, total))
            arrived = []
        below, above = heads_line.moving
        step = heads_line.step
        if 2 * step > heads_line.hops:
            arrived.append((step, [below, above]))
        else:
            arrived += [(step, [below]), (-step, [above])]

    mid, normed_two = out_step(total, arrived, rank, w_out, own, gain_two)
    mid, normed_two, w_gate_up, d_hidden = close((mid, normed_two, w_gate_up, d_hidden))
    hidden, d_gate_up = close(gate_and_back(normed_two, w_gate_up, d_hidden, 1024, wide))
    down_grad = contract_rows(hidden, grad_rows).astype(low)
    down_grad, hidden, d_gate_up, normed_two, grad_rows = close(
        (down_grad, hidden, d_gate_up, normed_two, grad_rows)
    )
    down_grad = lax.psum_scatter(down_grad, "seq", scatter_dimension=1, tiled=True)
    peers = peers_of("tp")
    first = blocks_times(d_gate_up, w_gate_up, peers[:1], own, 512, 9)
    first, side = close((first, (hidden, d_gate_up, normed_two, grad_rows)))
    back_line = LineScatter(first, "tp")
    for index in range(back_line.hops):
        back_line.hop()
        hidden, d_gate_up, normed_two, grad_rows = side
        if index == 0:
            second = blocks_times(d_gate_up, w_gate_up, peers[1:], own, 256, 22)
            back_line.moving, side, second = close((back_line.moving, side, second))
            back_line.made += second
        elif index == 1:
            gate_up_grad = contract_rows(normed_two, d_gate_up).astype(low)
            back_line.moving, side, gate_up_grad = close((back_line.moving, side, gate_up_grad))
            gate_up_grad = lax.psum_scatter(gate_up_grad, "seq", scatter_dimension=0, tiled=True)
        elif index == 2:
            partial_out = jnp.dot(hidden, w_down, preferred_element_type=full).astype(low)
            back_line.moving, side, partial_out = close((back_line.moving, side, partial_out))
        else:
            back_line.moving, side = close((back_line.moving, side))
    d_mid, d_branch, gain_two_grad = back_to_mid(back_line.parts, mid, output_grad, gain_two)

    d_attn = contract_cols(d_branch, w_out).astype(low)
    d_attn, d_branch, d_mid, mid, gain_two_grad, partial_out = close(
        (d_attn, d_branch, d_mid, mid, gain_two_grad, partial_out)
    )
    d_attn = lax.all_to_all(d_attn, "tp", split_axis=1, concat_axis=0, tiled=True)
    own_heads = own_rows_of_heads(heads_line.pieces, rank, own)
    out_grad = contract_rows(own_heads, d_branch).astype(low)
    d_attn, out_grad, partial_out, down_grad = close((d_attn, out_grad, partial_out, down_grad))
    out_grad = lax.psum_scatter(out_grad, "seq", scatter_dimension=1, tiled=True)
    result = swap_scatter_parts(partial_out, "tp")
    grads = []
    travelled = []
    for group in range(groups):
        made = attend_back(
            queries, d_attn, attn[group], lse[group], [*far, kv], positions, back_rows,
            cos, sin, group, 256, 512,
        )
        made, d_attn, travelled = close((made, d_attn, travelled))
        grads.append(made)
        travelled.append(
            [along_sequence(made[2], -1, tokens), along_sequence(made[1], -2, tokens)]
        )
    down_grad = down_grad.astype(full)
    down_new = adam_step(down_weight, down_grad, down_moment, down_square)
    down_new, grads, travelled, down_grad = close((down_new, grads, travelled, down_grad))
    d_mixed = mix_grads(
        [(made[0], made[3], *moved) for made, moved in zip(grads, travelled, strict=True)],
        cos, sin, tile,
    )
    made = blocks_times(d_mixed, w_qkv, peers[:1], own, 512, 2)
    made, d_mixed, gate_up_grad = close((made, d_mixed, gate_up_grad))
    in_line = LineScatter(made, "tp")
    for index in range(in_line.hops):
        in_line.hop()
        if index == 0:
            made = blocks_times(d_mixed, w_qkv, peers[1:], own, 512, 5)
            qkv_grad = contract_rows(normed_one, d_mixed).astype(low)
            gain_one_grad = row_products(qkv_grad, w_qkv, min(512, width)) / gain_one
            gains_grad = jnp.stack([gain_one_grad, gain_two_grad])
            in_line.moving, qkv_grad, gains_grad, result, made = close(
                (in_line.moving, qkv_grad, gains_grad, result, made)
            )
            in_line.made += made
            qkv_grad = lax.psum_scatter(qkv_grad, "seq", scatter_dimension=0, tiled=True)
        elif index == 1:
            gate_up_new = adam_interleaved(
                gate_up_grad, gate_up_weight, gate_up_moment, gate_up_square, wide
            )
            gains_grad = sum_by_swaps(gains_grad, "seq")
            in_line.moving, gate_up_new, gains_grad, out_grad = close(
                (in_line.moving, gate_up_new, gains_grad, out_grad)
            )
            out_parts = swap_scatter_parts(out_grad, "tp")
        elif index == 2:
            gains_grad = sum_at_once(gains_grad, "tp")
            outputs = (mid + sum_parts(result)).astype(low)
            qkv_grad = qkv_grad.astype(full)
            qkv_new = adam_step(qkv_weight, qkv_grad, qkv_moment, qkv_square)
            in_line.moving, gains_grad, out_parts, outputs, qkv_grad, qkv_new = close(
                (in_line.moving, gains_grad, out_parts, outputs, qkv_grad, qkv_new)
            )
        else:
            in_line.moving = close(in_line.moving)
    input_grad = back_to_input(in_line.parts, layer_input, d_mid, gain_one)
    out_grad = sum_parts(out_parts)
    out_new = adam_step(out_weight, out_grad, out_moment, out_square)

    out_grad = out_grad.astype(full)
    gains_new = adam_step(norm_gains, gains_grad, gains_moment, gains_square)
    return (
        outputs,
        input_grad,
        qkv_grad,
        qkv_new[0],
        qkv_new[1],
        qkv_new[2],
        qkv_new[0].astype(low),
        out_grad,
        out_new[3],
        out_new[1],
        out_new[2],
        *gate_up_new,
        down_grad,
        down_new[0],
        down_new[1],
        down_new[2],
        down_new[0].astype(low),
        gains_grad,
        gains_new[3],
        gains_new[1],
        gains_new[2],
    )


def solution(mesh):
    tokens = P(("seq", "tp"), None)
    rows = P("seq", "tp")
    columns = P("tp", "seq")
    pair = P(None, "seq", "tp")
    return jax.shard_map(
        local,
        mesh=mesh,
        in_specs=(
            (tokens,) * 2 + (P("seq"),) * 2 + (rows,) * 3 + (columns,) * 3 + (pair,) * 3
            + (columns,) * 3 + (P(),) * 3
        ),
        out_specs=(
            (tokens,) * 2 + (rows,) * 5 + (columns,) * 4 + (pair,) * 5 + (columns,) * 5 + (P(),) * 4
        ),
        check_vma=False,
    )
```

```python
import functools

import jax
import jax.numpy as jnp
from jax import lax
from jax.experimental import pallas as pl
from jax.experimental.pallas import tpu as pltpu
from jax.sharding import PartitionSpec as P

HD = 64
QPK = 4
REACH = 2
SEQLEN = 4096

NORM_EPS = 1e-05
ROPE_BASE = 500000.0
BETA = 0.5
RATE = 0.02
DECAY = 0.1
ADAM_EPS = 1e-08
NEG_FILL = -1e30
LOG2E = 1.4426950408889634
EXP_SCALE = HD**-0.5 * LOG2E
VMEM_LIMIT = 48 * 2**20

ROWS_BY_ROWS = (((0,), (0,)), ((), ()))
COLS_BY_COLS = (((1,), (1,)), ((), ()))


def cost(micros):
    return pl.CostEstimate(
        flops=int(micros * 1.15e9), transcendentals=0, bytes_accessed=int(micros * 3.0e6)
    )


def after(block, *others):
    return lax.optimization_barrier((block, *others))[0]


def contract_rows(left, right):
    return lax.dot_general(left, right, ROWS_BY_ROWS, preferred_element_type=jnp.float32)


def contract_cols(left, right):
    return lax.dot_general(left, right, COLS_BY_COLS, preferred_element_type=jnp.float32)


class LineGather:
    def __init__(self, block, axis):
        self.axis = axis
        self.hops = lax.axis_size(axis) - 1
        self.from_low = [block]
        self.from_high = [block]

    @property
    def step(self):
        return len(self.from_low) - 1

    def hop(self):
        size, passed = self.hops + 1, self.step
        up = [(i, i + 1) for i in range(passed, size - 1)]
        down = [(i, i - 1) for i in range(1, size - passed)]
        self.from_low.append(lax.ppermute(self.from_low[-1], self.axis, up))
        self.from_high.append(lax.ppermute(self.from_high[-1], self.axis, down))

    @property
    def moving(self):
        return self.from_low[-1], self.from_high[-1]

    @moving.setter
    def moving(self, pair):
        self.from_low[-1], self.from_high[-1] = pair

    @property
    def pieces(self):
        return [*self.from_low, *self.from_high[1:]]


def send_order(size):
    return [sorted(range(size), key=lambda peer: (-abs(peer - me), peer)) for me in range(size)]


def peers_of(axis):
    size = lax.axis_size(axis)
    return jnp.array(send_order(size), jnp.int32)[lax.axis_index(axis)]


class LineScatter:
    def __init__(self, made, axis):
        self.axis = axis
        self.hops = lax.axis_size(axis) - 1
        self.made = list(made)
        self.step = 0
        self.moving = None

    def addend(self, distance):
        order = send_order(self.hops + 1)
        slots = [
            order[me].index(me + distance) if 0 <= me + distance <= self.hops else None
            for me in range(self.hops + 1)
        ]
        choices = sorted(set(slots) - {None})
        table = jnp.array([choices[0] if slot is None else slot for slot in slots], jnp.int32)
        block = self.made[choices[0]]
        for choice in choices[1:]:
            chosen = table[lax.axis_index(self.axis)] == choice
            block = jnp.where(chosen, self.made[choice], block)
        return block

    def hop(self):
        self.step += 1
        size, step = self.hops + 1, self.step
        to_high = self.addend(size - step)
        to_low = self.addend(step - size)
        if step > 1:
            to_high = to_high + self.moving[0]
            to_low = to_low + self.moving[1]
        self.moving = (
            lax.ppermute(to_high, self.axis, [(i, i + 1) for i in range(step)]),
            lax.ppermute(to_low, self.axis, [(i, i - 1) for i in range(size - step, size)]),
        )

    @property
    def parts(self):
        return [self.made[-1], *self.moving]


def swap_gather(block, axis):
    copies = jnp.broadcast_to(block[None], (lax.axis_size(axis), *block.shape))
    return lax.all_to_all(copies, axis, split_axis=0, concat_axis=0, tiled=True)


def swap_scatter_parts(block, axis):
    size = lax.axis_size(axis)
    parts = block.reshape(size, block.shape[0] // size, block.shape[1])
    return lax.all_to_all(parts, axis, split_axis=0, concat_axis=0, tiled=True)


def sum_parts(parts):
    return jnp.sum(parts.astype(jnp.float32), axis=0)


def sum_by_swaps(block, axis):
    size = lax.axis_size(axis)
    hop = 1
    while hop < size:
        block = block + lax.ppermute(block, axis, [(i, i ^ hop) for i in range(size)])
        hop *= 2
    return block


def sum_at_once(block, axis):
    size = lax.axis_size(axis)
    came = [block]
    for distance in range(1, size):
        route = [(i, (i + distance) % size) for i in range(size)]
        came.append(lax.ppermute(block, axis, route))
    came = jnp.stack(came)
    rank = lax.axis_index(axis)
    total = lax.dynamic_index_in_dim(came, rank, keepdims=False)
    for peer in range(1, size):
        total = total + lax.dynamic_index_in_dim(came, (rank - peer) % size, keepdims=False)
    return total


def along_sequence(block, distance, tokens):
    shards = SEQLEN // tokens
    route = [
        (i, i + distance)
        for i in range(lax.axis_size("seq"))
        if 0 <= i + distance < lax.axis_size("seq") and i // shards == (i + distance) // shards
    ]
    return lax.ppermute(block, "seq", route)


def turn_halves(block):
    lane = lax.broadcasted_iota(jnp.int32, block.shape, 1)
    return jnp.where(lane % HD < HD // 2, pltpu.roll(block, 96, 1), pltpu.roll(block, 32, 1))


def pick_piece(pieces, below, put):
    size = (len(pieces) + 1) // 2
    for distance in range(1 - size, size):
        piece = pieces[distance if distance >= 0 else size - 1 - distance]
        pl.when(below == distance)(functools.partial(put, piece))


def place_kernel(rank_ref, *refs):
    *pieces, out_ref = refs

    def put(piece):
        out_ref[...] = piece[...]

    pick_piece(pieces, rank_ref[0] - pl.program_id(0), put)


def place_rows(pieces, rank):
    own, width = pieces[0].shape
    size = (len(pieces) + 1) // 2
    return pl.pallas_call(
        place_kernel,
        grid_spec=pltpu.PrefetchScalarGridSpec(
            num_scalar_prefetch=1,
            grid=(size,),
            in_specs=[pl.BlockSpec((own, width), lambda i, r: (0, 0))] * len(pieces),
            out_specs=pl.BlockSpec((own, width), lambda i, r: (i, 0)),
        ),
        out_shape=jax.ShapeDtypeStruct((own * size, width), pieces[0].dtype),
        compiler_params=pltpu.CompilerParams(vmem_limit_bytes=VMEM_LIMIT),
        cost_estimate=cost(4),
        name="place_rows",
    )(jnp.reshape(rank, (1,)).astype(jnp.int32), *pieces)


def qkv_kernel(rank_ref, w_ref, gain_ref, cos_ref, sin_ref, *refs):
    x_ref, normed_ref, q_ref, kv_ref = refs[-4:]

    def put(piece):
        x_ref[...] = piece[...]

    pick_piece(refs[:-4], rank_ref[0] - pl.program_id(0), put)
    x = x_ref[...].astype(jnp.float32)
    inverse = lax.rsqrt(jnp.mean(x * x, axis=1, keepdims=True) + NORM_EPS)
    normed = (x * inverse * gain_ref[...]).astype(jnp.bfloat16)
    normed_ref[...] = normed
    mixed = jnp.dot(normed, w_ref[...], preferred_element_type=jnp.float32)
    cos, sin = cos_ref[...], sin_ref[...]
    key_lane = lax.broadcasted_iota(jnp.int32, cos.shape, 1) < HD
    for group in range(mixed.shape[1] // ((QPK + 2) * HD)):
        base = group * (QPK + 2) * HD
        for pair in range(QPK // 2):
            part = mixed[:, base + pair * 128 : base + (pair + 1) * 128]
            part = part * cos + turn_halves(part) * sin
            q_ref[:, group * QPK * HD + pair * 128 : group * QPK * HD + (pair + 1) * 128] = (
                part.astype(jnp.bfloat16)
            )
        part = mixed[:, base + QPK * HD : base + (QPK + 2) * HD]
        part = jnp.where(key_lane, part * cos + turn_halves(part) * sin, part)
        kv_ref[:, group * 128 : (group + 1) * 128] = part.astype(jnp.bfloat16)


def project_qkv(pieces, rank, weight, gain, cos, sin):
    own, width = pieces[0].shape
    size = (len(pieces) + 1) // 2
    tokens = own * size
    groups = weight.shape[1] // ((QPK + 2) * HD)

    def rows(wide):
        return pl.BlockSpec((own, wide), lambda i, r: (i, 0))

    def whole(shape):
        return pl.BlockSpec(shape, lambda i, r: (0, 0))

    widths = (width, width, groups * QPK * HD, groups * 2 * HD)
    return pl.pallas_call(
        qkv_kernel,
        grid_spec=pltpu.PrefetchScalarGridSpec(
            num_scalar_prefetch=1,
            grid=(size,),
            in_specs=[whole(weight.shape), whole((1, width)), rows(128), rows(128)]
            + [whole((own, width))] * len(pieces),
            out_specs=[rows(wide) for wide in widths],
        ),
        out_shape=[jax.ShapeDtypeStruct((tokens, wide), jnp.bfloat16) for wide in widths],
        compiler_params=pltpu.CompilerParams(vmem_limit_bytes=VMEM_LIMIT),
        cost_estimate=cost(9),
        name="project_qkv",
    )(jnp.reshape(rank, (1,)).astype(jnp.int32), weight, gain[None], cos, sin, *pieces)


def stack_heads(block, low_lanes):
    rows = block.shape[0]
    lane = lax.broadcasted_iota(jnp.int32, (rows, 128), 1)
    keep = (lane < HD) if low_lanes else (lane >= HD)
    stacked = []
    for pair in range(QPK // 2):
        both = block[:, pair * 128 : (pair + 1) * 128].astype(jnp.float32)
        turned = pltpu.roll(both, HD, 1)
        for part in (both, turned) if low_lanes else (turned, both):
            stacked.append(jnp.where(keep, part, 0.0))
    return jnp.concatenate(stacked, axis=0).astype(jnp.bfloat16)


def unstack_heads(stacked, low_lanes):
    rows = stacked.shape[0] // QPK
    lane = lax.broadcasted_iota(jnp.int32, (rows, 128), 1)
    blocks = []
    for pair in range(QPK // 2):
        first = stacked[2 * pair * rows : (2 * pair + 1) * rows]
        second = stacked[(2 * pair + 1) * rows : (2 * pair + 2) * rows]
        if low_lanes:
            second = pltpu.roll(second, HD, 1)
        else:
            first = pltpu.roll(first, HD, 1)
        blocks.append(jnp.where(lane < HD, first, second))
    return blocks


def key_blocks(pos_ref, tile, tq, tk, step, low=0, high=None):
    tokens = pos_ref.shape[0]
    query = tile * tq
    start = REACH * tokens + query
    first = jnp.maximum(start - pos_ref[query], low)
    last_start = start + tq - 1 - pos_ref[query + tq - 1]
    end = (start + tq - 1) // tk + 1
    if high is not None:
        end = jnp.minimum(end, high // tk)

    def body(block, carry):
        key = block * tk
        clear = (key >= last_start) & (key + tk - 1 <= start)

        @pl.when(clear)
        def _():
            step(key, False)

        @pl.when(jnp.logical_not(clear))
        def _():
            step(key, True)

        return carry

    lax.fori_loop(first // tk, end, body, 0)


def allowed_block(key, tile, tokens, tk, tq, back_row):
    key_at = key + lax.broadcasted_iota(jnp.int32, (tk, tq), 0)
    query_at = REACH * tokens + tile * tq + lax.broadcasted_iota(jnp.int32, (tk, tq), 1)
    back = query_at - key_at
    allowed = (back >= 0) & (back <= back_row)
    return jnp.concatenate([allowed] * QPK, axis=1)


def attend_step(key, masked, tile, tk, base, back_ref, kv, vx, qs, acc, top, tokens):
    tq = qs.shape[0] // QPK
    scores = lax.dot_general(
        kv[pl.ds(key - base, tk), :], qs[...], COLS_BY_COLS, preferred_element_type=jnp.float32
    )
    if masked:
        allowed = allowed_block(key, tile, tokens, tk, tq, back_ref[0:1, :])
        scores = jnp.where(allowed, scores, NEG_FILL)
    old = top[0:1, :]
    new = jnp.maximum(old, jnp.max(scores, axis=0, keepdims=True))
    top[0:1, :] = new
    probs = jnp.exp2((scores - new) * EXP_SCALE).astype(jnp.bfloat16)
    fade = jnp.exp2((old - new) * EXP_SCALE)
    acc[...] = acc[...] * fade + lax.dot_general(
        vx[pl.ds(key - base, tk), :], probs, ROWS_BY_ROWS, preferred_element_type=jnp.float32
    )


def load_sources(refs, kv, vx):
    tokens = refs[0].shape[0]
    lane = lax.broadcasted_iota(jnp.int32, (tokens, 2 * HD), 1)
    for i, ref in enumerate(refs):
        kv[pl.ds(i * tokens, tokens), :] = ref[...]
        vx[pl.ds(i * tokens, tokens), :] = jnp.where(lane < HD, jnp.ones_like(ref), ref[...])


def attend_here_kernel(tk, pos_ref, q_ref, back_ref, here, acc_ref, top_ref, vx, qs):
    tokens = here.shape[0]
    tq = q_ref.shape[0]
    tile = pl.program_id(1)
    acc, top = acc_ref.at[0, 0], top_ref.at[0, 0]

    @pl.when(tile == 0)
    def _():
        lane = lax.broadcasted_iota(jnp.int32, (tokens, 2 * HD), 1)
        vx[...] = jnp.where(lane < HD, jnp.ones_like(here), here[...])

    qs[...] = stack_heads(q_ref[...], True)
    acc[...] = jnp.zeros_like(acc)
    top[...] = jnp.full_like(top, NEG_FILL)
    base = REACH * tokens

    def step(key, masked):
        attend_step(key, masked, tile, tk, base, back_ref, here, vx, qs, acc, top, tokens)

    key_blocks(pos_ref, tile, tq, tk, step, low=base)


def attend_far_kernel(
    tk, pos_ref, q_ref, back_ref, far_two, far_one, acc_ref, top_ref,
    out_ref, lse_ref, kv, vx, qs, acc, top
):
    tokens = far_one.shape[0]
    tq = q_ref.shape[0]
    tile = pl.program_id(1)

    @pl.when(tile == 0)
    def _():
        load_sources((far_two, far_one), kv, vx)

    qs[...] = stack_heads(q_ref[...], True)
    acc[...] = acc_ref[0, 0]
    top[...] = top_ref[0, 0]

    def step(key, masked):
        attend_step(key, masked, tile, tk, 0, back_ref, kv, vx, qs, acc, top, tokens)

    key_blocks(pos_ref, tile, tq, tk, step, high=REACH * tokens)
    total = acc[...]
    weight = total[0:1]
    blocks = unstack_heads(jnp.transpose(total / weight), False)
    out_ref[...] = jnp.concatenate(blocks, axis=1).astype(jnp.bfloat16)
    lse = top[0:1, :] * EXP_SCALE + jnp.log2(weight)
    lse_ref[...] = jnp.broadcast_to(lse, (8, lse.shape[1]))[None, None]


def attend_here(queries, here, positions, back_rows, tq, tk):
    tokens = queries.shape[0]
    groups = queries.shape[1] // (QPK * HD)
    state = (
        jax.ShapeDtypeStruct((groups, tokens // tq, 2 * HD, QPK * tq), jnp.float32),
        jax.ShapeDtypeStruct((groups, tokens // tq, 8, QPK * tq), jnp.float32),
    )
    return pl.pallas_call(
        functools.partial(attend_here_kernel, tk),
        grid_spec=pltpu.PrefetchScalarGridSpec(
            num_scalar_prefetch=1,
            grid=(groups, tokens // tq),
            in_specs=[
                pl.BlockSpec((tq, QPK * HD), lambda g, i, p: (i, g)),
                pl.BlockSpec((8, tq), lambda g, i, p: (0, i)),
                pl.BlockSpec((tokens, 2 * HD), lambda g, i, p: (0, g)),
            ],
            out_specs=[
                pl.BlockSpec((1, 1, *shape.shape[2:]), lambda g, i, p: (g, i, 0, 0)) for shape in state
            ],
            scratch_shapes=[
                pltpu.VMEM((tokens, 2 * HD), jnp.bfloat16),
                pltpu.VMEM((QPK * tq, 2 * HD), jnp.bfloat16),
            ],
        ),
        out_shape=state,
        compiler_params=pltpu.CompilerParams(vmem_limit_bytes=VMEM_LIMIT),
        cost_estimate=cost(15),
        name="attend_here",
    )(positions, queries, back_rows, here)


def attend_far(queries, far, state, positions, back_rows, tq, tk):
    tokens = queries.shape[0]
    groups = queries.shape[1] // (QPK * HD)
    kv_spec = pl.BlockSpec((tokens, 2 * HD), lambda g, i, p: (0, g))
    return pl.pallas_call(
        functools.partial(attend_far_kernel, tk),
        grid_spec=pltpu.PrefetchScalarGridSpec(
            num_scalar_prefetch=1,
            grid=(groups, tokens // tq),
            in_specs=[
                pl.BlockSpec((tq, QPK * HD), lambda g, i, p: (i, g)),
                pl.BlockSpec((8, tq), lambda g, i, p: (0, i)),
                kv_spec,
                kv_spec,
            ]
            + [
                pl.BlockSpec((1, 1, *part.shape[2:]), lambda g, i, p: (g, i, 0, 0)) for part in state
            ],
            out_specs=[
                pl.BlockSpec((tq, QPK * HD), lambda g, i, p: (i, g)),
                pl.BlockSpec((1, 1, 8, QPK * tq), lambda g, i, p: (g, i, 0, 0)),
            ],
            scratch_shapes=[
                pltpu.VMEM((REACH * tokens, 2 * HD), jnp.bfloat16),
                pltpu.VMEM((REACH * tokens, 2 * HD), jnp.bfloat16),
                pltpu.VMEM((QPK * tq, 2 * HD), jnp.bfloat16),
                pltpu.VMEM((2 * HD, QPK * tq), jnp.float32),
                pltpu.VMEM((8, QPK * tq), jnp.float32),
            ],
        ),
        out_shape=[
            jax.ShapeDtypeStruct((tokens, groups * QPK * HD), jnp.bfloat16),
            jax.ShapeDtypeStruct((groups, tokens // tq, 8, QPK * tq), jnp.float32),
        ],
        compiler_params=pltpu.CompilerParams(vmem_limit_bytes=VMEM_LIMIT),
        cost_estimate=cost(21),
        name="attend_far",
    )(positions, queries, back_rows, *far, *state)


def attend_back_kernel(
    tk, pos_ref, q_ref, do_ref, o_ref, back_ref, lse_ref, cos_ref, sin_ref, far_two, far_one, here,
    dq_ref, d_far_two, d_far_one, d_here, kv, dkv, qs, dos, dq
):
    tokens = here.shape[0]
    tq = q_ref.shape[0]
    tile = pl.program_id(0)

    @pl.when(tile == 0)
    def _():
        for i, ref in enumerate((far_two, far_one, here)):
            kv[pl.ds(i * tokens, tokens), :] = ref[...]
        dkv[...] = jnp.zeros_like(dkv)

    qs[...] = stack_heads(q_ref[...], True)
    dos[...] = stack_heads(do_ref[...], False)
    dq[...] = jnp.zeros_like(dq)
    product = dos[...].astype(jnp.float32) * stack_heads(o_ref[...], False).astype(jnp.float32)
    delta = jnp.sum(jnp.transpose(product), axis=0, keepdims=True)
    lse = lse_ref[0, 0, 0:1, :]

    def step(key, masked):
        keys = kv[pl.ds(key, tk), :]
        scores = lax.dot_general(keys, qs[...], COLS_BY_COLS, preferred_element_type=jnp.float32)
        probs = jnp.exp2(scores * EXP_SCALE - lse)
        if masked:
            allowed = allowed_block(key, tile, tokens, tk, tq, back_ref[0:1, :])
            probs = jnp.where(allowed, probs, 0.0)
        d_probs = lax.dot_general(keys, dos[...], COLS_BY_COLS, preferred_element_type=jnp.float32)
        d_scores = (probs * (d_probs - delta)).astype(jnp.bfloat16)
        d_keys = jnp.dot(d_scores, qs[...], preferred_element_type=jnp.float32)
        d_values = jnp.dot(probs.astype(jnp.bfloat16), dos[...], preferred_element_type=jnp.float32)
        dkv[pl.ds(key, tk), :] += d_keys * HD**-0.5 + d_values
        dq[...] += lax.dot_general(
            d_scores, keys, ROWS_BY_ROWS, preferred_element_type=jnp.float32
        )

    key_blocks(pos_ref, tile, tq, tk, step)
    cos, sin = cos_ref[...], sin_ref[...]
    blocks = unstack_heads(dq[...] * HD**-0.5, True)
    blocks = [block * cos - turn_halves(block) * sin for block in blocks]
    dq_ref[...] = jnp.concatenate(blocks, axis=1).astype(jnp.bfloat16)

    @pl.when(tile == pl.num_programs(0) - 1)
    def _():
        d_far_two[...] = dkv[pl.ds(0, tokens), :].astype(jnp.bfloat16)
        d_far_one[...] = dkv[pl.ds(tokens, tokens), :].astype(jnp.bfloat16)
        d_here[...] = dkv[pl.ds(2 * tokens, tokens), :]


def attend_back(
    queries, d_attn, attn, lse, sources, positions, back_rows, cos, sin, group, tq, tk
):
    tokens = queries.shape[0]
    kv_spec = pl.BlockSpec((tokens, 2 * HD), lambda i, p: (0, group))
    own_kv = pl.BlockSpec((tokens, 2 * HD), lambda i, p: (0, 0))
    q_spec = pl.BlockSpec((tq, QPK * HD), lambda i, p: (i, group))
    own_q = pl.BlockSpec((tq, QPK * HD), lambda i, p: (i, 0))
    angle_spec = pl.BlockSpec((tq, 128), lambda i, p: (i, 0))
    return pl.pallas_call(
        functools.partial(attend_back_kernel, tk),
        grid_spec=pltpu.PrefetchScalarGridSpec(
            num_scalar_prefetch=1,
            grid=(tokens // tq,),
            in_specs=[
                q_spec,
                q_spec,
                q_spec,
                pl.BlockSpec((8, tq), lambda i, p: (0, i)),
                pl.BlockSpec((1, 1, 8, QPK * tq), lambda i, p: (group, i, 0, 0)),
                angle_spec,
                angle_spec,
                kv_spec,
                kv_spec,
                kv_spec,
            ],
            out_specs=[own_q, own_kv, own_kv, own_kv],
            scratch_shapes=[
                pltpu.VMEM(((REACH + 1) * tokens, 2 * HD), jnp.bfloat16),
                pltpu.VMEM(((REACH + 1) * tokens, 2 * HD), jnp.float32),
                pltpu.VMEM((QPK * tq, 2 * HD), jnp.bfloat16),
                pltpu.VMEM((QPK * tq, 2 * HD), jnp.bfloat16),
                pltpu.VMEM((QPK * tq, 2 * HD), jnp.float32),
            ],
        ),
        out_shape=[
            jax.ShapeDtypeStruct((tokens, QPK * HD), jnp.bfloat16),
            jax.ShapeDtypeStruct((tokens, 2 * HD), jnp.bfloat16),
            jax.ShapeDtypeStruct((tokens, 2 * HD), jnp.bfloat16),
            jax.ShapeDtypeStruct((tokens, 2 * HD), jnp.float32),
        ],
        compiler_params=pltpu.CompilerParams(vmem_limit_bytes=VMEM_LIMIT),
        cost_estimate=cost(28),
        name="attend_back",
    )(positions, queries, d_attn, attn, back_rows, lse, cos, sin, *sources)


def mix_kernel(groups, cos_ref, sin_ref, *refs):
    out_ref = refs[-1]
    cos, sin = cos_ref[...], sin_ref[...]
    key_lane = lax.broadcasted_iota(jnp.int32, cos.shape, 1) < HD
    for group in range(groups):
        dq_ref, here, from_one, from_two = refs[4 * group : 4 * group + 4]
        base = group * (QPK + 2) * HD
        out_ref[:, base : base + QPK * HD] = dq_ref[...]
        total = here[...] + from_one[...].astype(jnp.float32) + from_two[...].astype(jnp.float32)
        turned = total * cos - turn_halves(total) * sin
        out_ref[:, base + QPK * HD : base + (QPK + 2) * HD] = jnp.where(
            key_lane, turned, total
        ).astype(jnp.bfloat16)


def mix_grads(parts, cos, sin, tile):
    tokens = cos.shape[0]
    groups = len(parts)

    def rows(wide):
        return pl.BlockSpec((tile, wide), lambda i: (i, 0))

    flat = [array for part in parts for array in part]
    return pl.pallas_call(
        functools.partial(mix_kernel, groups),
        grid=(tokens // tile,),
        in_specs=[rows(128), rows(128)] + [rows(array.shape[1]) for array in flat],
        out_specs=rows(groups * (QPK + 2) * HD),
        out_shape=jax.ShapeDtypeStruct((tokens, groups * (QPK + 2) * HD), jnp.bfloat16),
        compiler_params=pltpu.CompilerParams(vmem_limit_bytes=VMEM_LIMIT),
        cost_estimate=cost(3),
        name="mix_grads",
    )(cos, sin, *flat)


def out_step_kernel(distances, last, rank_ref, *refs):
    refs = list(refs)
    base_ref = refs.pop(0)
    gain_ref = refs.pop(0) if last else None
    total = base_ref[...].astype(jnp.float32)
    for distance, count in distances:
        piece = refs.pop(0)[...]
        if count == 2:
            piece = jnp.where(rank_ref[0] >= distance, piece, refs.pop(0)[...])
        total = total + jnp.dot(piece, refs.pop(0)[...], preferred_element_type=jnp.float32)
    if not last:
        refs[0][...] = total
    else:

        @pl.when(pl.program_id(0) == rank_ref[0])
        def _():
            refs[0][...] = total

        inverse = lax.rsqrt(jnp.mean(total * total, axis=1, keepdims=True) + NORM_EPS)
        refs[1][...] = (total * inverse * gain_ref[...]).astype(jnp.bfloat16)


def out_step(base, pieces, rank, weight, tile, gain=None):
    tokens, width = base.shape
    depth = pieces[0][1][0].shape[1]
    last = gain is not None
    slots = weight.shape[0] // depth

    def rows(wide):
        return pl.BlockSpec((tile, wide), lambda i, r: (i, 0))

    def slot_rows(distance, count):
        def index(i, r):
            slot = r[0] - distance
            if count == 2:
                slot = jnp.where(r[0] >= distance, slot, r[0] + distance)
            return jnp.clip(slot, 0, slots - 1), 0

        return pl.BlockSpec((depth, width), index)

    operands, specs = [base], [rows(width)]
    if last:
        operands.append(gain[None])
        specs.append(pl.BlockSpec((1, width), lambda i, r: (0, 0)))
    for distance, blocks in pieces:
        operands += [*blocks, weight]
        specs += [rows(depth)] * len(blocks) + [slot_rows(distance, len(blocks))]
    outs = [jax.ShapeDtypeStruct((tile if last else tokens, width), jnp.float32)]
    out_specs = [pl.BlockSpec((tile, width), lambda i, r: (0, 0)) if last else rows(width)]
    if last:
        outs.append(jax.ShapeDtypeStruct((tokens, width), jnp.bfloat16))
        out_specs.append(rows(width))
    distances = tuple((distance, len(blocks)) for distance, blocks in pieces)
    made = pl.pallas_call(
        functools.partial(out_step_kernel, distances, last),
        grid_spec=pltpu.PrefetchScalarGridSpec(
            num_scalar_prefetch=1,
            grid=(tokens // tile,),
            in_specs=specs,
            out_specs=out_specs,
        ),
        out_shape=outs,
        compiler_params=pltpu.CompilerParams(vmem_limit_bytes=VMEM_LIMIT),
        cost_estimate=cost(7),
        name="out_step",
    )(jnp.reshape(rank, (1,)).astype(jnp.int32), *operands)
    return made if last else made[0]


def own_kernel(rank_ref, *refs):
    *pieces, out_ref = refs

    def put(piece):
        out_ref[...] = piece[...]

    pick_piece(pieces, rank_ref[0] - pl.program_id(0), put)


def own_rows_of_heads(pieces, rank, own):
    size = (len(pieces) + 1) // 2
    columns = pieces[0].shape[1]
    return pl.pallas_call(
        own_kernel,
        grid_spec=pltpu.PrefetchScalarGridSpec(
            num_scalar_prefetch=1,
            grid=(size,),
            in_specs=[pl.BlockSpec((own, columns), lambda i, r: (r[0], 0))] * len(pieces),
            out_specs=pl.BlockSpec((own, columns), lambda i, r: (0, i)),
        ),
        out_shape=jax.ShapeDtypeStruct((own, columns * size), pieces[0].dtype),
        compiler_params=pltpu.CompilerParams(vmem_limit_bytes=VMEM_LIMIT),
        cost_estimate=cost(2),
        name="own_rows_of_heads",
    )(jnp.reshape(rank, (1,)).astype(jnp.int32), *pieces)


def gate_kernel(n_ref, w_ref, dh_ref, hidden_ref, dgu_ref):
    wide = dh_ref.shape[1]
    both = jnp.dot(n_ref[...], w_ref[...], preferred_element_type=jnp.float32)
    gate, up = both[:, :wide], both[:, wide:]
    sigmoid = jax.nn.sigmoid(gate)
    silu = gate * sigmoid
    d_hidden = dh_ref[...].astype(jnp.float32)
    hidden_ref[...] = (silu * up).astype(jnp.bfloat16)
    d_gate = d_hidden * up * (sigmoid + silu * (1.0 - sigmoid))
    dgu_ref[...] = jnp.concatenate([d_gate, d_hidden * silu], axis=1).astype(jnp.bfloat16)


def gate_and_back(normed, weight, d_hidden, tile, wide):
    tokens, width = normed.shape
    units = d_hidden.shape[1]
    cell = pl.BlockSpec((tile, wide), lambda j, i: (i, j))
    pair_cell = pl.BlockSpec((tile, 2 * wide), lambda j, i: (i, j))
    return pl.pallas_call(
        gate_kernel,
        grid=(units // wide, tokens // tile),
        in_specs=[
            pl.BlockSpec((tile, width), lambda j, i: (i, 0)),
            pl.BlockSpec((width, 2 * wide), lambda j, i: (0, j)),
            cell,
        ],
        out_specs=[cell, pair_cell],
        out_shape=[
            jax.ShapeDtypeStruct((tokens, units), jnp.bfloat16),
            jax.ShapeDtypeStruct((tokens, 2 * units), jnp.bfloat16),
        ],
        compiler_params=pltpu.CompilerParams(vmem_limit_bytes=VMEM_LIMIT),
        cost_estimate=cost(27),
        name="gate_and_back",
    )(normed, weight, d_hidden)


def blocks_kernel(chunks_ref, *refs):
    count = (len(refs) - 1) // 2
    left = jnp.concatenate([ref[...] for ref in refs[:count]], axis=0)
    product = lax.dot_general(
        left, refs[count][...], COLS_BY_COLS, preferred_element_type=jnp.float32
    ).astype(jnp.bfloat16)
    rows = refs[0].shape[0]
    for i, out_ref in enumerate(refs[count + 1 :]):
        out_ref[...] = product[i * rows : (i + 1) * rows]


def blocks_times(left, right, chunks, rows, wide, micros):
    depth = left.shape[1]
    count = chunks.shape[0]

    def block_spec(i):
        return pl.BlockSpec((rows, depth), lambda j, c: (c[i], 0))

    return pl.pallas_call(
        blocks_kernel,
        grid_spec=pltpu.PrefetchScalarGridSpec(
            num_scalar_prefetch=1,
            grid=(right.shape[0] // wide,),
            in_specs=[block_spec(i) for i in range(count)]
            + [pl.BlockSpec((wide, depth), lambda j, c: (j, 0))],
            out_specs=[pl.BlockSpec((rows, wide), lambda j, c: (0, j))] * count,
        ),
        out_shape=[jax.ShapeDtypeStruct((rows, right.shape[0]), jnp.bfloat16)] * count,
        compiler_params=pltpu.CompilerParams(vmem_limit_bytes=VMEM_LIMIT),
        cost_estimate=cost(micros),
        name="blocks_times",
    )(chunks, *[left] * count, right)


def gain_kernel(part_ref, w_ref, out_ref):
    product = part_ref[...].astype(jnp.float32) * w_ref[...].astype(jnp.float32)
    ones = jnp.ones((8, product.shape[1]), jnp.float32)
    out_ref[...] = lax.dot_general(
        ones, product, COLS_BY_COLS, precision=lax.Precision.HIGHEST,
        preferred_element_type=jnp.float32,
    )


def row_products(part, weight, tile):
    rows, columns = part.shape
    cell = pl.BlockSpec((tile, columns), lambda i: (i, 0))
    sums = pl.pallas_call(
        gain_kernel,
        grid=(rows // tile,),
        in_specs=[cell, cell],
        out_specs=pl.BlockSpec((8, tile), lambda i: (0, i)),
        out_shape=jax.ShapeDtypeStruct((8, rows), jnp.float32),
        compiler_params=pltpu.CompilerParams(vmem_limit_bytes=VMEM_LIMIT),
        cost_estimate=cost(4),
        name="row_products",
    )(part, weight)
    return sums[0]


def norm_back_rows(vector, grad_in, gain):
    inverse = lax.rsqrt(jnp.mean(vector * vector, axis=1, keepdims=True) + NORM_EPS)
    scaled = grad_in * gain
    mean = jnp.mean(vector * scaled, axis=1, keepdims=True)
    grad = inverse * scaled - vector * (inverse * inverse * inverse * mean)
    return grad, jnp.sum(grad_in * vector * inverse, axis=0, keepdims=True)


def sum_refs(refs):
    total = refs[0][...].astype(jnp.float32)
    for ref in refs[1:]:
        total = total + ref[...].astype(jnp.float32)
    return total


def mid_kernel(mid_ref, dy_ref, gain_ref, *refs):
    *parts, d_mid_ref, branch_ref, gain_grad_ref = refs
    grad, gain_grad = norm_back_rows(mid_ref[...], sum_refs(parts), gain_ref[...])
    d_mid = dy_ref[...].astype(jnp.float32) + grad
    d_mid_ref[...] = d_mid
    branch_ref[...] = d_mid.astype(jnp.bfloat16)
    gain_grad = jnp.broadcast_to(gain_grad, gain_grad_ref.shape)

    @pl.when(pl.program_id(0) == 0)
    def _():
        gain_grad_ref[...] = gain_grad

    @pl.when(pl.program_id(0) > 0)
    def _():
        gain_grad_ref[...] += gain_grad


def back_to_mid(parts, mid, output_grad, gain):
    own, width = output_grad.shape
    tile = min(64, own)
    rows = pl.BlockSpec((tile, width), lambda i: (i, 0))
    outs = pl.pallas_call(
        mid_kernel,
        grid=(own // tile,),
        in_specs=[rows, rows, pl.BlockSpec((1, width), lambda i: (0, 0))] + [rows] * len(parts),
        out_specs=[rows, rows, pl.BlockSpec((8, width), lambda i: (0, 0))],
        out_shape=[
            jax.ShapeDtypeStruct((own, width), jnp.float32),
            jax.ShapeDtypeStruct((own, width), jnp.bfloat16),
            jax.ShapeDtypeStruct((8, width), jnp.float32),
        ],
        compiler_params=pltpu.CompilerParams(vmem_limit_bytes=VMEM_LIMIT),
        cost_estimate=cost(4),
        name="back_to_mid",
    )(mid, output_grad, gain[None], *parts)
    return outs[0], outs[1], outs[2][0]


def input_kernel(x_ref, d_mid_ref, gain_ref, *refs):
    *parts, out_ref = refs
    x = x_ref[...].astype(jnp.float32)
    grad, _ = norm_back_rows(x, sum_refs(parts), gain_ref[...])
    out_ref[...] = d_mid_ref[...] + grad


def back_to_input(parts, layer_input, d_mid, gain):
    own, width = layer_input.shape
    tile = min(64, own)
    rows = pl.BlockSpec((tile, width), lambda i: (i, 0))
    return pl.pallas_call(
        input_kernel,
        grid=(own // tile,),
        in_specs=[rows, rows, pl.BlockSpec((1, width), lambda i: (0, 0))] + [rows] * len(parts),
        out_specs=rows,
        out_shape=jax.ShapeDtypeStruct((own, width), jnp.float32),
        compiler_params=pltpu.CompilerParams(vmem_limit_bytes=VMEM_LIMIT),
        cost_estimate=cost(4),
        name="back_to_input",
    )(layer_input, d_mid, gain[None], *parts)


def round_kernel(wide, w_ref, out_ref):
    for block in range(w_ref.shape[2] // wide):
        for half in range(2):
            column = (2 * block + half) * wide
            out_ref[:, column : column + wide] = w_ref[
                half, :, block * wide : (block + 1) * wide
            ].astype(jnp.bfloat16)


def round_interleaved(weight, wide):
    _, rows, units = weight.shape
    tile = min(64, rows)
    return pl.pallas_call(
        functools.partial(round_kernel, wide),
        grid=(rows // tile,),
        in_specs=[pl.BlockSpec((2, tile, units), lambda i: (0, i, 0))],
        out_specs=pl.BlockSpec((tile, 2 * units), lambda i: (i, 0)),
        out_shape=jax.ShapeDtypeStruct((rows, 2 * units), jnp.bfloat16),
        compiler_params=pltpu.CompilerParams(vmem_limit_bytes=VMEM_LIMIT),
        cost_estimate=cost(3),
        name="round_interleaved",
    )(weight)


def norm_back_rows(vector, grad_in, gain):
    inverse = lax.rsqrt(jnp.mean(vector * vector, axis=1, keepdims=True) + NORM_EPS)
    scaled = grad_in * gain
    mean = jnp.mean(vector * scaled, axis=1, keepdims=True)
    grad = inverse * scaled - vector * (inverse * inverse * inverse * mean)
    return grad, jnp.sum(grad_in * vector * inverse, axis=0, keepdims=True)


def sum_refs(refs):
    total = refs[0][...].astype(jnp.float32)
    for ref in refs[1:]:
        total = total + ref[...].astype(jnp.float32)
    return total


def mid_kernel(mid_ref, dy_ref, gain_ref, *refs):
    *parts, d_mid_ref, branch_ref, gain_grad_ref = refs
    grad, gain_grad = norm_back_rows(mid_ref[...], sum_refs(parts), gain_ref[...])
    d_mid = dy_ref[...].astype(jnp.float32) + grad
    d_mid_ref[...] = d_mid
    branch_ref[...] = d_mid.astype(jnp.bfloat16)
    gain_grad = jnp.broadcast_to(gain_grad, gain_grad_ref.shape)

    @pl.when(pl.program_id(0) == 0)
    def _():
        gain_grad_ref[...] = gain_grad

    @pl.when(pl.program_id(0) > 0)
    def _():
        gain_grad_ref[...] += gain_grad


def back_to_mid(parts, mid, output_grad, gain):
    own, width = output_grad.shape
    tile = min(64, own)
    rows = pl.BlockSpec((tile, width), lambda i: (i, 0))
    outs = pl.pallas_call(
        mid_kernel,
        grid=(own // tile,),
        in_specs=[rows, rows, pl.BlockSpec((1, width), lambda i: (0, 0))] + [rows] * len(parts),
        out_specs=[rows, rows, pl.BlockSpec((8, width), lambda i: (0, 0))],
        out_shape=[
            jax.ShapeDtypeStruct((own, width), jnp.float32),
            jax.ShapeDtypeStruct((own, width), jnp.bfloat16),
            jax.ShapeDtypeStruct((8, width), jnp.float32),
        ],
        compiler_params=pltpu.CompilerParams(vmem_limit_bytes=VMEM_LIMIT),
        cost_estimate=cost(4),
        name="back_to_mid",
    )(mid, output_grad, gain[None], *parts)
    return outs[0], outs[1], outs[2][0]


def input_kernel(x_ref, d_mid_ref, gain_ref, *refs):
    *parts, out_ref = refs
    x = x_ref[...].astype(jnp.float32)
    grad, _ = norm_back_rows(x, sum_refs(parts), gain_ref[...])
    out_ref[...] = d_mid_ref[...] + grad


def back_to_input(parts, layer_input, d_mid, gain):
    own, width = layer_input.shape
    tile = min(64, own)
    rows = pl.BlockSpec((tile, width), lambda i: (i, 0))
    return pl.pallas_call(
        input_kernel,
        grid=(own // tile,),
        in_specs=[rows, rows, pl.BlockSpec((1, width), lambda i: (0, 0))] + [rows] * len(parts),
        out_specs=rows,
        out_shape=jax.ShapeDtypeStruct((own, width), jnp.float32),
        compiler_params=pltpu.CompilerParams(vmem_limit_bytes=VMEM_LIMIT),
        cost_estimate=cost(4),
        name="back_to_input",
    )(layer_input, d_mid, gain[None], *parts)


def round_kernel(w_ref, out_ref):
    out_ref[...] = w_ref[0].astype(jnp.bfloat16)


def round_interleaved(weight, wide):
    _, rows, units = weight.shape
    return pl.pallas_call(
        round_kernel,
        grid=(units // wide, 2),
        in_specs=[pl.BlockSpec((1, rows, wide), lambda j, k: (k, 0, j))],
        out_specs=pl.BlockSpec((rows, wide), lambda j, k: (0, 2 * j + k)),
        out_shape=jax.ShapeDtypeStruct((rows, 2 * units), jnp.bfloat16),
        cost_estimate=cost(6),
        name="round_interleaved",
    )(weight)


def adam_kernel(g_ref, w_ref, m_ref, s_ref, grad_ref, w_out, m_out, s_out, copy_out):
    grad = g_ref[...].astype(jnp.float32)
    new, moment, square, _ = adam_step(w_ref[0], grad, m_ref[0], s_ref[0])
    grad_ref[0] = grad
    w_out[0] = new
    m_out[0] = moment
    s_out[0] = square
    copy_out[0] = new.astype(jnp.bfloat16)


def adam_interleaved(grad, weight, moment, square, wide):
    _, rows, units = weight.shape
    cell = pl.BlockSpec((1, rows, wide), lambda j, k: (k, 0, j))
    shape = jax.ShapeDtypeStruct(weight.shape, jnp.float32)
    return pl.pallas_call(
        adam_kernel,
        grid=(units // wide, 2),
        in_specs=[pl.BlockSpec((rows, wide), lambda j, k: (0, 2 * j + k)), cell, cell, cell],
        out_specs=[cell] * 5,
        out_shape=[shape] * 4 + [jax.ShapeDtypeStruct(weight.shape, jnp.bfloat16)],
        compiler_params=pltpu.CompilerParams(vmem_limit_bytes=VMEM_LIMIT),
        cost_estimate=cost(13),
        name="adam_interleaved",
    )(grad, weight, moment, square)


def angle_tables(positions):
    half_size = HD // 2
    freq = ROPE_BASE ** (-(jnp.arange(half_size).astype(jnp.float32) * 2.0 / HD))
    angle = positions.astype(jnp.float32)[:, None] * freq[None, :]
    cos, sin = jnp.cos(angle), jnp.sin(angle)
    return jnp.concatenate([cos] * 4, axis=1), jnp.concatenate([-sin, sin] * 2, axis=1)


def adam_step(weight_old, grad_new, moment_one, moment_two):
    moment_next = BETA * moment_one + (1.0 - BETA) * grad_new
    square_next = BETA * moment_two + (1.0 - BETA) * grad_new * grad_new
    change = -RATE * (moment_next / (jnp.sqrt(square_next) + ADAM_EPS) + DECAY * weight_old)
    return (weight_old + change, moment_next, square_next, change)


def local(
    layer_input,
    output_grad,
    segment_ids,
    positions,
    qkv_weight,
    qkv_moment,
    qkv_square,
    out_weight,
    out_moment,
    out_square,
    gate_up_weight,
    gate_up_moment,
    gate_up_square,
    down_weight,
    down_moment,
    down_square,
    norm_gains,
    gains_moment,
    gains_square,
):
    low = low_type = jnp.bfloat16
    full = jnp.float32
    own, width = layer_input.shape
    tokens = positions.shape[0]
    rank = lax.axis_index("tp")
    units = down_weight.shape[0]
    groups = qkv_weight.shape[1] // ((QPK + 2) * HD)
    head_columns = groups * QPK * HD
    tile = min(256, own)
    gain_one = norm_gains[0]
    gain_two = norm_gains[1]

    wide = min(512, units)

    close = lax.optimization_barrier

    w_qkv = lax.all_gather(qkv_weight.astype(low), "seq", axis=0, tiled=True)
    side = (gate_up_weight, down_weight, out_weight, positions)
    x_line = LineGather(layer_input, "tp")
    for index in range(x_line.hops):
        x_line.hop()
        if index == 1:
            held_gate_up, held_down, held_out, held_positions = side
            w_gate_up = lax.all_gather(
                round_interleaved(held_gate_up, wide), "seq", axis=0, tiled=True
            )
            cos, sin = angle_tables(held_positions)
            back_rows = jnp.broadcast_to(held_positions[None, :], (8, tokens))
            side = (held_down.astype(low), held_out.astype(low), cos, sin, back_rows)
        x_line.moving, side = close((x_line.moving, side))
    pieces, side, w_qkv, output_grad = close((x_line.pieces, side, w_qkv, output_grad))
    low_down, low_out, cos, sin, back_rows = side

    dy_line = LineGather(output_grad, "tp")
    dy_line.hop()
    made = project_qkv(pieces, rank, w_qkv, gain_one, cos, sin)
    made, dy_line.moving, low_out, low_down = close((made, dy_line.moving, low_out, low_down))
    x_rows, normed_one, queries, kv = made
    w_down = lax.all_gather(low_down, "seq", axis=1, tiled=True)
    far = [along_sequence(kv, distance, tokens) for distance in (2, 1)]
    if dy_line.hops > 1:
        dy_line.hop()
    states = attend_here(queries, kv, positions, back_rows, 256, 512)
    out_strip = swap_gather(after(low_out, states[1]), "tp")
    far, states, queries, w_gate_up, dy_line.moving = close(
        (far, states, queries, w_gate_up, dy_line.moving)
    )
    for _ in range(2, dy_line.hops):
        dy_line.hop()
    attn, lse = attend_far(queries, far, states, positions, back_rows, 256, 512)
    attn, lse, dy_pieces, x_rows, out_strip = close(
        (attn, lse, dy_line.pieces, x_rows, out_strip)
    )
    w_out = lax.all_gather(out_strip.reshape(-1, low_out.shape[1]), "seq", axis=1, tiled=True)

    heads_line = LineGather(attn, "tp")
    arrived = [(0, [heads_line.from_low[0]])]
    total = x_rows
    for index in range(heads_line.hops):
        heads_line.hop()
        if index == 0:
            grad_rows = place_rows(dy_pieces, rank)
            d_hidden = contract_cols(grad_rows, w_down).astype(low)
            heads_line.moving, grad_rows, d_hidden, total = close(
                (heads_line.moving, grad_rows, d_hidden, total)
            )
        elif index < heads_line.hops - 1:
            heads_line.moving, w_out = close((heads_line.moving, w_out))
        else:
            total = out_step(total, arrived, rank, w_out, own)
            heads_line.moving, total = close((heads_line.moving, total))
            arrived = []
        below, above = heads_line.moving
        step = heads_line.step
        if 2 * step > heads_line.hops:
            arrived.append((step, [below, above]))
        else:
            arrived += [(step, [below]), (-step, [above])]

    mid, normed_two = out_step(total, arrived, rank, w_out, own, gain_two)
    mid, normed_two, w_gate_up, d_hidden = close((mid, normed_two, w_gate_up, d_hidden))
    hidden, d_gate_up = close(gate_and_back(normed_two, w_gate_up, d_hidden, 1024, wide))
    down_grad = contract_rows(hidden, grad_rows).astype(low)
    down_grad, hidden, d_gate_up, normed_two, grad_rows = close(
        (down_grad, hidden, d_gate_up, normed_two, grad_rows)
    )
    down_grad = lax.psum_scatter(down_grad, "seq", scatter_dimension=1, tiled=True)
    peers = peers_of("tp")
    first = blocks_times(d_gate_up, w_gate_up, peers[:1], own, 512, 9)
    first, side = close((first, (hidden, d_gate_up, normed_two, grad_rows)))
    back_line = LineScatter(first, "tp")
    for index in range(back_line.hops):
        back_line.hop()
        hidden, d_gate_up, normed_two, grad_rows = side
        if index == 0:
            second = blocks_times(d_gate_up, w_gate_up, peers[1:], own, 256, 22)
            back_line.moving, side, second = close((back_line.moving, side, second))
            back_line.made += second
        elif index == 1:
            gate_up_grad = contract_rows(normed_two, d_gate_up).astype(low)
            back_line.moving, side, gate_up_grad = close((back_line.moving, side, gate_up_grad))
            gate_up_grad = lax.psum_scatter(gate_up_grad, "seq", scatter_dimension=0, tiled=True)
        elif index == 2:
            partial_out = jnp.dot(hidden, w_down, preferred_element_type=full).astype(low)
            back_line.moving, side, partial_out = close((back_line.moving, side, partial_out))
        else:
            back_line.moving, side = close((back_line.moving, side))
    d_mid, d_branch, gain_two_grad = back_to_mid(back_line.parts, mid, output_grad, gain_two)

    d_attn = contract_cols(d_branch, w_out).astype(low)
    d_attn, d_branch, d_mid, mid, gain_two_grad, partial_out = close(
        (d_attn, d_branch, d_mid, mid, gain_two_grad, partial_out)
    )
    d_attn = lax.all_to_all(d_attn, "tp", split_axis=1, concat_axis=0, tiled=True)
    own_heads = own_rows_of_heads(heads_line.pieces, rank, own)
    out_grad = contract_rows(own_heads, d_branch).astype(low)
    d_attn, out_grad, partial_out, down_grad = close((d_attn, out_grad, partial_out, down_grad))
    out_grad = lax.psum_scatter(out_grad, "seq", scatter_dimension=1, tiled=True)
    result = swap_scatter_parts(partial_out, "tp")
    grads = []
    travelled = []
    for group in range(groups):
        made = attend_back(
            queries, d_attn, attn, lse, [*far, kv], positions, back_rows,
            cos, sin, group, 256, 512,
        )
        made, d_attn, travelled = close((made, d_attn, travelled))
        grads.append(made)
        travelled.append(
            [along_sequence(made[2], -1, tokens), along_sequence(made[1], -2, tokens)]
        )
    down_grad = down_grad.astype(full)
    down_new = adam_step(down_weight, down_grad, down_moment, down_square)
    down_new, grads, travelled, down_grad = close((down_new, grads, travelled, down_grad))
    d_mixed = mix_grads(
        [(made[0], made[3], *moved) for made, moved in zip(grads, travelled, strict=True)],
        cos, sin, tile,
    )
    made = blocks_times(d_mixed, w_qkv, peers[:1], own, 512, 2)
    made, d_mixed, gate_up_grad = close((made, d_mixed, gate_up_grad))
    in_line = LineScatter(made, "tp")
    for index in range(in_line.hops):
        in_line.hop()
        if index == 0:
            made = blocks_times(d_mixed, w_qkv, peers[1:], own, 512, 5)
            qkv_grad = contract_rows(normed_one, d_mixed).astype(low)
            gain_one_grad = row_products(qkv_grad, w_qkv, min(512, width)) / gain_one
            gains_grad = jnp.stack([gain_one_grad, gain_two_grad])
            in_line.moving, qkv_grad, gains_grad, result, made = close(
                (in_line.moving, qkv_grad, gains_grad, result, made)
            )
            in_line.made += made
            qkv_grad = lax.psum_scatter(qkv_grad, "seq", scatter_dimension=0, tiled=True)
        elif index == 1:
            outputs = (mid + sum_parts(result)).astype(low)
            gains_grad = sum_by_swaps(gains_grad, "seq")
            in_line.moving, outputs, gains_grad, out_grad, gate_up_grad = close(
                (in_line.moving, outputs, gains_grad, out_grad, gate_up_grad)
            )
            out_parts = swap_scatter_parts(out_grad, "tp")
        elif index == 2:
            gate_up_new = adam_interleaved(
                gate_up_grad, gate_up_weight, gate_up_moment, gate_up_square, wide
            )
            gains_grad = sum_at_once(after(gains_grad, gate_up_new[4]), "tp")
            in_line.moving, gains_grad, out_parts, gate_up_new = close(
                (in_line.moving, gains_grad, out_parts, gate_up_new)
            )
        else:
            in_line.moving = close(in_line.moving)
    input_grad = back_to_input(in_line.parts, layer_input, d_mid, gain_one)
    out_grad = sum_parts(out_parts)
    out_new = adam_step(out_weight, out_grad, out_moment, out_square)

    out_grad = out_grad.astype(full)
    qkv_grad = qkv_grad.astype(full)
    qkv_new = adam_step(qkv_weight, qkv_grad, qkv_moment, qkv_square)
    gains_new = adam_step(norm_gains, gains_grad, gains_moment, gains_square)
    return (
        outputs,
        input_grad,
        qkv_grad,
        qkv_new[0],
        qkv_new[1],
        qkv_new[2],
        qkv_new[0].astype(low),
        out_grad,
        out_new[3],
        out_new[1],
        out_new[2],
        *gate_up_new,
        down_grad,
        down_new[0],
        down_new[1],
        down_new[2],
        down_new[0].astype(low),
        gains_grad,
        gains_new[3],
        gains_new[1],
        gains_new[2],
    )


def solution(mesh):
    tokens = P(("seq", "tp"), None)
    rows = P("seq", "tp")
    columns = P("tp", "seq")
    pair = P(None, "seq", "tp")
    return jax.shard_map(
        local,
        mesh=mesh,
        in_specs=(
            (tokens,) * 2 + (P("seq"),) * 2 + (rows,) * 3 + (columns,) * 3 + (pair,) * 3
            + (columns,) * 3 + (P(),) * 3
        ),
        out_specs=(
            (tokens,) * 2 + (rows,) * 5 + (columns,) * 4 + (pair,) * 5 + (columns,) * 5 + (P(),) * 4
        ),
        check_vma=False,
    )
```

```python
import functools

import jax
import jax.numpy as jnp
from jax import lax
from jax.experimental import pallas as pl
from jax.experimental.pallas import tpu as pltpu
from jax.sharding import PartitionSpec as P

HD = 64
QPK = 4
REACH = 2
SEQLEN = 4096

NORM_EPS = 1e-05
ROPE_BASE = 500000.0
BETA = 0.5
RATE = 0.02
DECAY = 0.1
ADAM_EPS = 1e-08
NEG_FILL = -1e30
LOG2E = 1.4426950408889634
EXP_SCALE = HD**-0.5 * LOG2E
VMEM_LIMIT = 48 * 2**20

ROWS_BY_ROWS = (((0,), (0,)), ((), ()))
COLS_BY_COLS = (((1,), (1,)), ((), ()))


def cost(micros):
    return pl.CostEstimate(
        flops=int(micros * 1.15e9), transcendentals=0, bytes_accessed=int(micros * 3.0e6)
    )


def after(block, *others):
    return lax.optimization_barrier((block, *others))[0]


def contract_rows(left, right):
    return lax.dot_general(left, right, ROWS_BY_ROWS, preferred_element_type=jnp.float32)


def contract_cols(left, right):
    return lax.dot_general(left, right, COLS_BY_COLS, preferred_element_type=jnp.float32)


class LineGather:
    def __init__(self, block, axis):
        self.axis = axis
        self.hops = lax.axis_size(axis) - 1
        self.from_low = [block]
        self.from_high = [block]

    @property
    def step(self):
        return len(self.from_low) - 1

    def hop(self):
        size, passed = self.hops + 1, self.step
        up = [(i, i + 1) for i in range(passed, size - 1)]
        down = [(i, i - 1) for i in range(1, size - passed)]
        self.from_low.append(lax.ppermute(self.from_low[-1], self.axis, up))
        self.from_high.append(lax.ppermute(self.from_high[-1], self.axis, down))

    @property
    def moving(self):
        return self.from_low[-1], self.from_high[-1]

    @moving.setter
    def moving(self, pair):
        self.from_low[-1], self.from_high[-1] = pair

    @property
    def pieces(self):
        return [*self.from_low, *self.from_high[1:]]


def send_order(size):
    return [sorted(range(size), key=lambda peer: (-abs(peer - me), peer)) for me in range(size)]


def peers_of(axis):
    size = lax.axis_size(axis)
    return jnp.array(send_order(size), jnp.int32)[lax.axis_index(axis)]


class LineScatter:
    def __init__(self, made, axis):
        self.axis = axis
        self.hops = lax.axis_size(axis) - 1
        self.made = list(made)
        self.step = 0
        self.moving = None

    def addend(self, distance):
        order = send_order(self.hops + 1)
        slots = [
            order[me].index(me + distance) if 0 <= me + distance <= self.hops else None
            for me in range(self.hops + 1)
        ]
        choices = sorted(set(slots) - {None})
        table = jnp.array([choices[0] if slot is None else slot for slot in slots], jnp.int32)
        block = self.made[choices[0]]
        for choice in choices[1:]:
            chosen = table[lax.axis_index(self.axis)] == choice
            block = jnp.where(chosen, self.made[choice], block)
        return block

    def hop(self):
        self.step += 1
        size, step = self.hops + 1, self.step
        to_high = self.addend(size - step)
        to_low = self.addend(step - size)
        if step > 1:
            to_high = to_high + self.moving[0]
            to_low = to_low + self.moving[1]
        self.moving = (
            lax.ppermute(to_high, self.axis, [(i, i + 1) for i in range(step)]),
            lax.ppermute(to_low, self.axis, [(i, i - 1) for i in range(size - step, size)]),
        )

    @property
    def parts(self):
        return [self.made[-1], *self.moving]


def swap_gather(block, axis):
    copies = jnp.broadcast_to(block[None], (lax.axis_size(axis), *block.shape))
    return lax.all_to_all(copies, axis, split_axis=0, concat_axis=0, tiled=True)


def swap_scatter_parts(block, axis):
    size = lax.axis_size(axis)
    parts = block.reshape(size, block.shape[0] // size, block.shape[1])
    return lax.all_to_all(parts, axis, split_axis=0, concat_axis=0, tiled=True)


def sum_parts(parts):
    return jnp.sum(parts.astype(jnp.float32), axis=0)


def sum_by_swaps(block, axis):
    size = lax.axis_size(axis)
    hop = 1
    while hop < size:
        block = block + lax.ppermute(block, axis, [(i, i ^ hop) for i in range(size)])
        hop *= 2
    return block


def sum_at_once(block, axis):
    size = lax.axis_size(axis)
    came = [block]
    for distance in range(1, size):
        route = [(i, (i + distance) % size) for i in range(size)]
        came.append(lax.ppermute(block, axis, route))
    came = jnp.stack(came)
    rank = lax.axis_index(axis)
    total = lax.dynamic_index_in_dim(came, rank, keepdims=False)
    for peer in range(1, size):
        total = total + lax.dynamic_index_in_dim(came, (rank - peer) % size, keepdims=False)
    return total


def along_sequence(block, distance, tokens):
    shards = SEQLEN // tokens
    route = [
        (i, i + distance)
        for i in range(lax.axis_size("seq"))
        if 0 <= i + distance < lax.axis_size("seq") and i // shards == (i + distance) // shards
    ]
    return lax.ppermute(block, "seq", route)


def turn_halves(block):
    lane = lax.broadcasted_iota(jnp.int32, block.shape, 1)
    return jnp.where(lane % HD < HD // 2, pltpu.roll(block, 96, 1), pltpu.roll(block, 32, 1))


def pick_piece(pieces, below, put):
    size = (len(pieces) + 1) // 2
    for distance in range(1 - size, size):
        piece = pieces[distance if distance >= 0 else size - 1 - distance]
        pl.when(below == distance)(functools.partial(put, piece))


def place_kernel(rank_ref, *refs):
    *pieces, out_ref = refs

    def put(piece):
        out_ref[...] = piece[...]

    pick_piece(pieces, rank_ref[0] - pl.program_id(0), put)


def place_rows(pieces, rank):
    own, width = pieces[0].shape
    size = (len(pieces) + 1) // 2
    return pl.pallas_call(
        place_kernel,
        grid_spec=pltpu.PrefetchScalarGridSpec(
            num_scalar_prefetch=1,
            grid=(size,),
            in_specs=[pl.BlockSpec((own, width), lambda i, r: (0, 0))] * len(pieces),
            out_specs=pl.BlockSpec((own, width), lambda i, r: (i, 0)),
        ),
        out_shape=jax.ShapeDtypeStruct((own * size, width), pieces[0].dtype),
        compiler_params=pltpu.CompilerParams(vmem_limit_bytes=VMEM_LIMIT),
        cost_estimate=cost(4),
        name="place_rows",
    )(jnp.reshape(rank, (1,)).astype(jnp.int32), *pieces)


def qkv_kernel(rank_ref, w_ref, gain_ref, cos_ref, sin_ref, *refs):
    x_ref, normed_ref, q_ref, kv_ref = refs[-4:]

    def put(piece):
        x_ref[...] = piece[...]

    pick_piece(refs[:-4], rank_ref[0] - pl.program_id(0), put)
    x = x_ref[...].astype(jnp.float32)
    inverse = lax.rsqrt(jnp.mean(x * x, axis=1, keepdims=True) + NORM_EPS)
    normed = (x * inverse * gain_ref[...]).astype(jnp.bfloat16)
    normed_ref[...] = normed
    mixed = jnp.dot(normed, w_ref[...], preferred_element_type=jnp.float32)
    cos, sin = cos_ref[...], sin_ref[...]
    key_lane = lax.broadcasted_iota(jnp.int32, cos.shape, 1) < HD
    for group in range(mixed.shape[1] // ((QPK + 2) * HD)):
        base = group * (QPK + 2) * HD
        for pair in range(QPK // 2):
            part = mixed[:, base + pair * 128 : base + (pair + 1) * 128]
            part = part * cos + turn_halves(part) * sin
            q_ref[:, group * QPK * HD + pair * 128 : group * QPK * HD + (pair + 1) * 128] = (
                part.astype(jnp.bfloat16)
            )
        part = mixed[:, base + QPK * HD : base + (QPK + 2) * HD]
        part = jnp.where(key_lane, part * cos + turn_halves(part) * sin, part)
        kv_ref[:, group * 128 : (group + 1) * 128] = part.astype(jnp.bfloat16)


def project_qkv(pieces, rank, weight, gain, cos, sin):
    own, width = pieces[0].shape
    size = (len(pieces) + 1) // 2
    tokens = own * size
    groups = weight.shape[1] // ((QPK + 2) * HD)

    def rows(wide):
        return pl.BlockSpec((own, wide), lambda i, r: (i, 0))

    def whole(shape):
        return pl.BlockSpec(shape, lambda i, r: (0, 0))

    widths = (width, width, groups * QPK * HD, groups * 2 * HD)
    return pl.pallas_call(
        qkv_kernel,
        grid_spec=pltpu.PrefetchScalarGridSpec(
            num_scalar_prefetch=1,
            grid=(size,),
            in_specs=[whole(weight.shape), whole((1, width)), rows(128), rows(128)]
            + [whole((own, width))] * len(pieces),
            out_specs=[rows(wide) for wide in widths],
        ),
        out_shape=[jax.ShapeDtypeStruct((tokens, wide), jnp.bfloat16) for wide in widths],
        compiler_params=pltpu.CompilerParams(vmem_limit_bytes=VMEM_LIMIT),
        cost_estimate=cost(9),
        name="project_qkv",
    )(jnp.reshape(rank, (1,)).astype(jnp.int32), weight, gain[None], cos, sin, *pieces)


def stack_heads(block, low_lanes):
    rows = block.shape[0]
    lane = lax.broadcasted_iota(jnp.int32, (rows, 128), 1)
    keep = (lane < HD) if low_lanes else (lane >= HD)
    stacked = []
    for pair in range(QPK // 2):
        both = block[:, pair * 128 : (pair + 1) * 128].astype(jnp.float32)
        turned = pltpu.roll(both, HD, 1)
        for part in (both, turned) if low_lanes else (turned, both):
            stacked.append(jnp.where(keep, part, 0.0))
    return jnp.concatenate(stacked, axis=0).astype(jnp.bfloat16)


def unstack_heads(stacked, low_lanes):
    rows = stacked.shape[0] // QPK
    lane = lax.broadcasted_iota(jnp.int32, (rows, 128), 1)
    blocks = []
    for pair in range(QPK // 2):
        first = stacked[2 * pair * rows : (2 * pair + 1) * rows]
        second = stacked[(2 * pair + 1) * rows : (2 * pair + 2) * rows]
        if low_lanes:
            second = pltpu.roll(second, HD, 1)
        else:
            first = pltpu.roll(first, HD, 1)
        blocks.append(jnp.where(lane < HD, first, second))
    return blocks


def key_blocks(pos_ref, tile, tq, tk, step, low=0, high=None):
    tokens = pos_ref.shape[0]
    query = tile * tq
    start = REACH * tokens + query
    first = jnp.maximum(start - pos_ref[query], low)
    last_start = start + tq - 1 - pos_ref[query + tq - 1]
    end = (start + tq - 1) // tk + 1
    if high is not None:
        end = jnp.minimum(end, high // tk)

    def body(block, carry):
        key = block * tk
        clear = (key >= last_start) & (key + tk - 1 <= start)

        @pl.when(clear)
        def _():
            step(key, False)

        @pl.when(jnp.logical_not(clear))
        def _():
            step(key, True)

        return carry

    lax.fori_loop(first // tk, end, body, 0)


def allowed_block(key, tile, tokens, tk, tq, back_row):
    key_at = key + lax.broadcasted_iota(jnp.int32, (tk, tq), 0)
    query_at = REACH * tokens + tile * tq + lax.broadcasted_iota(jnp.int32, (tk, tq), 1)
    back = query_at - key_at
    allowed = (back >= 0) & (back <= back_row)
    return jnp.concatenate([allowed] * QPK, axis=1)


def attend_step(key, masked, tile, tk, base, back_ref, kv, vx, qs, acc, top, tokens):
    tq = qs.shape[0] // QPK
    scores = lax.dot_general(
        kv[pl.ds(key - base, tk), :], qs[...], COLS_BY_COLS, preferred_element_type=jnp.float32
    )
    if masked:
        allowed = allowed_block(key, tile, tokens, tk, tq, back_ref[0:1, :])
        scores = jnp.where(allowed, scores, NEG_FILL)
    old = top[0:1, :]
    new = jnp.maximum(old, jnp.max(scores, axis=0, keepdims=True))
    top[0:1, :] = new
    probs = jnp.exp2((scores - new) * EXP_SCALE).astype(jnp.bfloat16)
    fade = jnp.exp2((old - new) * EXP_SCALE)
    acc[...] = acc[...] * fade + lax.dot_general(
        vx[pl.ds(key - base, tk), :], probs, ROWS_BY_ROWS, preferred_element_type=jnp.float32
    )


def load_sources(refs, kv, vx):
    tokens = refs[0].shape[0]
    lane = lax.broadcasted_iota(jnp.int32, (tokens, 2 * HD), 1)
    for i, ref in enumerate(refs):
        kv[pl.ds(i * tokens, tokens), :] = ref[...]
        vx[pl.ds(i * tokens, tokens), :] = jnp.where(lane < HD, jnp.ones_like(ref), ref[...])


def attend_here_kernel(tk, pos_ref, q_ref, back_ref, here, acc_ref, top_ref, vx, qs):
    tokens = here.shape[0]
    tq = q_ref.shape[0]
    tile = pl.program_id(1)
    acc, top = acc_ref.at[0, 0], top_ref.at[0, 0]

    @pl.when(tile == 0)
    def _():
        lane = lax.broadcasted_iota(jnp.int32, (tokens, 2 * HD), 1)
        vx[...] = jnp.where(lane < HD, jnp.ones_like(here), here[...])

    qs[...] = stack_heads(q_ref[...], True)
    acc[...] = jnp.zeros_like(acc)
    top[...] = jnp.full_like(top, NEG_FILL)
    base = REACH * tokens

    def step(key, masked):
        attend_step(key, masked, tile, tk, base, back_ref, here, vx, qs, acc, top, tokens)

    key_blocks(pos_ref, tile, tq, tk, step, low=base)


def attend_far_kernel(
    tk, pos_ref, q_ref, back_ref, far_two, far_one, acc_ref, top_ref,
    out_ref, lse_ref, kv, vx, qs, acc, top
):
    tokens = far_one.shape[0]
    tq = q_ref.shape[0]
    tile = pl.program_id(1)

    @pl.when(tile == 0)
    def _():
        load_sources((far_two, far_one), kv, vx)

    qs[...] = stack_heads(q_ref[...], True)
    acc[...] = acc_ref[0, 0]
    top[...] = top_ref[0, 0]

    def step(key, masked):
        attend_step(key, masked, tile, tk, 0, back_ref, kv, vx, qs, acc, top, tokens)

    key_blocks(pos_ref, tile, tq, tk, step, high=REACH * tokens)
    total = acc[...]
    weight = total[0:1]
    blocks = unstack_heads(jnp.transpose(total / weight), False)
    out_ref[...] = jnp.concatenate(blocks, axis=1).astype(jnp.bfloat16)
    lse = top[0:1, :] * EXP_SCALE + jnp.log2(weight)
    lse_ref[...] = jnp.broadcast_to(lse, (8, lse.shape[1]))[None, None]


def attend_here(queries, here, positions, back_rows, tq, tk):
    tokens = queries.shape[0]
    groups = queries.shape[1] // (QPK * HD)
    state = (
        jax.ShapeDtypeStruct((groups, tokens // tq, 2 * HD, QPK * tq), jnp.float32),
        jax.ShapeDtypeStruct((groups, tokens // tq, 8, QPK * tq), jnp.float32),
    )
    return pl.pallas_call(
        functools.partial(attend_here_kernel, tk),
        grid_spec=pltpu.PrefetchScalarGridSpec(
            num_scalar_prefetch=1,
            grid=(groups, tokens // tq),
            in_specs=[
                pl.BlockSpec((tq, QPK * HD), lambda g, i, p: (i, g)),
                pl.BlockSpec((8, tq), lambda g, i, p: (0, i)),
                pl.BlockSpec((tokens, 2 * HD), lambda g, i, p: (0, g)),
            ],
            out_specs=[
                pl.BlockSpec((1, 1, *shape.shape[2:]), lambda g, i, p: (g, i, 0, 0)) for shape in state
            ],
            scratch_shapes=[
                pltpu.VMEM((tokens, 2 * HD), jnp.bfloat16),
                pltpu.VMEM((QPK * tq, 2 * HD), jnp.bfloat16),
            ],
        ),
        out_shape=state,
        compiler_params=pltpu.CompilerParams(vmem_limit_bytes=VMEM_LIMIT),
        cost_estimate=cost(15),
        name="attend_here",
    )(positions, queries, back_rows, here)


def attend_far(queries, far, state, positions, back_rows, tq, tk):
    tokens = queries.shape[0]
    groups = queries.shape[1] // (QPK * HD)
    kv_spec = pl.BlockSpec((tokens, 2 * HD), lambda g, i, p: (0, g))
    return pl.pallas_call(
        functools.partial(attend_far_kernel, tk),
        grid_spec=pltpu.PrefetchScalarGridSpec(
            num_scalar_prefetch=1,
            grid=(groups, tokens // tq),
            in_specs=[
                pl.BlockSpec((tq, QPK * HD), lambda g, i, p: (i, g)),
                pl.BlockSpec((8, tq), lambda g, i, p: (0, i)),
                kv_spec,
                kv_spec,
            ]
            + [
                pl.BlockSpec((1, 1, *part.shape[2:]), lambda g, i, p: (g, i, 0, 0)) for part in state
            ],
            out_specs=[
                pl.BlockSpec((tq, QPK * HD), lambda g, i, p: (i, g)),
                pl.BlockSpec((1, 1, 8, QPK * tq), lambda g, i, p: (g, i, 0, 0)),
            ],
            scratch_shapes=[
                pltpu.VMEM((REACH * tokens, 2 * HD), jnp.bfloat16),
                pltpu.VMEM((REACH * tokens, 2 * HD), jnp.bfloat16),
                pltpu.VMEM((QPK * tq, 2 * HD), jnp.bfloat16),
                pltpu.VMEM((2 * HD, QPK * tq), jnp.float32),
                pltpu.VMEM((8, QPK * tq), jnp.float32),
            ],
        ),
        out_shape=[
            jax.ShapeDtypeStruct((tokens, groups * QPK * HD), jnp.bfloat16),
            jax.ShapeDtypeStruct((groups, tokens // tq, 8, QPK * tq), jnp.float32),
        ],
        compiler_params=pltpu.CompilerParams(vmem_limit_bytes=VMEM_LIMIT),
        cost_estimate=cost(21),
        name="attend_far",
    )(positions, queries, back_rows, *far, *state)


def attend_back_kernel(
    tk, pos_ref, q_ref, do_ref, o_ref, back_ref, lse_ref, cos_ref, sin_ref, far_two, far_one, here,
    dq_ref, d_far_two, d_far_one, d_here, kv, dkv, qs, dos, dq
):
    tokens = here.shape[0]
    tq = q_ref.shape[0]
    tile = pl.program_id(0)

    @pl.when(tile == 0)
    def _():
        for i, ref in enumerate((far_two, far_one, here)):
            kv[pl.ds(i * tokens, tokens), :] = ref[...]
        dkv[...] = jnp.zeros_like(dkv)

    qs[...] = stack_heads(q_ref[...], True)
    dos[...] = stack_heads(do_ref[...], False)
    dq[...] = jnp.zeros_like(dq)
    product = dos[...].astype(jnp.float32) * stack_heads(o_ref[...], False).astype(jnp.float32)
    delta = jnp.sum(jnp.transpose(product), axis=0, keepdims=True)
    lse = lse_ref[0, 0, 0:1, :]

    def step(key, masked):
        keys = kv[pl.ds(key, tk), :]
        scores = lax.dot_general(keys, qs[...], COLS_BY_COLS, preferred_element_type=jnp.float32)
        probs = jnp.exp2(scores * EXP_SCALE - lse)
        if masked:
            allowed = allowed_block(key, tile, tokens, tk, tq, back_ref[0:1, :])
            probs = jnp.where(allowed, probs, 0.0)
        d_probs = lax.dot_general(keys, dos[...], COLS_BY_COLS, preferred_element_type=jnp.float32)
        d_scores = (probs * (d_probs - delta)).astype(jnp.bfloat16)
        d_keys = jnp.dot(d_scores, qs[...], preferred_element_type=jnp.float32)
        d_values = jnp.dot(probs.astype(jnp.bfloat16), dos[...], preferred_element_type=jnp.float32)
        dkv[pl.ds(key, tk), :] += d_keys * HD**-0.5 + d_values
        dq[...] += lax.dot_general(
            d_scores, keys, ROWS_BY_ROWS, preferred_element_type=jnp.float32
        )

    key_blocks(pos_ref, tile, tq, tk, step)
    cos, sin = cos_ref[...], sin_ref[...]
    blocks = unstack_heads(dq[...] * HD**-0.5, True)
    blocks = [block * cos - turn_halves(block) * sin for block in blocks]
    dq_ref[...] = jnp.concatenate(blocks, axis=1).astype(jnp.bfloat16)

    @pl.when(tile == pl.num_programs(0) - 1)
    def _():
        d_far_two[...] = dkv[pl.ds(0, tokens), :].astype(jnp.bfloat16)
        d_far_one[...] = dkv[pl.ds(tokens, tokens), :].astype(jnp.bfloat16)
        d_here[...] = dkv[pl.ds(2 * tokens, tokens), :]


def attend_back(
    queries, d_attn, attn, lse, sources, positions, back_rows, cos, sin, group, tq, tk
):
    tokens = queries.shape[0]
    kv_spec = pl.BlockSpec((tokens, 2 * HD), lambda i, p: (0, group))
    own_kv = pl.BlockSpec((tokens, 2 * HD), lambda i, p: (0, 0))
    q_spec = pl.BlockSpec((tq, QPK * HD), lambda i, p: (i, group))
    own_q = pl.BlockSpec((tq, QPK * HD), lambda i, p: (i, 0))
    angle_spec = pl.BlockSpec((tq, 128), lambda i, p: (i, 0))
    return pl.pallas_call(
        functools.partial(attend_back_kernel, tk),
        grid_spec=pltpu.PrefetchScalarGridSpec(
            num_scalar_prefetch=1,
            grid=(tokens // tq,),
            in_specs=[
                q_spec,
                q_spec,
                q_spec,
                pl.BlockSpec((8, tq), lambda i, p: (0, i)),
                pl.BlockSpec((1, 1, 8, QPK * tq), lambda i, p: (group, i, 0, 0)),
                angle_spec,
                angle_spec,
                kv_spec,
                kv_spec,
                kv_spec,
            ],
            out_specs=[own_q, own_kv, own_kv, own_kv],
            scratch_shapes=[
                pltpu.VMEM(((REACH + 1) * tokens, 2 * HD), jnp.bfloat16),
                pltpu.VMEM(((REACH + 1) * tokens, 2 * HD), jnp.float32),
                pltpu.VMEM((QPK * tq, 2 * HD), jnp.bfloat16),
                pltpu.VMEM((QPK * tq, 2 * HD), jnp.bfloat16),
                pltpu.VMEM((QPK * tq, 2 * HD), jnp.float32),
            ],
        ),
        out_shape=[
            jax.ShapeDtypeStruct((tokens, QPK * HD), jnp.bfloat16),
            jax.ShapeDtypeStruct((tokens, 2 * HD), jnp.bfloat16),
            jax.ShapeDtypeStruct((tokens, 2 * HD), jnp.bfloat16),
            jax.ShapeDtypeStruct((tokens, 2 * HD), jnp.float32),
        ],
        compiler_params=pltpu.CompilerParams(vmem_limit_bytes=VMEM_LIMIT),
        cost_estimate=cost(28),
        name="attend_back",
    )(positions, queries, d_attn, attn, back_rows, lse, cos, sin, *sources)


def mix_kernel(groups, cos_ref, sin_ref, *refs):
    out_ref = refs[-1]
    cos, sin = cos_ref[...], sin_ref[...]
    key_lane = lax.broadcasted_iota(jnp.int32, cos.shape, 1) < HD
    for group in range(groups):
        dq_ref, here, from_one, from_two = refs[4 * group : 4 * group + 4]
        base = group * (QPK + 2) * HD
        out_ref[:, base : base + QPK * HD] = dq_ref[...]
        total = here[...] + from_one[...].astype(jnp.float32) + from_two[...].astype(jnp.float32)
        turned = total * cos - turn_halves(total) * sin
        out_ref[:, base + QPK * HD : base + (QPK + 2) * HD] = jnp.where(
            key_lane, turned, total
        ).astype(jnp.bfloat16)


def mix_grads(parts, cos, sin, tile):
    tokens = cos.shape[0]
    groups = len(parts)

    def rows(wide):
        return pl.BlockSpec((tile, wide), lambda i: (i, 0))

    flat = [array for part in parts for array in part]
    return pl.pallas_call(
        functools.partial(mix_kernel, groups),
        grid=(tokens // tile,),
        in_specs=[rows(128), rows(128)] + [rows(array.shape[1]) for array in flat],
        out_specs=rows(groups * (QPK + 2) * HD),
        out_shape=jax.ShapeDtypeStruct((tokens, groups * (QPK + 2) * HD), jnp.bfloat16),
        compiler_params=pltpu.CompilerParams(vmem_limit_bytes=VMEM_LIMIT),
        cost_estimate=cost(3),
        name="mix_grads",
    )(cos, sin, *flat)


def out_step_kernel(distances, last, rank_ref, *refs):
    refs = list(refs)
    base_ref = refs.pop(0)
    gain_ref = refs.pop(0) if last else None
    total = base_ref[...].astype(jnp.float32)
    for distance, count in distances:
        piece = refs.pop(0)[...]
        if count == 2:
            piece = jnp.where(rank_ref[0] >= distance, piece, refs.pop(0)[...])
        total = total + jnp.dot(piece, refs.pop(0)[...], preferred_element_type=jnp.float32)
    if not last:
        refs[0][...] = total
    else:

        @pl.when(pl.program_id(0) == rank_ref[0])
        def _():
            refs[0][...] = total

        inverse = lax.rsqrt(jnp.mean(total * total, axis=1, keepdims=True) + NORM_EPS)
        refs[1][...] = (total * inverse * gain_ref[...]).astype(jnp.bfloat16)


def out_step(base, pieces, rank, weight, tile, gain=None):
    tokens, width = base.shape
    depth = pieces[0][1][0].shape[1]
    last = gain is not None
    slots = weight.shape[0] // depth

    def rows(wide):
        return pl.BlockSpec((tile, wide), lambda i, r: (i, 0))

    def slot_rows(distance, count):
        def index(i, r):
            slot = r[0] - distance
            if count == 2:
                slot = jnp.where(r[0] >= distance, slot, r[0] + distance)
            return jnp.clip(slot, 0, slots - 1), 0

        return pl.BlockSpec((depth, width), index)

    operands, specs = [base], [rows(width)]
    if last:
        operands.append(gain[None])
        specs.append(pl.BlockSpec((1, width), lambda i, r: (0, 0)))
    for distance, blocks in pieces:
        operands += [*blocks, weight]
        specs += [rows(depth)] * len(blocks) + [slot_rows(distance, len(blocks))]
    outs = [jax.ShapeDtypeStruct((tile if last else tokens, width), jnp.float32)]
    out_specs = [pl.BlockSpec((tile, width), lambda i, r: (0, 0)) if last else rows(width)]
    if last:
        outs.append(jax.ShapeDtypeStruct((tokens, width), jnp.bfloat16))
        out_specs.append(rows(width))
    distances = tuple((distance, len(blocks)) for distance, blocks in pieces)
    made = pl.pallas_call(
        functools.partial(out_step_kernel, distances, last),
        grid_spec=pltpu.PrefetchScalarGridSpec(
            num_scalar_prefetch=1,
            grid=(tokens // tile,),
            in_specs=specs,
            out_specs=out_specs,
        ),
        out_shape=outs,
        compiler_params=pltpu.CompilerParams(vmem_limit_bytes=VMEM_LIMIT),
        cost_estimate=cost(7),
        name="out_step",
    )(jnp.reshape(rank, (1,)).astype(jnp.int32), *operands)
    return made if last else made[0]


def own_kernel(rank_ref, *refs):
    *pieces, out_ref = refs

    def put(piece):
        out_ref[...] = piece[...]

    pick_piece(pieces, rank_ref[0] - pl.program_id(0), put)


def own_rows_of_heads(pieces, rank, own):
    size = (len(pieces) + 1) // 2
    columns = pieces[0].shape[1]
    return pl.pallas_call(
        own_kernel,
        grid_spec=pltpu.PrefetchScalarGridSpec(
            num_scalar_prefetch=1,
            grid=(size,),
            in_specs=[pl.BlockSpec((own, columns), lambda i, r: (r[0], 0))] * len(pieces),
            out_specs=pl.BlockSpec((own, columns), lambda i, r: (0, i)),
        ),
        out_shape=jax.ShapeDtypeStruct((own, columns * size), pieces[0].dtype),
        compiler_params=pltpu.CompilerParams(vmem_limit_bytes=VMEM_LIMIT),
        cost_estimate=cost(2),
        name="own_rows_of_heads",
    )(jnp.reshape(rank, (1,)).astype(jnp.int32), *pieces)


def gate_kernel(n_ref, w_ref, dh_ref, hidden_ref, dgu_ref):
    wide = dh_ref.shape[1]
    both = jnp.dot(n_ref[...], w_ref[...], preferred_element_type=jnp.float32)
    gate, up = both[:, :wide], both[:, wide:]
    sigmoid = jax.nn.sigmoid(gate)
    silu = gate * sigmoid
    d_hidden = dh_ref[...].astype(jnp.float32)
    hidden_ref[...] = (silu * up).astype(jnp.bfloat16)
    d_gate = d_hidden * up * (sigmoid + silu * (1.0 - sigmoid))
    dgu_ref[...] = jnp.concatenate([d_gate, d_hidden * silu], axis=1).astype(jnp.bfloat16)


def gate_and_back(normed, weight, d_hidden, tile, wide):
    tokens, width = normed.shape
    units = d_hidden.shape[1]
    cell = pl.BlockSpec((tile, wide), lambda j, i: (i, j))
    pair_cell = pl.BlockSpec((tile, 2 * wide), lambda j, i: (i, j))
    return pl.pallas_call(
        gate_kernel,
        grid=(units // wide, tokens // tile),
        in_specs=[
            pl.BlockSpec((tile, width), lambda j, i: (i, 0)),
            pl.BlockSpec((width, 2 * wide), lambda j, i: (0, j)),
            cell,
        ],
        out_specs=[cell, pair_cell],
        out_shape=[
            jax.ShapeDtypeStruct((tokens, units), jnp.bfloat16),
            jax.ShapeDtypeStruct((tokens, 2 * units), jnp.bfloat16),
        ],
        compiler_params=pltpu.CompilerParams(vmem_limit_bytes=VMEM_LIMIT),
        cost_estimate=cost(27),
        name="gate_and_back",
    )(normed, weight, d_hidden)


def blocks_kernel(chunks_ref, *refs):
    count = (len(refs) - 1) // 2
    left = jnp.concatenate([ref[...] for ref in refs[:count]], axis=0)
    product = lax.dot_general(
        left, refs[count][...], COLS_BY_COLS, preferred_element_type=jnp.float32
    ).astype(jnp.bfloat16)
    rows = refs[0].shape[0]
    for i, out_ref in enumerate(refs[count + 1 :]):
        out_ref[...] = product[i * rows : (i + 1) * rows]


def blocks_times(left, right, chunks, rows, wide, micros):
    depth = left.shape[1]
    count = chunks.shape[0]

    def block_spec(i):
        return pl.BlockSpec((rows, depth), lambda j, c: (c[i], 0))

    return pl.pallas_call(
        blocks_kernel,
        grid_spec=pltpu.PrefetchScalarGridSpec(
            num_scalar_prefetch=1,
            grid=(right.shape[0] // wide,),
            in_specs=[block_spec(i) for i in range(count)]
            + [pl.BlockSpec((wide, depth), lambda j, c: (j, 0))],
            out_specs=[pl.BlockSpec((rows, wide), lambda j, c: (0, j))] * count,
        ),
        out_shape=[jax.ShapeDtypeStruct((rows, right.shape[0]), jnp.bfloat16)] * count,
        compiler_params=pltpu.CompilerParams(vmem_limit_bytes=VMEM_LIMIT),
        cost_estimate=cost(micros),
        name="blocks_times",
    )(chunks, *[left] * count, right)


def gain_kernel(part_ref, w_ref, out_ref):
    product = part_ref[...].astype(jnp.float32) * w_ref[...].astype(jnp.float32)
    ones = jnp.ones((8, product.shape[1]), jnp.float32)
    out_ref[...] = lax.dot_general(
        ones, product, COLS_BY_COLS, precision=lax.Precision.HIGHEST,
        preferred_element_type=jnp.float32,
    )


def row_products(part, weight, tile):
    rows, columns = part.shape
    cell = pl.BlockSpec((tile, columns), lambda i: (i, 0))
    sums = pl.pallas_call(
        gain_kernel,
        grid=(rows // tile,),
        in_specs=[cell, cell],
        out_specs=pl.BlockSpec((8, tile), lambda i: (0, i)),
        out_shape=jax.ShapeDtypeStruct((8, rows), jnp.float32),
        compiler_params=pltpu.CompilerParams(vmem_limit_bytes=VMEM_LIMIT),
        cost_estimate=cost(4),
        name="row_products",
    )(part, weight)
    return sums[0]


def norm_back_rows(vector, grad_in, gain):
    inverse = lax.rsqrt(jnp.mean(vector * vector, axis=1, keepdims=True) + NORM_EPS)
    scaled = grad_in * gain
    mean = jnp.mean(vector * scaled, axis=1, keepdims=True)
    grad = inverse * scaled - vector * (inverse * inverse * inverse * mean)
    return grad, jnp.sum(grad_in * vector * inverse, axis=0, keepdims=True)


def sum_refs(refs):
    total = refs[0][...].astype(jnp.float32)
    for ref in refs[1:]:
        total = total + ref[...].astype(jnp.float32)
    return total


def mid_kernel(mid_ref, dy_ref, gain_ref, *refs):
    *parts, d_mid_ref, branch_ref, gain_grad_ref = refs
    grad, gain_grad = norm_back_rows(mid_ref[...], sum_refs(parts), gain_ref[...])
    d_mid = dy_ref[...].astype(jnp.float32) + grad
    d_mid_ref[...] = d_mid
    branch_ref[...] = d_mid.astype(jnp.bfloat16)
    gain_grad = jnp.broadcast_to(gain_grad, gain_grad_ref.shape)

    @pl.when(pl.program_id(0) == 0)
    def _():
        gain_grad_ref[...] = gain_grad

    @pl.when(pl.program_id(0) > 0)
    def _():
        gain_grad_ref[...] += gain_grad


def back_to_mid(parts, mid, output_grad, gain):
    own, width = output_grad.shape
    tile = min(64, own)
    rows = pl.BlockSpec((tile, width), lambda i: (i, 0))
    outs = pl.pallas_call(
        mid_kernel,
        grid=(own // tile,),
        in_specs=[rows, rows, pl.BlockSpec((1, width), lambda i: (0, 0))] + [rows] * len(parts),
        out_specs=[rows, rows, pl.BlockSpec((8, width), lambda i: (0, 0))],
        out_shape=[
            jax.ShapeDtypeStruct((own, width), jnp.float32),
            jax.ShapeDtypeStruct((own, width), jnp.bfloat16),
            jax.ShapeDtypeStruct((8, width), jnp.float32),
        ],
        compiler_params=pltpu.CompilerParams(vmem_limit_bytes=VMEM_LIMIT),
        cost_estimate=cost(4),
        name="back_to_mid",
    )(mid, output_grad, gain[None], *parts)
    return outs[0], outs[1], outs[2][0]


def input_kernel(x_ref, d_mid_ref, gain_ref, *refs):
    *parts, out_ref = refs
    x = x_ref[...].astype(jnp.float32)
    grad, _ = norm_back_rows(x, sum_refs(parts), gain_ref[...])
    out_ref[...] = d_mid_ref[...] + grad


def back_to_input(parts, layer_input, d_mid, gain):
    own, width = layer_input.shape
    tile = min(64, own)
    rows = pl.BlockSpec((tile, width), lambda i: (i, 0))
    return pl.pallas_call(
        input_kernel,
        grid=(own // tile,),
        in_specs=[rows, rows, pl.BlockSpec((1, width), lambda i: (0, 0))] + [rows] * len(parts),
        out_specs=rows,
        out_shape=jax.ShapeDtypeStruct((own, width), jnp.float32),
        compiler_params=pltpu.CompilerParams(vmem_limit_bytes=VMEM_LIMIT),
        cost_estimate=cost(4),
        name="back_to_input",
    )(layer_input, d_mid, gain[None], *parts)


def round_kernel(wide, w_ref, out_ref):
    for block in range(w_ref.shape[2] // wide):
        for half in range(2):
            column = (2 * block + half) * wide
            out_ref[:, column : column + wide] = w_ref[
                half, :, block * wide : (block + 1) * wide
            ].astype(jnp.bfloat16)


def round_interleaved(weight, wide):
    _, rows, units = weight.shape
    tile = min(64, rows)
    return pl.pallas_call(
        functools.partial(round_kernel, wide),
        grid=(rows // tile,),
        in_specs=[pl.BlockSpec((2, tile, units), lambda i: (0, i, 0))],
        out_specs=pl.BlockSpec((tile, 2 * units), lambda i: (i, 0)),
        out_shape=jax.ShapeDtypeStruct((rows, 2 * units), jnp.bfloat16),
        compiler_params=pltpu.CompilerParams(vmem_limit_bytes=VMEM_LIMIT),
        cost_estimate=cost(3),
        name="round_interleaved",
    )(weight)


def norm_back_rows(vector, grad_in, gain):
    inverse = lax.rsqrt(jnp.mean(vector * vector, axis=1, keepdims=True) + NORM_EPS)
    scaled = grad_in * gain
    mean = jnp.mean(vector * scaled, axis=1, keepdims=True)
    grad = inverse * scaled - vector * (inverse * inverse * inverse * mean)
    return grad, jnp.sum(grad_in * vector * inverse, axis=0, keepdims=True)


def sum_refs(refs):
    total = refs[0][...].astype(jnp.float32)
    for ref in refs[1:]:
        total = total + ref[...].astype(jnp.float32)
    return total


def mid_kernel(mid_ref, dy_ref, gain_ref, *refs):
    *parts, d_mid_ref, branch_ref, gain_grad_ref = refs
    grad, gain_grad = norm_back_rows(mid_ref[...], sum_refs(parts), gain_ref[...])
    d_mid = dy_ref[...].astype(jnp.float32) + grad
    d_mid_ref[...] = d_mid
    branch_ref[...] = d_mid.astype(jnp.bfloat16)
    gain_grad = jnp.broadcast_to(gain_grad, gain_grad_ref.shape)

    @pl.when(pl.program_id(0) == 0)
    def _():
        gain_grad_ref[...] = gain_grad

    @pl.when(pl.program_id(0) > 0)
    def _():
        gain_grad_ref[...] += gain_grad


def back_to_mid(parts, mid, output_grad, gain):
    own, width = output_grad.shape
    tile = min(64, own)
    rows = pl.BlockSpec((tile, width), lambda i: (i, 0))
    outs = pl.pallas_call(
        mid_kernel,
        grid=(own // tile,),
        in_specs=[rows, rows, pl.BlockSpec((1, width), lambda i: (0, 0))] + [rows] * len(parts),
        out_specs=[rows, rows, pl.BlockSpec((8, width), lambda i: (0, 0))],
        out_shape=[
            jax.ShapeDtypeStruct((own, width), jnp.float32),
            jax.ShapeDtypeStruct((own, width), jnp.bfloat16),
            jax.ShapeDtypeStruct((8, width), jnp.float32),
        ],
        compiler_params=pltpu.CompilerParams(vmem_limit_bytes=VMEM_LIMIT),
        cost_estimate=cost(4),
        name="back_to_mid",
    )(mid, output_grad, gain[None], *parts)
    return outs[0], outs[1], outs[2][0]


def input_kernel(x_ref, d_mid_ref, gain_ref, *refs):
    *parts, out_ref = refs
    x = x_ref[...].astype(jnp.float32)
    grad, _ = norm_back_rows(x, sum_refs(parts), gain_ref[...])
    out_ref[...] = d_mid_ref[...] + grad


def back_to_input(parts, layer_input, d_mid, gain):
    own, width = layer_input.shape
    tile = min(64, own)
    rows = pl.BlockSpec((tile, width), lambda i: (i, 0))
    return pl.pallas_call(
        input_kernel,
        grid=(own // tile,),
        in_specs=[rows, rows, pl.BlockSpec((1, width), lambda i: (0, 0))] + [rows] * len(parts),
        out_specs=rows,
        out_shape=jax.ShapeDtypeStruct((own, width), jnp.float32),
        compiler_params=pltpu.CompilerParams(vmem_limit_bytes=VMEM_LIMIT),
        cost_estimate=cost(4),
        name="back_to_input",
    )(layer_input, d_mid, gain[None], *parts)


def round_kernel(w_ref, out_ref):
    out_ref[...] = w_ref[0].astype(jnp.bfloat16)


def round_interleaved(weight, wide):
    _, rows, units = weight.shape
    return pl.pallas_call(
        round_kernel,
        grid=(units // wide, 2),
        in_specs=[pl.BlockSpec((1, rows, wide), lambda j, k: (k, 0, j))],
        out_specs=pl.BlockSpec((rows, wide), lambda j, k: (0, 2 * j + k)),
        out_shape=jax.ShapeDtypeStruct((rows, 2 * units), jnp.bfloat16),
        cost_estimate=cost(6),
        name="round_interleaved",
    )(weight)


def adam_kernel(g_ref, w_ref, m_ref, s_ref, grad_ref, w_out, m_out, s_out, copy_out):
    grad = g_ref[...].astype(jnp.float32)
    new, moment, square, _ = adam_step(w_ref[0], grad, m_ref[0], s_ref[0])
    grad_ref[0] = grad
    w_out[0] = new
    m_out[0] = moment
    s_out[0] = square
    copy_out[0] = new.astype(jnp.bfloat16)


def adam_interleaved(grad, weight, moment, square, wide):
    _, rows, units = weight.shape
    cell = pl.BlockSpec((1, rows, wide), lambda j, k: (k, 0, j))
    shape = jax.ShapeDtypeStruct(weight.shape, jnp.float32)
    return pl.pallas_call(
        adam_kernel,
        grid=(units // wide, 2),
        in_specs=[pl.BlockSpec((rows, wide), lambda j, k: (0, 2 * j + k)), cell, cell, cell],
        out_specs=[cell] * 5,
        out_shape=[shape] * 4 + [jax.ShapeDtypeStruct(weight.shape, jnp.bfloat16)],
        compiler_params=pltpu.CompilerParams(vmem_limit_bytes=VMEM_LIMIT),
        cost_estimate=cost(13),
        name="adam_interleaved",
    )(grad, weight, moment, square)


def angle_tables(positions):
    half_size = HD // 2
    freq = ROPE_BASE ** (-(jnp.arange(half_size).astype(jnp.float32) * 2.0 / HD))
    angle = positions.astype(jnp.float32)[:, None] * freq[None, :]
    cos, sin = jnp.cos(angle), jnp.sin(angle)
    return jnp.concatenate([cos] * 4, axis=1), jnp.concatenate([-sin, sin] * 2, axis=1)


def adam_step(weight_old, grad_new, moment_one, moment_two):
    moment_next = BETA * moment_one + (1.0 - BETA) * grad_new
    square_next = BETA * moment_two + (1.0 - BETA) * grad_new * grad_new
    change = -RATE * (moment_next / (jnp.sqrt(square_next) + ADAM_EPS) + DECAY * weight_old)
    return (weight_old + change, moment_next, square_next, change)


def local(
    layer_input,
    output_grad,
    segment_ids,
    positions,
    qkv_weight,
    qkv_moment,
    qkv_square,
    out_weight,
    out_moment,
    out_square,
    gate_up_weight,
    gate_up_moment,
    gate_up_square,
    down_weight,
    down_moment,
    down_square,
    norm_gains,
    gains_moment,
    gains_square,
):
    low = low_type = jnp.bfloat16
    full = jnp.float32
    own, width = layer_input.shape
    tokens = positions.shape[0]
    rank = lax.axis_index("tp")
    units = down_weight.shape[0]
    groups = qkv_weight.shape[1] // ((QPK + 2) * HD)
    head_columns = groups * QPK * HD
    tile = min(256, own)
    gain_one = norm_gains[0]
    gain_two = norm_gains[1]

    wide = min(512, units)

    close = lax.optimization_barrier

    w_qkv = lax.all_gather(qkv_weight.astype(low), "seq", axis=0, tiled=True)
    side = (gate_up_weight, down_weight, out_weight, positions)
    x_line = LineGather(layer_input, "tp")
    for index in range(x_line.hops):
        x_line.hop()
        if index == 1:
            held_gate_up, held_down, held_out, held_positions = side
            w_gate_up = lax.all_gather(
                round_interleaved(held_gate_up, wide), "seq", axis=0, tiled=True
            )
            cos, sin = angle_tables(held_positions)
            back_rows = jnp.broadcast_to(held_positions[None, :], (8, tokens))
            side = (held_down.astype(low), held_out.astype(low), cos, sin, back_rows)
        x_line.moving, side = close((x_line.moving, side))
    pieces, side, w_qkv, output_grad = close((x_line.pieces, side, w_qkv, output_grad))
    low_down, low_out, cos, sin, back_rows = side

    dy_line = LineGather(output_grad, "tp")
    dy_line.hop()
    made = project_qkv(pieces, rank, w_qkv, gain_one, cos, sin)
    made, dy_line.moving, low_out, low_down = close((made, dy_line.moving, low_out, low_down))
    x_rows, normed_one, queries, kv = made
    w_down = lax.all_gather(low_down, "seq", axis=1, tiled=True)
    far = [along_sequence(kv, distance, tokens) for distance in (2, 1)]
    if dy_line.hops > 1:
        dy_line.hop()
    states = attend_here(queries, kv, positions, back_rows, 256, 512)
    out_strip = swap_gather(after(low_out, states[1]), "tp")
    far, states, queries, w_gate_up, dy_line.moving = close(
        (far, states, queries, w_gate_up, dy_line.moving)
    )
    for _ in range(2, dy_line.hops):
        dy_line.hop()
    attn, lse = attend_far(queries, far, states, positions, back_rows, 256, 512)
    attn, lse, dy_pieces, x_rows, out_strip = close(
        (attn, lse, dy_line.pieces, x_rows, out_strip)
    )
    w_out = lax.all_gather(out_strip.reshape(-1, low_out.shape[1]), "seq", axis=1, tiled=True)

    heads_line = LineGather(attn, "tp")
    arrived = [(0, [heads_line.from_low[0]])]
    total = x_rows
    for index in range(heads_line.hops):
        heads_line.hop()
        if index == 0:
            grad_rows = place_rows(dy_pieces, rank)
            d_hidden = contract_cols(grad_rows, w_down).astype(low)
            heads_line.moving, grad_rows, d_hidden, total = close(
                (heads_line.moving, grad_rows, d_hidden, total)
            )
        elif index < heads_line.hops - 1:
            heads_line.moving = close(heads_line.moving)
        else:
            total = out_step(total, arrived, rank, w_out, own)
            heads_line.moving, total = close((heads_line.moving, total))
            arrived = []
        below, above = heads_line.moving
        step = heads_line.step
        if 2 * step > heads_line.hops:
            arrived.append((step, [below, above]))
        else:
            arrived += [(step, [below]), (-step, [above])]

    mid, normed_two = out_step(total, arrived, rank, w_out, own, gain_two)
    mid, normed_two, w_gate_up, d_hidden = close((mid, normed_two, w_gate_up, d_hidden))
    hidden, d_gate_up = close(gate_and_back(normed_two, w_gate_up, d_hidden, 1024, wide))
    down_grad = contract_rows(hidden, grad_rows).astype(low)
    down_grad, hidden, d_gate_up, normed_two, grad_rows = close(
        (down_grad, hidden, d_gate_up, normed_two, grad_rows)
    )
    down_grad = lax.psum_scatter(down_grad, "seq", scatter_dimension=1, tiled=True)
    peers = peers_of("tp")
    first = blocks_times(d_gate_up, w_gate_up, peers[:1], own, 512, 9)
    first, side = close((first, (hidden, d_gate_up, normed_two, grad_rows)))
    back_line = LineScatter(first, "tp")
    for index in range(back_line.hops):
        back_line.hop()
        hidden, d_gate_up, normed_two, grad_rows = side
        if index == 0:
            second = blocks_times(d_gate_up, w_gate_up, peers[1:], own, 256, 22)
            back_line.moving, side, second = close((back_line.moving, side, second))
            back_line.made += second
        elif index == 1:
            gate_up_grad = contract_rows(normed_two, d_gate_up).astype(low)
            back_line.moving, side, gate_up_grad = close((back_line.moving, side, gate_up_grad))
            gate_up_grad = lax.psum_scatter(gate_up_grad, "seq", scatter_dimension=0, tiled=True)
        elif index == 2:
            partial_out = jnp.dot(hidden, w_down, preferred_element_type=full).astype(low)
            back_line.moving, side, partial_out = close((back_line.moving, side, partial_out))
        else:
            back_line.moving, side = close((back_line.moving, side))
    d_mid, d_branch, gain_two_grad = back_to_mid(back_line.parts, mid, output_grad, gain_two)

    d_attn = contract_cols(d_branch, w_out).astype(low)
    d_attn, d_branch, d_mid, mid, gain_two_grad, partial_out = close(
        (d_attn, d_branch, d_mid, mid, gain_two_grad, partial_out)
    )
    d_attn = lax.all_to_all(d_attn, "tp", split_axis=1, concat_axis=0, tiled=True)
    own_heads = own_rows_of_heads(heads_line.pieces, rank, own)
    out_grad = contract_rows(own_heads, d_branch).astype(low)
    d_attn, out_grad, partial_out, down_grad = close((d_attn, out_grad, partial_out, down_grad))
    out_grad = lax.psum_scatter(out_grad, "seq", scatter_dimension=1, tiled=True)
    result = swap_scatter_parts(partial_out, "tp")
    grads = []
    travelled = []
    for group in range(groups):
        made = attend_back(
            queries, d_attn, attn, lse, [*far, kv], positions, back_rows,
            cos, sin, group, 256, 512,
        )
        made, d_attn, travelled = close((made, d_attn, travelled))
        grads.append(made)
        travelled.append(
            [along_sequence(made[2], -1, tokens), along_sequence(made[1], -2, tokens)]
        )
    down_grad = down_grad.astype(full)
    down_new = adam_step(down_weight, down_grad, down_moment, down_square)
    down_new, grads, travelled, down_grad = close((down_new, grads, travelled, down_grad))
    d_mixed = mix_grads(
        [(made[0], made[3], *moved) for made, moved in zip(grads, travelled, strict=True)],
        cos, sin, tile,
    )
    made = blocks_times(d_mixed, w_qkv, peers[:1], own, 512, 2)
    made, d_mixed, gate_up_grad = close((made, d_mixed, gate_up_grad))
    in_line = LineScatter(made, "tp")
    for index in range(in_line.hops):
        in_line.hop()
        if index == 0:
            made = blocks_times(d_mixed, w_qkv, peers[1:], own, 512, 5)
            qkv_grad = contract_rows(normed_one, d_mixed).astype(low)
            gain_one_grad = row_products(qkv_grad, w_qkv, min(512, width)) / gain_one
            gains_grad = jnp.stack([gain_one_grad, gain_two_grad])
            in_line.moving, qkv_grad, gains_grad, result, made = close(
                (in_line.moving, qkv_grad, gains_grad, result, made)
            )
            in_line.made += made
            qkv_grad = lax.psum_scatter(qkv_grad, "seq", scatter_dimension=0, tiled=True)
        elif index == 1:
            outputs = (mid + sum_parts(result)).astype(low)
            gains_grad = sum_by_swaps(gains_grad, "seq")
            in_line.moving, outputs, gains_grad, out_grad, gate_up_grad = close(
                (in_line.moving, outputs, gains_grad, out_grad, gate_up_grad)
            )
            out_parts = swap_scatter_parts(out_grad, "tp")
        elif index == 2:
            gate_up_new = adam_interleaved(
                gate_up_grad, gate_up_weight, gate_up_moment, gate_up_square, wide
            )
            gains_grad = sum_at_once(after(gains_grad, gate_up_new[4]), "tp")
            in_line.moving, gains_grad, out_parts, gate_up_new = close(
                (in_line.moving, gains_grad, out_parts, gate_up_new)
            )
        else:
            in_line.moving = close(in_line.moving)
    input_grad = back_to_input(in_line.parts, layer_input, d_mid, gain_one)
    out_grad = sum_parts(out_parts)
    out_new = adam_step(out_weight, out_grad, out_moment, out_square)

    out_grad = out_grad.astype(full)
    qkv_grad = qkv_grad.astype(full)
    qkv_new = adam_step(qkv_weight, qkv_grad, qkv_moment, qkv_square)
    gains_new = adam_step(norm_gains, gains_grad, gains_moment, gains_square)
    return (
        outputs,
        input_grad,
        qkv_grad,
        qkv_new[0],
        qkv_new[1],
        qkv_new[2],
        qkv_new[0].astype(low),
        out_grad,
        out_new[3],
        out_new[1],
        out_new[2],
        *gate_up_new,
        down_grad,
        down_new[0],
        down_new[1],
        down_new[2],
        down_new[0].astype(low),
        gains_grad,
        gains_new[3],
        gains_new[1],
        gains_new[2],
    )


def solution(mesh):
    tokens = P(("seq", "tp"), None)
    rows = P("seq", "tp")
    columns = P("tp", "seq")
    pair = P(None, "seq", "tp")
    return jax.shard_map(
        local,
        mesh=mesh,
        in_specs=(
            (tokens,) * 2 + (P("seq"),) * 2 + (rows,) * 3 + (columns,) * 3 + (pair,) * 3
            + (columns,) * 3 + (P(),) * 3
        ),
        out_specs=(
            (tokens,) * 2 + (rows,) * 5 + (columns,) * 4 + (pair,) * 5 + (columns,) * 5 + (P(),) * 4
        ),
        check_vma=False,
    )
```
